512 devices in a mesh: docs: 64 (over y, z), heads: 8 (over x, core).
Axes of the slice: x: 4, y: 4, z: 16, core: 2. Of those that a mesh axis runs over, the one named last changes fastest.
Arguments:
- queries: bfloat16 [24576, 8192], P('docs', 'heads'), may hold values from -6 to 6
- own_kv: bfloat16 [24576, 2048], P('docs', 'heads'), may hold values from -6 to 6
- cache: bfloat16 [49152, 2048], P('docs', 'heads'), may hold values from -6 to 6
- doc_lists: int32 [128, 20], replicated, may hold values from 0 to 383, as said below
- doc_counts: int32 [128], replicated, may hold values from 8 to 20, as said below
- dev_pos: int32 [384, 24], P('docs'), may hold values from 0 to 127, as said below
- blend_gain: float32 [8, 256], P('heads'), may hold values from 2 to 51
Outputs:
- att_out: bfloat16 [24576, 8192], P('docs', 'heads')
- returned_kv: bfloat16 [4096, 24, 2048], P('docs', None, 'heads')
- dev_score: float32 [128, 20, 24], P('docs')
The draws below stay inside these ranges and needn't reach their ends.
Inputs may be any that keep to these rules, and one draw needn't show every extreme that they name: `doc_lists`: document d is held by index d // 6 of docs; the lists of one home's 2 requests together hold at most 1 entry naming a document of any one holder. `doc_counts`: some request uses all 20 entries and some uses 8. `dev_pos`: each document's positions are distinct and rising.
All inputs are finite; a program needn't handle non-finite values.
Results may differ from the reference program's by a relative error of at most 0.0046.
Values may be sent and summed in bfloat16 or wider, within the bound.
A program may use at most 64 MiB of HBM per device.

```python
import jax
import jax.numpy as jnp
from jax import lax

QH = 64
KVH = 8
HD = 128
Q_LEN = 192
REQ_DEV = 2
DOC_LEN = 128
DOC_DEV = 6
SLOTS = 20
DEV_TOK = 24
REQUESTS = 128
DOCS = 384
CAP = 1
N_DOCS = 64


def positions_of(key):
    base = jax.random.fold_in(key, 11)
    doc_keys = jax.random.split(base, DOCS)

    def one_doc(doc_key):
        order = jax.random.permutation(doc_key, DOC_LEN)
        return jnp.sort(order[:DEV_TOK]).astype(jnp.int32)
    return jax.vmap(one_doc)(doc_keys)


def draw_dev_pos(key, part):
    return positions_of(key)


def draw_cache(key, part):
    key = jax.random.fold_in(key, 3)
    shape = (DOCS * DOC_LEN, KVH * 2 * HD)
    values = jnp.clip(jax.random.normal(key, shape, jnp.float32), -6.0, 6.0)
    return values.astype(jnp.bfloat16)


def draw_queries(key, part):
    key = jax.random.fold_in(key, 7)
    shape = (REQUESTS * Q_LEN, QH * HD)
    values = jnp.clip(jax.random.normal(key, shape, jnp.float32), -6.0, 6.0)
    return values.astype(jnp.bfloat16)


def draw_blend_gain(key, part):
    key = jax.random.fold_in(key, 9)
    steps = jnp.arange(KVH, dtype=jnp.float32)[:, None] / max(KVH - 1, 1)
    spread = jax.random.uniform(key, (KVH, 2 * HD), jnp.float32, 0.7, 1.4)
    base = 4.0 * 3.0 ** steps
    return base * spread


def draw_doc_lists(key, part):
    key = jax.random.fold_in(key, 13)
    order_key, local_key = jax.random.split(key)
    homes = REQUESTS // REQ_DEV
    home_keys = jax.random.split(order_key, homes)
    entry_ids = jnp.arange(REQ_DEV * SLOTS, dtype=jnp.int32) % homes

    def one_home(home_key):
        holders = jax.random.permutation(home_key, homes).astype(jnp.int32)
        return holders[entry_ids]
    holders = jax.vmap(one_home)(home_keys).reshape(REQUESTS, SLOTS)
    local = jax.random.randint(local_key, (REQUESTS, SLOTS), 0, DOC_DEV)
    return (holders * DOC_DEV + local).astype(jnp.int32)


def draw_doc_counts(key, part):
    key = jax.random.fold_in(key, 17)
    count_key, top_key, low_key = jax.random.split(key, 3)
    counts = jax.random.randint(count_key, (REQUESTS,), 8, SLOTS + 1)
    top_at = jax.random.randint(top_key, (), 0, REQUESTS)
    low_at = (top_at + 1 + jax.random.randint(low_key, (), 0, REQUESTS - 1)) % REQUESTS
    spots = jnp.arange(REQUESTS, dtype=jnp.int32)
    counts = jnp.where(spots == top_at, SLOTS, counts)
    counts = jnp.where(spots == low_at, 8, counts)
    return counts.astype(jnp.int32)


def level_of(rng, extent, shards, smallest, largest):
    loudness, own = 1.0, jax.random.fold_in(rng, 6)
    for axis_at, blocks in shards:
        heights = jnp.exp(jax.random.uniform(jax.random.fold_in(own, axis_at), (blocks,), jnp.float32, smallest / len(shards), largest / len(shards)))
        loudness = loudness * jnp.repeat(heights, extent[axis_at] // blocks).reshape([-1 if axis == axis_at else 1 for axis in range(len(extent))])
    return loudness


def bell_draw(stream_key, dims, scale, most, pieces=(), kind=jnp.bfloat16):
    result = scale * jax.random.normal(stream_key, dims, jnp.float32)
    if pieces:
        result = result * level_of(stream_key, dims, pieces, -0.22, 0.18)
    return jnp.clip(result, -most, most).astype(kind)


def setup_inputs(seed: int = 0) -> dict:
    splits = jax.random.split(jax.random.key(seed), 8)
    return {
        "queries": draw_queries(jax.random.fold_in(splits[7], 71), 0),
        "own_kv": bell_draw(splits[1], (REQUESTS * Q_LEN, KVH * 2 * HD), 1.0, 6.0, ((0, 64), (1, 8))),
        "cache": draw_cache(jax.random.fold_in(splits[7], 71), 0),
        "doc_lists": draw_doc_lists(jax.random.fold_in(splits[7], 71), 0),
        "doc_counts": draw_doc_counts(jax.random.fold_in(splits[7], 71), 0),
        "dev_pos": draw_dev_pos(jax.random.fold_in(splits[7], 71), 0),
        "blend_gain": draw_blend_gain(jax.random.fold_in(splits[7], 71), 0),
    }


very_low = -1e30


def start_state(head_rows, own, dev_rows):
    width = own.shape[1]
    head_dim = width // 2
    group = head_rows.shape[0] // own.shape[0]
    scores = jnp.dot(head_rows, own[:, :head_dim].T, preferred_element_type=jnp.float32) * (head_dim ** -0.5)
    token = jnp.arange(head_rows.shape[0], dtype=jnp.int32) // group
    causal = token[:, None] >= jnp.arange(own.shape[0], dtype=jnp.int32)[None, :]
    maxima = jnp.max(jnp.where(causal, scores, very_low), axis=1)
    weights = jnp.where(causal, jnp.exp(scores - maxima[:, None]), 0.0)
    totals = jnp.sum(weights, axis=1)
    summed = jnp.dot(weights.astype(jnp.bfloat16), own[:, head_dim:], preferred_element_type=jnp.float32)
    dev_count = dev_rows.shape[0]
    return (maxima, totals, summed, jnp.full((dev_count,), very_low, jnp.float32),
            jnp.zeros((dev_count,), jnp.float32), jnp.zeros((dev_count, width), jnp.float32))


def slot_step(state, block, slot, head_rows, dev_rows, dev_slot):
    maxima, totals, summed, dev_max, dev_tot, dev_sum = state
    head_dim = head_rows.shape[1]
    scale = head_dim ** -0.5
    keys = block[:, :head_dim]
    scores = jnp.dot(head_rows, keys.T, preferred_element_type=jnp.float32) * scale
    new_max = jnp.maximum(maxima, jnp.max(scores, axis=1))
    factor = jnp.exp(maxima - new_max)
    weights = jnp.exp(scores - new_max[:, None])
    totals = totals * factor + jnp.sum(weights, axis=1)
    summed = summed * factor[:, None] + jnp.dot(weights.astype(jnp.bfloat16), block[:, head_dim:], preferred_element_type=jnp.float32)
    dev_scores = jnp.dot(dev_rows[:, :head_dim], keys.T, preferred_element_type=jnp.float32) * scale
    valid = (dev_slot >= slot)[:, None]
    dev_new = jnp.maximum(dev_max, jnp.max(jnp.where(valid, dev_scores, very_low), axis=1))
    dev_factor = jnp.exp(dev_max - dev_new)
    dev_weights = jnp.where(valid, jnp.exp(dev_scores - dev_new[:, None]), 0.0)
    dev_tot = dev_tot * dev_factor + jnp.sum(dev_weights, axis=1)
    dev_sum = dev_sum * dev_factor[:, None] + jnp.dot(dev_weights.astype(jnp.bfloat16), block, preferred_element_type=jnp.float32)
    return (new_max, totals, summed, dev_new, dev_tot, dev_sum)


def finish(state, dev_rows, gain, tokens):
    maxima, totals, summed, dev_max, dev_tot, dev_sum = state
    head_out = (summed / totals[:, None]).astype(jnp.bfloat16).reshape(tokens, -1)
    correction = dev_sum / dev_tot[:, None]
    delta = gain[None, :] * correction
    updated = (dev_rows.astype(jnp.float32) + delta).astype(jnp.bfloat16)
    squares = jnp.mean(delta * delta, axis=1)
    return head_out, updated, squares


def head_work(head_rows, own, context_head, dev_head, gain, count, tokens):
    state = start_state(head_rows, own, dev_head)
    dev_slot = jnp.arange(dev_head.shape[0], dtype=jnp.int32) // DEV_TOK

    def advance(carry, inputs):
        block, slot = inputs
        moved = slot_step(carry, block, slot, head_rows, dev_head, dev_slot)
        keep = slot < count
        return jax.tree.map(lambda new_val, old_val: jnp.where(keep, new_val, old_val), moved, carry), None

    state, _ = lax.scan(advance, state, (context_head, jnp.arange(SLOTS, dtype=jnp.int32)))
    return finish(state, dev_head, gain, tokens)


def reference(queries, own_kv, cache, doc_lists, doc_counts, dev_pos, blend_gain):
    width = 2 * HD
    group = QH // KVH
    blocks = cache.reshape(DOCS, DOC_LEN, KVH * width)
    dev_cache = jnp.take_along_axis(blocks, dev_pos[:, :, None], axis=1)

    def one_request(request):
        chosen = doc_lists[request]
        count = doc_counts[request]
        context = blocks[chosen]
        context_dev = dev_cache[chosen]
        query_rows = lax.dynamic_slice_in_dim(queries, request * Q_LEN, Q_LEN, 0)
        own_rows = lax.dynamic_slice_in_dim(own_kv, request * Q_LEN, Q_LEN, 0)
        outputs = []
        updates = []
        total = jnp.zeros((SLOTS * DEV_TOK,), jnp.float32)
        for head in range(KVH):
            head_rows = query_rows[:, head * group * HD:(head + 1) * group * HD].reshape(Q_LEN * group, HD)
            lower = head * width
            upper = (head + 1) * width
            head_out, updated, squares = head_work(
                head_rows, own_rows[:, lower:upper], context[:, :, lower:upper],
                context_dev[:, :, lower:upper].reshape(SLOTS * DEV_TOK, width),
                blend_gain[head], count, Q_LEN)
            outputs.append(head_out)
            updates.append(updated)
            total = total + squares
        return (jnp.concatenate(outputs, axis=1),
                jnp.concatenate(updates, axis=1).reshape(SLOTS, DEV_TOK, KVH * width),
                (total / KVH).reshape(SLOTS, DEV_TOK))

    att, updates, scores = lax.map(one_request, jnp.arange(REQUESTS, dtype=jnp.int32))
    live = jnp.arange(SLOTS, dtype=jnp.int32)[None, :] < doc_counts[:, None]
    dev_score = jnp.where(live[:, :, None], scores, 0.0).astype(jnp.float32)
    entries = REQ_DEV * SLOTS
    owners = (doc_lists // DOC_DEV).reshape(N_DOCS, entries)
    same = owners[:, :, None] == owners[:, None, :]
    earlier = jnp.arange(entries, dtype=jnp.int32)[None, :] < jnp.arange(entries, dtype=jnp.int32)[:, None]
    ranks = jnp.sum((same & earlier[None]).astype(jnp.int32), axis=2)
    flat = owners * (N_DOCS * CAP) + jnp.arange(N_DOCS, dtype=jnp.int32)[:, None] * CAP + ranks
    values = jnp.where(live[:, :, None, None], updates, jnp.zeros((), jnp.bfloat16))
    returned_kv = jnp.zeros((N_DOCS * N_DOCS * CAP, DEV_TOK, KVH * width), jnp.bfloat16)
    returned_kv = returned_kv.at[flat.reshape(-1)].set(values.reshape(REQUESTS * SLOTS, DEV_TOK, KVH * width))
    return att.reshape(REQUESTS * Q_LEN, QH * HD), returned_kv, dev_score
```

```python
import functools

import jax
import jax.numpy as jnp
from jax import lax
from jax.experimental import pallas as pl
from jax.experimental.pallas import tpu as pltpu
from jax.sharding import PartitionSpec as P

KVH = 8
REQ_DEV = 2
DOC_DEV = 6
NZ = 16
very_low = -1e30
VMEM = pltpu.VMEM
SMEM = pltpu.SMEM
LOG2E = 1.4426950408889634
GROUPS = 4


def whole(space):
    return pl.BlockSpec(memory_space=space)


def place(ny, y, z):
    return lax.rem(y + 2 * ny, ny) * NZ + lax.rem(z + 2 * NZ, NZ)


def gather_kernel(ny, sel_ref, cache_ref, ctx_ref, *scratch):
    half = NZ // 2
    full = half - 1
    plus = scratch[:full]
    minus = scratch[full : 2 * full]
    far, picked, zsend, zrecv, ysend, yrecv, local_sem = scratch[2 * full :]
    me = lax.axis_index("docs")
    y, z = me // NZ, lax.rem(me, NZ)
    part = DOC_DEV // 2

    barrier = pltpu.get_barrier_semaphore()
    partners = [place(ny, y, z + 1), place(ny, y, z - 1)]
    partners += [place(ny, y + t, z) for t in range(1, ny)]
    for partner in partners:
        pl.semaphore_signal(barrier, inc=1, device_id={"docs": partner}, device_id_type=pl.DeviceIdType.MESH)
    pl.semaphore_wait(barrier, len(partners))

    def ring(way, step, chunk):
        bufs = plus if way == 0 else minus
        src = cache_ref if step == 1 else bufs[step - 2]
        dst = far if step == half else bufs[step - 1]
        rows = pl.ds(chunk * part, part)
        return pltpu.make_async_remote_copy(
            src_ref=src.at[rows],
            dst_ref=dst.at[rows],
            send_sem=zsend.at[way, step - 1, chunk],
            recv_sem=zrecv.at[way, step - 1, chunk],
            device_id={"docs": partners[way]},
            device_id_type=pl.DeviceIdType.MESH,
        )

    def across(t, j):
        return pltpu.make_async_remote_copy(
            src_ref=picked.at[t, j],
            dst_ref=ctx_ref.at[t * NZ + j],
            send_sem=ysend.at[t, j],
            recv_sem=yrecv.at[t, j],
            device_id={"docs": place(ny, y + t, z)},
            device_id_type=pl.DeviceIdType.MESH,
        )

    def keep(j):
        return pltpu.make_async_copy(picked.at[0, j], ctx_ref.at[j], local_sem.at[j])

    def pick(buf, j):
        for t in list(range(1, ny)) + [0]:
            picked[t, j] = buf[sel_ref[t * NZ + j]]
            if t:
                across(t, j).start()
            else:
                keep(j).start()

    for chunk in range(2):
        for way in range(2):
            ring(way, 1, chunk).start()
    pick(cache_ref, 0)
    for step in range(1, half):
        for chunk in range(2):
            for way in range(2):
                ring(way, step, chunk).wait_recv()
                if step < full or chunk == way:
                    ring(way, step + 1, chunk).start()
        pick(plus[step - 1], step)
        pick(minus[step - 1], NZ - step)
    for way in range(2):
        ring(way, half, way).wait_recv()
    pick(far, half)
    for way in range(2):
        for step in range(1, half + 1):
            for chunk in range(2):
                if step < half or chunk == way:
                    ring(way, step, chunk).wait_send()
    for j in range(NZ):
        for t in range(1, ny):
            across(t, j).wait()
        keep(j).wait()


def gather_docs(sel, cache):
    peers = lax.axis_size("docs")
    ny = peers // NZ
    full = NZ // 2 - 1
    block = cache.shape
    one = block[1:]
    return pl.pallas_call(
        functools.partial(gather_kernel, ny),
        out_shape=jax.ShapeDtypeStruct((peers,) + one, cache.dtype),
        in_specs=[whole(SMEM), whole(VMEM)],
        out_specs=whole(pl.ANY),
        scratch_shapes=[VMEM(block, cache.dtype)] * (2 * full + 1)
        + [
            VMEM((ny, NZ) + one, cache.dtype),
            pltpu.SemaphoreType.DMA((2, NZ // 2, 2)),
            pltpu.SemaphoreType.DMA((2, NZ // 2, 2)),
            pltpu.SemaphoreType.DMA((ny, NZ)),
            pltpu.SemaphoreType.DMA((ny, NZ)),
            pltpu.SemaphoreType.DMA((NZ,)),
        ],
        compiler_params=pltpu.CompilerParams(
            collective_id=0, has_side_effects=True, vmem_limit_bytes=24 * 2**20
        ),
        cost_estimate=pl.CostEstimate(flops=0, bytes_accessed=200 * 10**6, transcendentals=0),
        name="gather_docs",
    )(sel, cache)


def dev_kernel(slots, slot_ref, count_ref, ctx_ref, pos_ref, gain_ref, upd_ref, sq_ref, kv, dev, sems):
    entries = REQ_DEV * slots
    doc_len, width = ctx_ref.shape[1:]
    head_dim = width // 2
    dev_tok = pos_ref.shape[0] // entries
    group = slots // GROUPS
    scale = head_dim ** (-0.5)

    def bring(e):
        return pltpu.make_async_copy(
            ctx_ref.at[slot_ref[e]], kv.at[pl.ds(e * doc_len, doc_len)], sems.at[e]
        )

    for e in range(entries):
        bring(e).start()
    upd_ref[...] = jnp.zeros_like(upd_ref)
    token = lax.broadcasted_iota(jnp.int32, (dev_tok, doc_len), 1)
    for r in range(REQ_DEV):
        count = count_ref[r]
        base = r * slots * doc_len
        for e in range(r * slots, (r + 1) * slots):
            bring(e).wait()
        for e in range(r * slots, (r + 1) * slots):
            hot = (pos_ref[e * dev_tok : (e + 1) * dev_tok] == token).astype(jnp.bfloat16)
            dev[e * dev_tok : (e + 1) * dev_tok] = jnp.dot(
                hot, kv[e * doc_len : (e + 1) * doc_len], preferred_element_type=jnp.float32
            )
        for g in range(GROUPS):
            first = r * slots + g * group
            rows = slice(first * dev_tok, (first + group) * dev_tok)
            tokens = (g + 1) * group * doc_len

            @pl.when(g * group < count)
            def _():
                mine = dev[rows]
                keys = kv[base : base + tokens, :head_dim]
                scores = lax.dot_general(
                    mine[:, :head_dim].astype(jnp.bfloat16),
                    keys,
                    (((1,), (1,)), ((), ())),
                    preferred_element_type=jnp.float32,
                )
                row_slot = lax.broadcasted_iota(jnp.int32, scores.shape, 0) // dev_tok + g * group
                key_slot = lax.broadcasted_iota(jnp.int32, scores.shape, 1) // doc_len
                scores = jnp.where(row_slot >= key_slot, scores, very_low)
                top = jnp.max(scores, axis=1, keepdims=True)
                weights = jnp.exp2((scores - top) * (scale * LOG2E))
                total = jnp.sum(weights, axis=1, keepdims=True)
                summed = jnp.dot(
                    weights.astype(jnp.bfloat16),
                    kv[base : base + tokens],
                    preferred_element_type=jnp.float32,
                )
                delta = gain_ref[...] * (summed / total)
                fresh = mine + delta
                square = jnp.sum(delta * delta, axis=1, keepdims=True) * (1.0 / width)
                sq_ref[rows] = jnp.broadcast_to(square, (group * dev_tok, 128))
                for i in range(group):

                    @pl.when(g * group + i < count)
                    def _():
                        one = fresh[i * dev_tok : (i + 1) * dev_tok]
                        upd_ref[slot_ref[first + i]] = jnp.concatenate(
                            [one[:, :head_dim], one[:, head_dim:]], axis=0
                        ).astype(jnp.bfloat16)

            @pl.when(g * group >= count)
            def _():
                sq_ref[rows] = jnp.zeros((group * dev_tok, 128), jnp.float32)


def deviations(slots, slot_of, counts, ctx, pos, gain):
    entries = REQ_DEV * slots
    peers, doc_len, width = ctx.shape
    dev_tok = pos.shape[0] // entries
    return pl.pallas_call(
        functools.partial(dev_kernel, slots),
        out_shape=(
            jax.ShapeDtypeStruct((peers, 2 * dev_tok, width // 2), jnp.bfloat16),
            jax.ShapeDtypeStruct((entries * dev_tok, 128), jnp.float32),
        ),
        in_specs=[whole(SMEM), whole(SMEM), whole(pl.ANY), whole(VMEM), whole(VMEM)],
        out_specs=(whole(VMEM), whole(VMEM)),
        scratch_shapes=[
            VMEM((entries * doc_len, width), jnp.bfloat16),
            VMEM((entries * dev_tok, width), jnp.float32),
            pltpu.SemaphoreType.DMA((entries,)),
        ],
        compiler_params=pltpu.CompilerParams(vmem_limit_bytes=40 * 2**20),
        cost_estimate=pl.CostEstimate(
            flops=2 * 2 * 480 * 2560 * 384, bytes_accessed=5 * 10**6, transcendentals=2 * 10**6
        ),
        name="deviations",
    )(slot_of, counts, ctx, pos, gain)


def attend_kernel(
    ny, slots, slot_ref, count_ref, ctx_ref, upd_ref, q_ref, own_ref, att_ref, ret_ref, ctx, kv, send, recv, local_sem
):
    peers, doc_len, width = ctx_ref.shape
    head_dim = width // 2
    tokens = own_ref.shape[0] // REQ_DEV
    group = q_ref.shape[1] // head_dim
    span = kv.shape[0]
    scale = head_dim ** (-0.5)
    me = lax.axis_index("docs")
    y, z = me // NZ, lax.rem(me, NZ)

    stage = pltpu.make_async_copy(ctx_ref, ctx, local_sem.at[0])
    stage.start()
    barrier = pltpu.get_barrier_semaphore()

    def greet(s, carry):
        pl.semaphore_signal(
            barrier,
            inc=1,
            device_id={"docs": place(ny, y - s // NZ, z - lax.rem(s, NZ))},
            device_id_type=pl.DeviceIdType.MESH,
        )
        return carry

    lax.fori_loop(1, peers, greet, 0)
    pl.semaphore_wait(barrier, peers - 1)

    def back(s):
        return pltpu.make_async_remote_copy(
            src_ref=upd_ref.at[s],
            dst_ref=ret_ref.at[me],
            send_sem=send.at[s],
            recv_sem=recv.at[s],
            device_id={"docs": place(ny, y - s // NZ, z - lax.rem(s, NZ))},
            device_id_type=pl.DeviceIdType.MESH,
        )

    def launch(i, carry):
        back(i).start()
        return carry

    lax.fori_loop(1, peers, launch, 0)
    mine = pltpu.make_async_copy(upd_ref.at[0], ret_ref.at[me], local_sem.at[1])
    mine.start()

    row = lax.broadcasted_iota(jnp.int32, (tokens, span - slots * doc_len), 0)
    col = lax.broadcasted_iota(jnp.int32, (tokens, span - slots * doc_len), 1)
    causal = row >= col
    used = lax.broadcasted_iota(jnp.int32, (1, slots * doc_len), 1)
    kv[slots * doc_len :] = jnp.zeros((span - slots * doc_len, width), kv.dtype)
    stage.wait()
    for r in range(REQ_DEV):
        count = count_ref[r]

        def load(k, carry):
            kv[pl.ds(pl.multiple_of(k * doc_len, doc_len), doc_len)] = ctx[slot_ref[r * slots + k]]
            return carry

        lax.fori_loop(0, slots, load, 0)
        kv[slots * doc_len : slots * doc_len + tokens] = own_ref[r * tokens : (r + 1) * tokens]
        live = used < count * doc_len

        def head(i, carry):
            cols = pl.ds(pl.multiple_of(i * head_dim, head_dim), head_dim)
            scores = lax.dot_general(
                q_ref[r * tokens : (r + 1) * tokens, cols],
                kv[:, :head_dim],
                (((1,), (1,)), ((), ())),
                preferred_element_type=jnp.float32,
            )
            docs = jnp.where(live, scores[:, : slots * doc_len], very_low)
            self = jnp.where(causal, scores[:, slots * doc_len :], very_low)
            top = jnp.maximum(
                jnp.max(docs, axis=1, keepdims=True), jnp.max(self, axis=1, keepdims=True)
            )
            docs = jnp.exp2((docs - top) * (scale * LOG2E))
            self = jnp.exp2((self - top) * (scale * LOG2E))
            total = jnp.sum(docs, axis=1, keepdims=True) + jnp.sum(self, axis=1, keepdims=True)
            summed = jnp.dot(
                docs.astype(jnp.bfloat16),
                kv[: slots * doc_len, head_dim:],
                preferred_element_type=jnp.float32,
            ) + jnp.dot(
                self.astype(jnp.bfloat16),
                kv[slots * doc_len :, head_dim:],
                preferred_element_type=jnp.float32,
            )
            att_ref[r * tokens : (r + 1) * tokens, cols] = (summed / total).astype(jnp.bfloat16)
            return carry

        lax.fori_loop(0, group, head, 0)

    def land(i, carry):
        back(i).wait()
        return carry

    lax.fori_loop(1, peers, land, 0)
    mine.wait()


def attend_and_return(slots, slot_of, counts, ctx, upd, queries, own):
    peers, doc_len, width = ctx.shape
    ny = peers // NZ
    tokens = own.shape[0] // REQ_DEV
    span = slots * doc_len + (tokens + 127) // 128 * 128
    return pl.pallas_call(
        functools.partial(attend_kernel, ny, slots),
        out_shape=(
            jax.ShapeDtypeStruct(queries.shape, jnp.bfloat16),
            jax.ShapeDtypeStruct(upd.shape, jnp.bfloat16),
        ),
        in_specs=[whole(SMEM), whole(SMEM), whole(pl.ANY), whole(pl.ANY), whole(VMEM), whole(VMEM)],
        out_specs=(whole(VMEM), whole(pl.ANY)),
        scratch_shapes=[
            VMEM(ctx.shape, ctx.dtype),
            VMEM((span, width), ctx.dtype),
            pltpu.SemaphoreType.DMA((peers,)),
            pltpu.SemaphoreType.DMA((peers,)),
            pltpu.SemaphoreType.DMA((2,)),
        ],
        compiler_params=pltpu.CompilerParams(
            collective_id=1, has_side_effects=True, vmem_limit_bytes=40 * 2**20
        ),
        cost_estimate=pl.CostEstimate(
            flops=9 * 10**9, bytes_accessed=100 * 10**6, transcendentals=9 * 10**6
        ),
        name="attend_and_return",
    )(slot_of, counts, ctx, upd, queries, own)


def shards(queries, own_kv, cache, doc_lists, doc_counts, dev_pos, blend_gain):
    width = blend_gain.shape[1]
    head_dim = width // 2
    peers = lax.axis_size("docs")
    ny = peers // NZ
    me = lax.axis_index("docs")
    y, z = me // NZ, me % NZ
    slots = doc_lists.shape[1]
    entries = REQ_DEV * slots
    dev_tok = dev_pos.shape[1]
    doc_len = cache.shape[0] // DOC_DEV
    combined = doc_lists.reshape(peers, entries)

    row_lists = jnp.roll(combined.reshape(ny, NZ, entries)[:, z], -y, axis=0)
    row_owner = row_lists // DOC_DEV
    steps = jnp.arange(NZ, dtype=jnp.int32)
    passing = y * NZ + (z - steps) % NZ
    hits = row_owner[:, :, None] == passing[None, None, :]
    sel = jnp.sum(jnp.where(hits, (row_lists % DOC_DEV)[:, :, None], 0), axis=1).reshape(-1)

    mine = combined[me]
    owner = mine // DOC_DEV
    slot_of = ((y - owner // NZ) % ny) * NZ + (z - owner % NZ) % NZ
    counts = lax.dynamic_slice_in_dim(doc_counts, me * REQ_DEV, REQ_DEV, 0)

    all_pos = lax.all_gather(dev_pos, "docs", axis=0, tiled=True)
    ctx = gather_docs(sel.astype(jnp.int32), cache.reshape(DOC_DEV, doc_len, width))
    pos = jnp.broadcast_to(all_pos[mine].reshape(-1, 1), (entries * dev_tok, doc_len))
    upd, squares = deviations(slots, slot_of, counts, ctx, pos, blend_gain)
    scores = lax.psum(squares[:, 0], "heads") / KVH
    live = jnp.arange(slots, dtype=jnp.int32)[None, :] < counts[:, None]
    dev_score = jnp.where(live[:, :, None], scores.reshape(REQ_DEV, slots, dev_tok), 0.0)
    att, ret = attend_and_return(slots, slot_of, counts, ctx, upd, queries, own_kv)
    returned = jnp.concatenate([ret[:, :dev_tok], ret[:, dev_tok:]], axis=2)
    return att, returned, dev_score


def solution(mesh):
    return jax.shard_map(
        shards,
        mesh=mesh,
        in_specs=(
            P("docs", "heads"),
            P("docs", "heads"),
            P("docs", "heads"),
            P(),
            P(),
            P("docs", None),
            P("heads", None),
        ),
        out_specs=(P("docs", "heads"), P("docs", None, "heads"), P("docs", None, None)),
        check_vma=False,
    )
```

```python
import functools

import jax
import jax.numpy as jnp
from jax import lax
from jax.experimental import pallas as pl
from jax.experimental.pallas import tpu as pltpu
from jax.sharding import PartitionSpec as P

KVH = 8
REQ_DEV = 2
DOC_DEV = 6
NZ = 16
very_low = -1e30
VMEM = pltpu.VMEM
SMEM = pltpu.SMEM
LOG2E = 1.4426950408889634
GROUPS = 4
WINDOW = 3


def whole(space):
    return pl.BlockSpec(memory_space=space)


def place(ny, y, z):
    return lax.rem(y + 2 * ny, ny) * NZ + lax.rem(z + 2 * NZ, NZ)


def gather_kernel(ny, sel_ref, cache_ref, pos_ref, ctx_ref, allpos_ref, *scratch):
    half = NZ // 2
    full = half - 1
    plus = scratch[:full]
    minus = scratch[full : 2 * full]
    far, picked, ring_pos, zsend, zrecv, ysend, yrecv, psend, precv, local_sem = scratch[2 * full :]
    me = lax.axis_index("docs")
    y, z = me // NZ, lax.rem(me, NZ)
    part = DOC_DEV // 2

    barrier = pltpu.get_barrier_semaphore()
    partners = [place(ny, y, z + 1), place(ny, y, z - 1)]
    partners += [place(ny, y + t, z) for t in range(1, ny)]
    for partner in partners:
        pl.semaphore_signal(barrier, inc=1, device_id={"docs": partner}, device_id_type=pl.DeviceIdType.MESH)
    ring_pos[0] = pos_ref[...]
    pl.semaphore_wait(barrier, len(partners))

    order = [(step, doc) for step in range(1, half) for doc in range(DOC_DEV)]
    orders = [order + [(half, way * part + doc) for doc in range(part)] for way in range(2)]

    def ring(way, step, doc):
        bufs = plus if way == 0 else minus
        src = cache_ref if step == 1 else bufs[step - 2]
        dst = far if step == half else bufs[step - 1]
        return pltpu.make_async_remote_copy(
            src_ref=src.at[doc],
            dst_ref=dst.at[doc],
            send_sem=zsend.at[way, step - 1, doc],
            recv_sem=zrecv.at[way, step - 1, doc],
            device_id={"docs": partners[way]},
            device_id_type=pl.DeviceIdType.MESH,
        )

    def ring_of_pos(way, step):
        src, dst = (step - 1, step) if way == 0 else ((NZ - step + 1) % NZ, NZ - step)
        return pltpu.make_async_remote_copy(
            src_ref=ring_pos.at[src],
            dst_ref=ring_pos.at[dst],
            send_sem=psend.at[way, step],
            recv_sem=precv.at[way, step],
            device_id={"docs": partners[way]},
            device_id_type=pl.DeviceIdType.MESH,
        )

    def pos_across(t):
        return pltpu.make_async_remote_copy(
            src_ref=ring_pos,
            dst_ref=allpos_ref.at[t],
            send_sem=psend.at[0, half + t],
            recv_sem=precv.at[0, half + t],
            device_id={"docs": place(ny, y + t, z)},
            device_id_type=pl.DeviceIdType.MESH,
        )

    def across(t, j):
        return pltpu.make_async_remote_copy(
            src_ref=picked.at[t, j],
            dst_ref=ctx_ref.at[t * NZ + j],
            send_sem=ysend.at[t, j],
            recv_sem=yrecv.at[t, j],
            device_id={"docs": place(ny, y + t, z)},
            device_id_type=pl.DeviceIdType.MESH,
        )

    def keep(j):
        return pltpu.make_async_copy(picked.at[0, j], ctx_ref.at[j], local_sem.at[j])

    keep_pos = pltpu.make_async_copy(ring_pos, allpos_ref.at[0], local_sem.at[NZ])

    def pick(buf, j):
        for t in list(range(1, ny)) + [0]:
            picked[t, j] = buf[sel_ref[t * NZ + j]]
            if t:
                across(t, j).start()
            else:
                keep(j).start()

    for n in range(len(orders[0])):
        for way in range(2):
            step, doc = orders[way][n]
            if step > 1:
                ring(way, step - 1, doc).wait_recv()
            if n >= WINDOW:
                ring(way, *orders[way][n - WINDOW]).wait_send()
            ring(way, step, doc).start()
        step, doc = order[n] if n < len(order) else (half, n - len(order))
        if doc == 0:
            for way in range(2):
                if step > 1 and (way == 0 or step <= half):
                    ring_of_pos(way, step - 1).wait_recv()
                if way == 0 or step < half:
                    ring_of_pos(way, step).start()
        if n == WINDOW - 1:
            pick(cache_ref, 0)
        if step > 1 and step < half and doc == DOC_DEV - 1:
            pick(plus[step - 2], step - 1)
            pick(minus[step - 2], NZ - step + 1)
    for way in range(2):
        for doc in range(DOC_DEV):
            if not part * way <= doc < part * (way + 1):
                ring(way, full, doc).wait_recv()
    pick(plus[full - 1], full)
    pick(minus[full - 1], NZ - full)
    ring_of_pos(0, half).wait_recv()
    for t in range(1, ny):
        pos_across(t).start()
    keep_pos.start()
    for way in range(2):
        for doc in range(part):
            ring(way, half, way * part + doc).wait_recv()
    pick(far, half)
    for way in range(2):
        for n in range(len(orders[way]) - WINDOW, len(orders[way])):
            ring(way, *orders[way][n]).wait_send()
        for step in range(1, half + 1):
            if way == 0 or step < half:
                ring_of_pos(way, step).wait_send()
    for j in range(NZ):
        for t in range(1, ny):
            across(t, j).wait()
        keep(j).wait()
    for t in range(1, ny):
        pos_across(t).wait()
    keep_pos.wait()


def gather_docs(sel, cache, pos):
    peers = lax.axis_size("docs")
    ny = peers // NZ
    full = NZ // 2 - 1
    block = cache.shape
    one = block[1:]
    return pl.pallas_call(
        functools.partial(gather_kernel, ny),
        out_shape=(
            jax.ShapeDtypeStruct((peers,) + one, cache.dtype),
            jax.ShapeDtypeStruct((ny, NZ) + pos.shape, pos.dtype),
        ),
        in_specs=[whole(SMEM), whole(VMEM), whole(VMEM)],
        out_specs=(whole(pl.ANY), whole(pl.ANY)),
        scratch_shapes=[VMEM(block, cache.dtype)] * (2 * full + 1)
        + [
            VMEM((ny, NZ) + one, cache.dtype),
            VMEM((NZ,) + pos.shape, pos.dtype),
            pltpu.SemaphoreType.DMA((2, NZ // 2, DOC_DEV)),
            pltpu.SemaphoreType.DMA((2, NZ // 2, DOC_DEV)),
            pltpu.SemaphoreType.DMA((ny, NZ)),
            pltpu.SemaphoreType.DMA((ny, NZ)),
            pltpu.SemaphoreType.DMA((2, NZ // 2 + ny)),
            pltpu.SemaphoreType.DMA((2, NZ // 2 + ny)),
            pltpu.SemaphoreType.DMA((NZ + 1,)),
        ],
        compiler_params=pltpu.CompilerParams(
            collective_id=0, has_side_effects=True, vmem_limit_bytes=24 * 2**20
        ),
        cost_estimate=pl.CostEstimate(flops=0, bytes_accessed=200 * 10**6, transcendentals=0),
        name="gather_docs",
    )(sel, cache, pos)


def dev_kernel(slots, dev_tok, slot_ref, local_ref, count_ref, ctx_ref, pos_ref, gain_ref, upd_ref, sq_ref, kv, dev, sems):
    entries = REQ_DEV * slots
    doc_len, width = ctx_ref.shape[1:]
    head_dim = width // 2
    group = slots // GROUPS
    scale = head_dim ** (-0.5)

    def bring(e):
        return pltpu.make_async_copy(
            ctx_ref.at[slot_ref[e]], kv.at[pl.ds(e * doc_len, doc_len)], sems.at[e]
        )

    for e in range(entries):
        bring(e).start()
    upd_ref[...] = jnp.zeros_like(upd_ref)
    sq_ref[...] = jnp.zeros_like(sq_ref)
    token = lax.broadcasted_iota(jnp.int32, (doc_len, 128), 0)
    lane_slot = lax.broadcasted_iota(jnp.int32, (1, group * dev_tok), 1) // dev_tok
    for r in range(REQ_DEV):
        count = count_ref[r]
        base = r * slots * doc_len
        for e in range(r * slots, (r + 1) * slots):
            bring(e).wait()
        for e in range(r * slots, (r + 1) * slots):
            where = pos_ref[pl.ds(slot_ref[e] * 8 + local_ref[e], 1)]
            hot = (where == token).astype(jnp.bfloat16)
            rows_of = lax.dot_general(
                hot,
                kv[e * doc_len : (e + 1) * doc_len],
                (((0,), (0,)), ((), ())),
                preferred_element_type=jnp.float32,
            )
            dev[e * dev_tok : (e + 1) * dev_tok] = rows_of[:dev_tok]
        for g in range(GROUPS):
            first = r * slots + g * group
            rows = slice(first * dev_tok, (first + group) * dev_tok)
            tokens = (g + 1) * group * doc_len

            @pl.when(g * group < count)
            def _():
                mine = dev[rows]
                keys = kv[base : base + tokens, :head_dim]
                scores = lax.dot_general(
                    mine[:, :head_dim].astype(jnp.bfloat16),
                    keys,
                    (((1,), (1,)), ((), ())),
                    preferred_element_type=jnp.float32,
                )
                row_slot = lax.broadcasted_iota(jnp.int32, scores.shape, 0) // dev_tok + g * group
                key_slot = lax.broadcasted_iota(jnp.int32, scores.shape, 1) // doc_len
                scores = jnp.where(row_slot >= key_slot, scores, very_low)
                top = jnp.max(scores, axis=1, keepdims=True)
                weights = jnp.exp2((scores - top) * (scale * LOG2E))
                total = jnp.sum(weights, axis=1, keepdims=True)
                summed = jnp.dot(
                    weights.astype(jnp.bfloat16),
                    kv[base : base + tokens],
                    preferred_element_type=jnp.float32,
                )
                delta = gain_ref[...] * (summed / total)
                fresh = mine + delta
                square = jnp.sum(delta * delta, axis=1, keepdims=True) * (1.0 / width)
                across_lanes = jnp.broadcast_to(square, (group * dev_tok, 128)).T[:1]
                sq_ref[r * GROUPS + g : r * GROUPS + g + 1, : group * dev_tok] = jnp.where(
                    lane_slot + g * group < count, across_lanes, 0.0
                )
                for i in range(group):

                    @pl.when(g * group + i < count)
                    def _():
                        one = fresh[i * dev_tok : (i + 1) * dev_tok]
                        upd_ref[slot_ref[first + i]] = jnp.concatenate(
                            [one[:, :head_dim], one[:, head_dim:]], axis=0
                        ).astype(jnp.bfloat16)


def deviations(slots, dev_tok, slot_of, local, counts, ctx, pos, gain):
    entries = REQ_DEV * slots
    peers, doc_len, width = ctx.shape
    return pl.pallas_call(
        functools.partial(dev_kernel, slots, dev_tok),
        out_shape=(
            jax.ShapeDtypeStruct((peers, 2 * dev_tok, width // 2), jnp.bfloat16),
            jax.ShapeDtypeStruct((REQ_DEV * GROUPS, 128), jnp.float32),
        ),
        in_specs=[whole(SMEM), whole(SMEM), whole(SMEM), whole(pl.ANY), whole(VMEM), whole(VMEM)],
        out_specs=(whole(VMEM), whole(VMEM)),
        scratch_shapes=[
            VMEM((entries * doc_len, width), jnp.bfloat16),
            VMEM((entries * dev_tok, width), jnp.float32),
            pltpu.SemaphoreType.DMA((entries,)),
        ],
        compiler_params=pltpu.CompilerParams(vmem_limit_bytes=40 * 2**20),
        cost_estimate=pl.CostEstimate(
            flops=2 * 2 * 480 * 2560 * 384, bytes_accessed=5 * 10**6, transcendentals=2 * 10**6
        ),
        name="deviations",
    )(slot_of, local, counts, ctx, pos, gain)


def attend_kernel(
    ny,
    nh,
    slots,
    slot_ref,
    count_ref,
    ctx_ref,
    upd_ref,
    sq_ref,
    q_ref,
    own_ref,
    att_ref,
    ret_ref,
    sum_ref,
    ctx,
    kv,
    parts,
    send,
    recv,
    hsend,
    hrecv,
    local_sem,
):
    peers, doc_len, width = ctx_ref.shape
    head_dim = width // 2
    tokens = own_ref.shape[0] // REQ_DEV
    group = q_ref.shape[1] // head_dim
    span = kv.shape[0]
    scale = head_dim ** (-0.5)
    me = lax.axis_index("docs")
    y, z = me // NZ, lax.rem(me, NZ)

    stage = pltpu.make_async_copy(ctx_ref, ctx, local_sem.at[0])
    stage.start()
    barrier = pltpu.get_barrier_semaphore()

    def greet(s, carry):
        pl.semaphore_signal(
            barrier,
            inc=1,
            device_id={"docs": place(ny, y - s // NZ, z - lax.rem(s, NZ))},
            device_id_type=pl.DeviceIdType.MESH,
        )
        return carry

    lax.fori_loop(1, peers, greet, 0)
    head_at = lax.axis_index("heads")
    fellows = [lax.rem(head_at + k, nh) for k in range(nh)]
    for k in range(1, nh):
        pl.semaphore_signal(barrier, inc=1, device_id={"heads": fellows[k]}, device_id_type=pl.DeviceIdType.MESH)
    pl.semaphore_wait(barrier, peers + nh - 2)

    def back(s):
        return pltpu.make_async_remote_copy(
            src_ref=upd_ref.at[s],
            dst_ref=ret_ref.at[me],
            send_sem=send.at[s],
            recv_sem=recv.at[s],
            device_id={"docs": place(ny, y - s // NZ, z - lax.rem(s, NZ))},
            device_id_type=pl.DeviceIdType.MESH,
        )

    def launch(i, carry):
        back(i).start()
        return carry

    lax.fori_loop(1, peers, launch, 0)
    mine = pltpu.make_async_copy(upd_ref.at[0], ret_ref.at[me], local_sem.at[1])
    mine.start()

    def share(k):
        return pltpu.make_async_remote_copy(
            src_ref=sq_ref,
            dst_ref=parts.at[head_at],
            send_sem=hsend.at[k],
            recv_sem=hrecv.at[k],
            device_id={"heads": fellows[k]},
            device_id_type=pl.DeviceIdType.MESH,
        )

    for k in range(1, nh):
        share(k).start()
    parts[head_at] = sq_ref[...]

    row = lax.broadcasted_iota(jnp.int32, (tokens, span - slots * doc_len), 0)
    col = lax.broadcasted_iota(jnp.int32, (tokens, span - slots * doc_len), 1)
    causal = row >= col
    used = lax.broadcasted_iota(jnp.int32, (1, slots * doc_len), 1)
    kv[slots * doc_len :] = jnp.zeros((span - slots * doc_len, width), kv.dtype)
    stage.wait()
    for r in range(REQ_DEV):
        count = count_ref[r]

        def load(k, carry):
            kv[pl.ds(pl.multiple_of(k * doc_len, doc_len), doc_len)] = ctx[slot_ref[r * slots + k]]
            return carry

        lax.fori_loop(0, slots, load, 0)
        kv[slots * doc_len : slots * doc_len + tokens] = own_ref[r * tokens : (r + 1) * tokens]
        live = used < count * doc_len

        def head(i, carry):
            cols = pl.ds(pl.multiple_of(i * head_dim, head_dim), head_dim)
            scores = lax.dot_general(
                q_ref[r * tokens : (r + 1) * tokens, cols],
                kv[:, :head_dim],
                (((1,), (1,)), ((), ())),
                preferred_element_type=jnp.float32,
            )
            docs = jnp.where(live, scores[:, : slots * doc_len], very_low)
            self = jnp.where(causal, scores[:, slots * doc_len :], very_low)
            top = jnp.maximum(
                jnp.max(docs, axis=1, keepdims=True), jnp.max(self, axis=1, keepdims=True)
            )
            docs = jnp.exp2((docs - top) * (scale * LOG2E))
            self = jnp.exp2((self - top) * (scale * LOG2E))
            total = jnp.sum(docs, axis=1, keepdims=True) + jnp.sum(self, axis=1, keepdims=True)
            summed = jnp.dot(
                docs.astype(jnp.bfloat16),
                kv[: slots * doc_len, head_dim:],
                preferred_element_type=jnp.float32,
            ) + jnp.dot(
                self.astype(jnp.bfloat16),
                kv[slots * doc_len :, head_dim:],
                preferred_element_type=jnp.float32,
            )
            att_ref[r * tokens : (r + 1) * tokens, cols] = (summed / total).astype(jnp.bfloat16)
            return carry

        lax.fori_loop(0, group, head, 0)

    def land(i, carry):
        back(i).wait()
        return carry

    for k in range(1, nh):
        share(k).wait()
    total = parts[0]
    for k in range(1, nh):
        total = total + parts[k]
    sum_ref[...] = total * (1.0 / KVH)
    lax.fori_loop(1, peers, land, 0)
    mine.wait()


def attend_and_return(slots, slot_of, counts, ctx, upd, squares, queries, own):
    peers, doc_len, width = ctx.shape
    ny = peers // NZ
    nh = lax.axis_size("heads")
    tokens = own.shape[0] // REQ_DEV
    span = slots * doc_len + (tokens + 127) // 128 * 128
    return pl.pallas_call(
        functools.partial(attend_kernel, ny, nh, slots),
        out_shape=(
            jax.ShapeDtypeStruct(queries.shape, jnp.bfloat16),
            jax.ShapeDtypeStruct(upd.shape, jnp.bfloat16),
            jax.ShapeDtypeStruct(squares.shape, jnp.float32),
        ),
        in_specs=[whole(SMEM), whole(SMEM), whole(pl.ANY), whole(pl.ANY), whole(VMEM), whole(VMEM), whole(VMEM)],
        out_specs=(whole(VMEM), whole(pl.ANY), whole(VMEM)),
        scratch_shapes=[
            VMEM(ctx.shape, ctx.dtype),
            VMEM((span, width), ctx.dtype),
            VMEM((nh,) + squares.shape, squares.dtype),
            pltpu.SemaphoreType.DMA((peers,)),
            pltpu.SemaphoreType.DMA((peers,)),
            pltpu.SemaphoreType.DMA((nh,)),
            pltpu.SemaphoreType.DMA((nh,)),
            pltpu.SemaphoreType.DMA((2,)),
        ],
        compiler_params=pltpu.CompilerParams(
            collective_id=1, has_side_effects=True, vmem_limit_bytes=40 * 2**20
        ),
        cost_estimate=pl.CostEstimate(
            flops=9 * 10**9, bytes_accessed=100 * 10**6, transcendentals=9 * 10**6
        ),
        name="attend_and_return",
    )(slot_of, counts, ctx, upd, squares, queries, own)


def shards(queries, own_kv, cache, doc_lists, doc_counts, dev_pos, blend_gain):
    width = blend_gain.shape[1]
    head_dim = width // 2
    peers = lax.axis_size("docs")
    ny = peers // NZ
    me = lax.axis_index("docs")
    y, z = me // NZ, me % NZ
    slots = doc_lists.shape[1]
    entries = REQ_DEV * slots
    dev_tok = dev_pos.shape[1]
    doc_len = cache.shape[0] // DOC_DEV
    combined = doc_lists.reshape(peers, entries)

    row_lists = jnp.roll(combined.reshape(ny, NZ, entries)[:, z], -y, axis=0)
    row_owner = row_lists // DOC_DEV
    steps = jnp.arange(NZ, dtype=jnp.int32)
    passing = y * NZ + (z - steps) % NZ
    hits = row_owner[:, :, None] == passing[None, None, :]
    sel = jnp.sum(jnp.where(hits, (row_lists % DOC_DEV)[:, :, None], 0), axis=1).reshape(-1)

    mine = combined[me]
    owner = mine // DOC_DEV
    slot_of = ((y - owner // NZ) % ny) * NZ + (z - owner % NZ) % NZ
    counts = lax.dynamic_slice_in_dim(doc_counts, me * REQ_DEV, REQ_DEV, 0)

    pos = jnp.pad(dev_pos, ((0, 8 - DOC_DEV), (0, 128 - dev_tok)), constant_values=-1)
    ctx, all_pos = gather_docs(sel.astype(jnp.int32), cache.reshape(DOC_DEV, doc_len, width), pos)
    upd, squares = deviations(
        slots, dev_tok, slot_of, mine % DOC_DEV, counts, ctx, all_pos.reshape(peers * 8, 128), blend_gain
    )
    att, ret, sums = attend_and_return(slots, slot_of, counts, ctx, upd, squares, queries, own_kv)
    group_rows = slots // GROUPS * dev_tok
    dev_score = sums.reshape(REQ_DEV, GROUPS, 128)[:, :, :group_rows].reshape(REQ_DEV, slots, dev_tok)
    returned = jnp.concatenate([ret[:, :dev_tok], ret[:, dev_tok:]], axis=2)
    return att, returned, dev_score


def solution(mesh):
    return jax.shard_map(
        shards,
        mesh=mesh,
        in_specs=(
            P("docs", "heads"),
            P("docs", "heads"),
            P("docs", "heads"),
            P(),
            P(),
            P("docs", None),
            P("heads", None),
        ),
        out_specs=(P("docs", "heads"), P("docs", None, "heads"), P("docs", None, None)),
        check_vma=False,
    )
```

```python
import functools

import jax
import jax.numpy as jnp
from jax import lax
from jax.experimental import pallas as pl
from jax.experimental.pallas import tpu as pltpu
from jax.sharding import PartitionSpec as P

KVH = 8
REQ_DEV = 2
DOC_DEV = 6
NZ = 16
very_low = -1e30
VMEM = pltpu.VMEM
SMEM = pltpu.SMEM
LOG2E = 1.4426950408889634
GROUPS = 4
WINDOW = 3


def whole(space):
    return pl.BlockSpec(memory_space=space)


def place(ny, y, z):
    return lax.rem(y + 2 * ny, ny) * NZ + lax.rem(z + 2 * NZ, NZ)


def gather_kernel(ny, sel_ref, cache_ref, pos_ref, ctx_ref, allpos_ref, *scratch):
    half = NZ // 2
    full = half - 1
    plus = scratch[:full]
    minus = scratch[full : 2 * full]
    far, picked, relay, ring_pos, zsend, zrecv, ysend, yrecv, fsend, frecv, psend, precv, local_sem = scratch[2 * full :]
    me = lax.axis_index("docs")
    y, z = me // NZ, lax.rem(me, NZ)
    part = DOC_DEV // 2

    barrier = pltpu.get_barrier_semaphore()
    partners = [place(ny, y, z + 1), place(ny, y, z - 1)]
    partners += [place(ny, y + t, z) for t in range(1, ny)]
    for partner in partners:
        pl.semaphore_signal(barrier, inc=1, device_id={"docs": partner}, device_id_type=pl.DeviceIdType.MESH)
    ring_pos[0] = pos_ref[...]
    pl.semaphore_wait(barrier, len(partners))

    order = [(step, doc) for step in range(1, half) for doc in range(DOC_DEV)]
    orders = [order + [(half, way * part + doc) for doc in range(part)] for way in range(2)]

    def ring(way, step, doc):
        bufs = plus if way == 0 else minus
        src = cache_ref if step == 1 else bufs[step - 2]
        dst = far if step == half else bufs[step - 1]
        return pltpu.make_async_remote_copy(
            src_ref=src.at[doc],
            dst_ref=dst.at[doc],
            send_sem=zsend.at[way, step - 1, doc],
            recv_sem=zrecv.at[way, step - 1, doc],
            device_id={"docs": partners[way]},
            device_id_type=pl.DeviceIdType.MESH,
        )

    def ring_of_pos(way, step):
        src, dst = (step - 1, step) if way == 0 else ((NZ - step + 1) % NZ, NZ - step)
        return pltpu.make_async_remote_copy(
            src_ref=ring_pos.at[src],
            dst_ref=ring_pos.at[dst],
            send_sem=psend.at[way, step],
            recv_sem=precv.at[way, step],
            device_id={"docs": partners[way]},
            device_id_type=pl.DeviceIdType.MESH,
        )

    def pos_across(t):
        return pltpu.make_async_remote_copy(
            src_ref=ring_pos,
            dst_ref=allpos_ref.at[t],
            send_sem=psend.at[0, half + t],
            recv_sem=precv.at[0, half + t],
            device_id={"docs": place(ny, y + t, z)},
            device_id_type=pl.DeviceIdType.MESH,
        )

    def aside(j):
        return partners[2] if j % 2 == 0 else partners[ny]

    def across(t, j):
        middle = 2 * t == ny
        return pltpu.make_async_remote_copy(
            src_ref=picked.at[t, j],
            dst_ref=relay.at[j] if middle else ctx_ref.at[t * NZ + j],
            send_sem=ysend.at[t, j],
            recv_sem=frecv.at[j] if middle else yrecv.at[t, j],
            device_id={"docs": aside(j) if middle else place(ny, y + t, z)},
            device_id_type=pl.DeviceIdType.MESH,
        )

    def forward(j):
        return pltpu.make_async_remote_copy(
            src_ref=relay.at[j],
            dst_ref=ctx_ref.at[ny // 2 * NZ + j],
            send_sem=fsend.at[j],
            recv_sem=yrecv.at[ny // 2, j],
            device_id={"docs": aside(j)},
            device_id_type=pl.DeviceIdType.MESH,
        )

    def keep(j):
        return pltpu.make_async_copy(picked.at[0, j], ctx_ref.at[j], local_sem.at[j])

    keep_pos = pltpu.make_async_copy(ring_pos, allpos_ref.at[0], local_sem.at[NZ])

    waiting = []

    def pass_on():
        for j in waiting:
            across(ny // 2, j).wait_recv()
            forward(j).start()
        waiting.clear()

    def pick(buf, j):
        for t in [ny // 2] + [t for t in range(1, ny) if 2 * t != ny] + [0]:
            picked[t, j] = buf[sel_ref[t * NZ + j]]
            if t:
                across(t, j).start()
            else:
                keep(j).start()

    for n in range(len(orders[0])):
        for way in range(2):
            step, doc = orders[way][n]
            if step > 1:
                ring(way, step - 1, doc).wait_recv()
            if n >= WINDOW:
                ring(way, *orders[way][n - WINDOW]).wait_send()
            ring(way, step, doc).start()
        step, doc = order[n] if n < len(order) else (half, n - len(order))
        if doc == 0:
            for way in range(2):
                if step > 1 and (way == 0 or step <= half):
                    ring_of_pos(way, step - 1).wait_recv()
                if way == 0 or step < half:
                    ring_of_pos(way, step).start()
        if n == WINDOW - 1:
            pick(cache_ref, 0)
            waiting.append(0)
        if step > 1 and step < half and doc == DOC_DEV - 1:
            pass_on()
            waiting.extend([step - 1, NZ - step + 1])
            pick(plus[step - 2], step - 1)
            pick(minus[step - 2], NZ - step + 1)
    for way in range(2):
        for doc in range(DOC_DEV):
            if not part * way <= doc < part * (way + 1):
                ring(way, full, doc).wait_recv()
    pass_on()
    pick(plus[full - 1], full)
    pick(minus[full - 1], NZ - full)
    waiting.extend([full, NZ - full])
    ring_of_pos(0, half).wait_recv()
    for t in range(1, ny):
        pos_across(t).start()
    keep_pos.start()
    for way in range(2):
        for doc in range(part):
            ring(way, half, way * part + doc).wait_recv()
    pick(far, half)
    waiting.append(half)
    pass_on()
    for way in range(2):
        for n in range(len(orders[way]) - WINDOW, len(orders[way])):
            ring(way, *orders[way][n]).wait_send()
        for step in range(1, half + 1):
            if way == 0 or step < half:
                ring_of_pos(way, step).wait_send()
    for j in range(NZ):
        for t in range(1, ny):
            across(t, j).wait_send()
            if 2 * t == ny:
                forward(j).wait()
            else:
                across(t, j).wait_recv()
        keep(j).wait()
    for t in range(1, ny):
        pos_across(t).wait()
    keep_pos.wait()


def gather_docs(sel, cache, pos):
    peers = lax.axis_size("docs")
    ny = peers // NZ
    full = NZ // 2 - 1
    block = cache.shape
    one = block[1:]
    return pl.pallas_call(
        functools.partial(gather_kernel, ny),
        out_shape=(
            jax.ShapeDtypeStruct((peers,) + one, cache.dtype),
            jax.ShapeDtypeStruct((ny, NZ) + pos.shape, pos.dtype),
        ),
        in_specs=[whole(SMEM), whole(VMEM), whole(VMEM)],
        out_specs=(whole(pl.ANY), whole(pl.ANY)),
        scratch_shapes=[VMEM(block, cache.dtype)] * (2 * full + 1)
        + [
            VMEM((ny, NZ) + one, cache.dtype),
            VMEM((NZ,) + one, cache.dtype),
            VMEM((NZ,) + pos.shape, pos.dtype),
            pltpu.SemaphoreType.DMA((2, NZ // 2, DOC_DEV)),
            pltpu.SemaphoreType.DMA((2, NZ // 2, DOC_DEV)),
            pltpu.SemaphoreType.DMA((ny, NZ)),
            pltpu.SemaphoreType.DMA((ny, NZ)),
            pltpu.SemaphoreType.DMA((NZ,)),
            pltpu.SemaphoreType.DMA((NZ,)),
            pltpu.SemaphoreType.DMA((2, NZ // 2 + ny)),
            pltpu.SemaphoreType.DMA((2, NZ // 2 + ny)),
            pltpu.SemaphoreType.DMA((NZ + 1,)),
        ],
        compiler_params=pltpu.CompilerParams(
            collective_id=0, has_side_effects=True, vmem_limit_bytes=24 * 2**20
        ),
        cost_estimate=pl.CostEstimate(flops=0, bytes_accessed=200 * 10**6, transcendentals=0),
        name="gather_docs",
    )(sel, cache, pos)


def finish_kernel(
    ny,
    nh,
    slots,
    dev_tok,
    slot_ref,
    local_ref,
    inv_ref,
    count_ref,
    ctx_ref,
    pos_ref,
    gain_ref,
    q_ref,
    own_ref,
    att_ref,
    ret_ref,
    sum_ref,
    kv,
    dev,
    fresh,
    upd,
    squares,
    parts,
    relay,
    send,
    recv,
    fsend,
    frecv,
    hsend,
    hrecv,
    local_sem,
):
    entries = REQ_DEV * slots
    peers, doc_len, width = ctx_ref.shape
    head_dim = width // 2
    tokens = own_ref.shape[0] // REQ_DEV
    heads = q_ref.shape[1] // head_dim
    context = slots * doc_len
    span = kv.shape[1]
    group = slots // GROUPS
    scale = head_dim ** (-0.5)
    half = NZ // 2
    me = lax.axis_index("docs")
    y, z = me // NZ, lax.rem(me, NZ)
    head_at = lax.axis_index("heads")
    fellows = [lax.rem(head_at + k, nh) for k in range(nh)]
    barrier = pltpu.get_barrier_semaphore()

    def holder(s):
        return place(ny, y - s // NZ, z - lax.rem(s, NZ))

    def greet(s, carry):
        pl.semaphore_signal(barrier, inc=1, device_id={"docs": holder(s)}, device_id_type=pl.DeviceIdType.MESH)
        return carry

    lax.fori_loop(1, peers, greet, 0)
    for k in range(1, nh):
        pl.semaphore_signal(barrier, inc=1, device_id={"heads": fellows[k]}, device_id_type=pl.DeviceIdType.MESH)

    token = lax.broadcasted_iota(jnp.int32, (doc_len, 128), 0)
    lane_slot = lax.broadcasted_iota(jnp.int32, (1, group * dev_tok), 1) // dev_tok
    squares[...] = jnp.zeros_like(squares)
    fresh[entries] = jnp.zeros(fresh.shape[1:], fresh.dtype)
    for r in range(REQ_DEV):
        kv[r, context:] = jnp.zeros((span - context, width), kv.dtype)
        kv[r, context : context + tokens] = own_ref[r * tokens : (r + 1) * tokens]
        for k in range(slots):
            e = r * slots + k
            doc = ctx_ref[slot_ref[e]]
            kv[r, k * doc_len : (k + 1) * doc_len] = doc
            where = pos_ref[pl.ds(slot_ref[e] * 8 + local_ref[e], 1)]
            hot = (where == token).astype(jnp.bfloat16)
            rows_of = lax.dot_general(hot, doc, (((0,), (0,)), ((), ())), preferred_element_type=jnp.float32)
            dev[e * dev_tok : (e + 1) * dev_tok] = rows_of[:dev_tok]
    for r in range(REQ_DEV):
        for g in range(GROUPS):
            first = r * slots + g * group
            known = (g + 1) * group * doc_len
            mine = dev[first * dev_tok : (first + group) * dev_tok]
            scores = lax.dot_general(
                mine[:, :head_dim].astype(jnp.bfloat16),
                kv[r, :known, :head_dim],
                (((1,), (1,)), ((), ())),
                preferred_element_type=jnp.float32,
            )
            shape = (group * dev_tok, group * doc_len)
            row_slot = lax.broadcasted_iota(jnp.int32, shape, 0) // dev_tok
            key_slot = lax.broadcasted_iota(jnp.int32, shape, 1) // doc_len
            last = jnp.where(row_slot >= key_slot, scores[:, known - shape[1] :], very_low)
            scores = last if g == 0 else jnp.concatenate([scores[:, : known - shape[1]], last], axis=1)
            top = jnp.max(scores, axis=1, keepdims=True)
            weights = jnp.exp2((scores - top) * (scale * LOG2E))
            total = jnp.sum(weights, axis=1, keepdims=True)
            summed = jnp.dot(weights.astype(jnp.bfloat16), kv[r, :known], preferred_element_type=jnp.float32)
            delta = gain_ref[...] * (summed / total)
            renewed = mine + delta
            square = jnp.sum(delta * delta, axis=1, keepdims=True) * (1.0 / width)
            across_lanes = jnp.broadcast_to(square, (group * dev_tok, 128)).T[:1]
            squares[r * GROUPS + g : r * GROUPS + g + 1, : group * dev_tok] = jnp.where(
                lane_slot + g * group < count_ref[me * REQ_DEV + r], across_lanes, 0.0
            )
            for i in range(group):
                one = renewed[i * dev_tok : (i + 1) * dev_tok]
                fresh[first + i] = jnp.concatenate([one[:, :head_dim], one[:, head_dim:]], axis=0).astype(
                    jnp.bfloat16
                )

    pl.semaphore_wait(barrier, peers + nh - 2)

    def back(s):
        return pltpu.make_async_remote_copy(
            src_ref=upd.at[s],
            dst_ref=ret_ref.at[me],
            send_sem=send.at[s],
            recv_sem=recv.at[s],
            device_id={"docs": holder(s)},
            device_id_type=pl.DeviceIdType.MESH,
        )

    def aside(t):
        s = t * NZ + half
        turn = 1 - 2 * (t % 2)
        return pltpu.make_async_remote_copy(
            src_ref=upd.at[s],
            dst_ref=relay.at[t],
            send_sem=send.at[s],
            recv_sem=frecv.at[t],
            device_id={"docs": place(ny, y, z + turn)},
            device_id_type=pl.DeviceIdType.MESH,
        )

    def forward(t):
        turn = 1 - 2 * (t % 2)
        return pltpu.make_async_remote_copy(
            src_ref=relay.at[t],
            dst_ref=ret_ref.at[place(ny, y, z - turn)],
            send_sem=fsend.at[t],
            recv_sem=recv.at[t * NZ + half],
            device_id={"docs": place(ny, y - t, z - turn - half)},
            device_id_type=pl.DeviceIdType.MESH,
        )

    for t in range(ny):
        upd[t * NZ + half] = fresh[inv_ref[t * NZ + half]]
        aside(t).start()

    def far_first(i):
        k = i // ny
        j = jnp.where(k % 2 == 0, half - 1 - k // 2, half + 1 + k // 2)
        return lax.rem(i, ny) * NZ + j

    def launch(i, carry):
        s = far_first(i)
        upd[s] = fresh[inv_ref[s]]
        back(s).start()
        return carry

    lax.fori_loop(0, ny * (NZ - 2), launch, 0)
    for t in range(1, ny):
        upd[t * NZ] = fresh[inv_ref[t * NZ]]
        back(t * NZ).start()
    ret_ref[me] = fresh[inv_ref[0]]

    def share(k):
        return pltpu.make_async_remote_copy(
            src_ref=squares,
            dst_ref=parts.at[head_at],
            send_sem=hsend.at[k],
            recv_sem=hrecv.at[k],
            device_id={"heads": fellows[k]},
            device_id_type=pl.DeviceIdType.MESH,
        )

    for k in range(1, nh):
        share(k).start()
    parts[head_at] = squares[...]

    row = lax.broadcasted_iota(jnp.int32, (tokens, span - context), 0)
    col = lax.broadcasted_iota(jnp.int32, (tokens, span - context), 1)
    causal = row >= col
    place_of = lax.broadcasted_iota(jnp.int32, (1, context), 1)
    for r in range(REQ_DEV):
        live = place_of < count_ref[me * REQ_DEV + r] * doc_len

        def head(i, carry):
            cols = pl.ds(pl.multiple_of(i * head_dim, head_dim), head_dim)
            scores = lax.dot_general(
                q_ref[r * tokens : (r + 1) * tokens, cols],
                kv[r, :, :head_dim],
                (((1,), (1,)), ((), ())),
                preferred_element_type=jnp.float32,
            )
            docs = jnp.where(live, scores[:, :context], very_low)
            own = jnp.where(causal, scores[:, context:], very_low)
            top = jnp.maximum(jnp.max(docs, axis=1, keepdims=True), jnp.max(own, axis=1, keepdims=True))
            docs = jnp.exp2((docs - top) * (scale * LOG2E))
            own = jnp.exp2((own - top) * (scale * LOG2E))
            total = jnp.sum(docs, axis=1, keepdims=True) + jnp.sum(own, axis=1, keepdims=True)
            summed = jnp.dot(
                docs.astype(jnp.bfloat16), kv[r, :context, head_dim:], preferred_element_type=jnp.float32
            ) + jnp.dot(own.astype(jnp.bfloat16), kv[r, context:, head_dim:], preferred_element_type=jnp.float32)
            att_ref[r * tokens : (r + 1) * tokens, cols] = (summed / total).astype(jnp.bfloat16)
            return carry

        if r == 0:
            lax.fori_loop(0, 1, head, 0)
            for t in range(ny):
                aside(t).wait_recv()
                forward(t).start()
            lax.fori_loop(1, heads, head, 0)
        else:
            lax.fori_loop(0, heads, head, 0)

    for k in range(1, nh):
        share(k).wait()
    total = parts[0]
    for k in range(1, nh):
        total = total + parts[k]
    sum_ref[...] = total * (1.0 / KVH)

    def land(i, carry):
        back(far_first(i)).wait()
        return carry

    lax.fori_loop(0, ny * (NZ - 2), land, 0)
    for t in range(ny):
        if t:
            back(t * NZ).wait()
        aside(t).wait_send()
        forward(t).wait()


def finish(slots, dev_tok, slot_of, local, inv, counts, ctx, pos, gain, queries, own):
    peers, doc_len, width = ctx.shape
    ny = peers // NZ
    nh = lax.axis_size("heads")
    entries = REQ_DEV * slots
    tokens = own.shape[0] // REQ_DEV
    span = slots * doc_len + (tokens + 127) // 128 * 128
    packet = (2 * dev_tok, width // 2)
    square = jax.ShapeDtypeStruct((REQ_DEV * GROUPS, 128), jnp.float32)
    return pl.pallas_call(
        functools.partial(finish_kernel, ny, nh, slots, dev_tok),
        out_shape=(
            jax.ShapeDtypeStruct(queries.shape, jnp.bfloat16),
            jax.ShapeDtypeStruct((peers,) + packet, jnp.bfloat16),
            square,
        ),
        in_specs=[whole(SMEM)] * 4 + [whole(VMEM)] * 5,
        out_specs=(whole(VMEM), whole(VMEM), whole(VMEM)),
        scratch_shapes=[
            VMEM((REQ_DEV, span, width), ctx.dtype),
            VMEM((entries * dev_tok, width), jnp.float32),
            VMEM((entries + 1,) + packet, jnp.bfloat16),
            VMEM((peers,) + packet, jnp.bfloat16),
            VMEM(square.shape, square.dtype),
            VMEM((nh,) + square.shape, square.dtype),
            VMEM((ny,) + packet, jnp.bfloat16),
            pltpu.SemaphoreType.DMA((peers,)),
            pltpu.SemaphoreType.DMA((peers,)),
            pltpu.SemaphoreType.DMA((ny,)),
            pltpu.SemaphoreType.DMA((ny,)),
            pltpu.SemaphoreType.DMA((nh,)),
            pltpu.SemaphoreType.DMA((nh,)),
            pltpu.SemaphoreType.DMA((2,)),
        ],
        compiler_params=pltpu.CompilerParams(
            collective_id=1, has_side_effects=True, vmem_limit_bytes=44 * 2**20
        ),
        cost_estimate=pl.CostEstimate(
            flops=9 * 10**9, bytes_accessed=100 * 10**6, transcendentals=9 * 10**6
        ),
        name="finish",
    )(slot_of, local, inv, counts, ctx, pos, gain, queries, own)


def shards(queries, own_kv, cache, doc_lists, doc_counts, dev_pos, blend_gain):
    width = blend_gain.shape[1]
    head_dim = width // 2
    peers = lax.axis_size("docs")
    ny = peers // NZ
    me = lax.axis_index("docs")
    y, z = me // NZ, me % NZ
    slots = doc_lists.shape[1]
    entries = REQ_DEV * slots
    dev_tok = dev_pos.shape[1]
    doc_len = cache.shape[0] // DOC_DEV
    combined = doc_lists.reshape(peers, entries)

    row_lists = jnp.roll(combined.reshape(ny, NZ, entries)[:, z], -y, axis=0)
    row_owner = row_lists // DOC_DEV
    steps = jnp.arange(NZ, dtype=jnp.int32)
    passing = y * NZ + (z - steps) % NZ
    hits = row_owner[:, :, None] == passing[None, None, :]
    sel = jnp.sum(jnp.where(hits, (row_lists % DOC_DEV)[:, :, None], 0), axis=1).reshape(-1)

    mine = combined[me]
    owner = mine // DOC_DEV
    slot_of = ((y - owner // NZ) % ny) * NZ + (z - owner % NZ) % NZ
    entry = jnp.arange(entries, dtype=jnp.int32)
    live = (jnp.arange(slots, dtype=jnp.int32)[None, :] < doc_counts.reshape(peers, REQ_DEV)[me][:, None]).reshape(-1)
    filled = (slot_of[None, :] == jnp.arange(peers, dtype=jnp.int32)[:, None]) & live[None, :]
    inv = entries + jnp.sum(jnp.where(filled, entry[None, :] - entries, 0), axis=1)

    pos = jnp.pad(dev_pos, ((0, 8 - DOC_DEV), (0, 128 - dev_tok)), constant_values=-1)
    ctx, all_pos = gather_docs(sel.astype(jnp.int32), cache.reshape(DOC_DEV, doc_len, width), pos)
    att, ret, sums = finish(
        slots,
        dev_tok,
        slot_of,
        mine % DOC_DEV,
        inv,
        doc_counts,
        ctx,
        all_pos.reshape(peers * 8, 128),
        blend_gain,
        queries,
        own_kv,
    )
    group_rows = slots // GROUPS * dev_tok
    dev_score = sums.reshape(REQ_DEV, GROUPS, 128)[:, :, :group_rows].reshape(REQ_DEV, slots, dev_tok)
    returned = jnp.concatenate([ret[:, :dev_tok], ret[:, dev_tok:]], axis=2)
    return att, returned, dev_score


def solution(mesh):
    return jax.shard_map(
        shards,
        mesh=mesh,
        in_specs=(
            P("docs", "heads"),
            P("docs", "heads"),
            P("docs", "heads"),
            P(),
            P(),
            P("docs", None),
            P("heads", None),
        ),
        out_specs=(P("docs", "heads"), P("docs", None, "heads"), P("docs", None, None)),
        check_vma=False,
    )
```

```python
import functools

import jax
import jax.numpy as jnp
from jax import lax
from jax.experimental import pallas as pl
from jax.experimental.pallas import tpu as pltpu
from jax.sharding import PartitionSpec as P

KVH = 8
REQ_DEV = 2
DOC_DEV = 6
NZ = 16
very_low = -1e30
VMEM = pltpu.VMEM
SMEM = pltpu.SMEM
DMA = pltpu.SemaphoreType.DMA
MESH = pl.DeviceIdType.MESH
LOG2E = 1.4426950408889634
GROUPS = 4
CHUNKS = 3
KEY, VALUE = 0, 1


def whole(space):
    return pl.BlockSpec(memory_space=space)


def place(ny, y, z):
    return lax.rem(y + 2 * ny, ny) * NZ + lax.rem(z + 2 * NZ, NZ)


def blend_kernel(
    ny, nh, slots, dev_tok, names, table_ref, list_ref, count_ref, cache_ref, pos_ref, gain_ref, q_ref, own_ref,
    att_ref, retk_ref, retv_ref, sum_ref, *scratch
):
    has = dict(zip(names, scratch))
    peers = ny * NZ
    entries = REQ_DEV * slots
    doc_len, head_dim = has["base0"].shape[1:]
    tokens = own_ref.shape[0] // REQ_DEV
    heads = q_ref.shape[1] // head_dim
    context = slots * doc_len
    span = has["all0"].shape[1]
    group = slots // GROUPS
    scale = head_dim ** (-0.5)
    half = NZ // 2
    full = half - 1
    each = DOC_DEV // CHUNKS
    me = lax.axis_index("docs")
    y, z = me // NZ, lax.rem(me, NZ)
    head_at = lax.axis_index("heads")
    fellows = [lax.rem(head_at + k, nh) for k in range(nh)]
    ret = (retk_ref, retv_ref)
    local_sem = has["local_sem"]

    def two(name):
        return has[name + "0"], has[name + "1"]

    base, far, last_pick, picked, relay, ctx, every, fresh, upd, turn_buf = map(
        two, ("base", "far", "last", "picked", "relay", "ctx", "all", "fresh", "upd", "turn")
    )
    passing = [[[has["ring%d%d%d" % (p, way, s)] for s in range(full)] for way in range(2)] for p in range(2)]
    ring_pos, all_pos, dev, squares, parts = (has[n] for n in ("ring_pos", "all_pos", "dev", "squares", "parts"))
    weights_of = [has["weights%d" % g] for g in range(GROUPS)]
    totals, columns = has["totals"], has["columns"]

    fetch = [
        pltpu.make_async_copy(cache_ref.at[:, :, pl.ds(p * head_dim, head_dim)], base[p], local_sem.at[p])
        for p in range(2)
    ]
    fetch += [
        pltpu.make_async_copy(q_ref, has["q"], local_sem.at[2]),
        pltpu.make_async_copy(own_ref, has["own"], local_sem.at[3]),
    ]
    for one in fetch:
        one.start()
    barrier = pltpu.get_barrier_semaphore()

    def holder(s):
        return place(ny, y - s // NZ, z - lax.rem(s, NZ))

    def greet(s, carry):
        pl.semaphore_signal(barrier, inc=1, device_id={"docs": holder(s)}, device_id_type=MESH)
        return carry

    lax.fori_loop(1, peers, greet, 0)
    for k in range(1, nh):
        pl.semaphore_signal(barrier, inc=1, device_id={"heads": fellows[k]}, device_id_type=MESH)
    ring_pos[0] = jnp.full(ring_pos.shape[1:], -1, jnp.int32)
    ring_pos[0, :DOC_DEV, :dev_tok] = pos_ref[...]
    squares[...] = jnp.zeros_like(squares)
    for p in range(2):
        fresh[p][entries] = jnp.zeros(fresh[p].shape[1:], fresh[p].dtype)
        every[p][...] = jnp.zeros_like(every[p])
    fetch[KEY].wait()
    pl.semaphore_wait(barrier, peers + nh - 2)

    along_z = [place(ny, y, z + 1), place(ny, y, z - 1)]
    along_y = [place(ny, y + t, z) for t in range(ny)]

    def remote(src, dst, send_sem, recv_sem, device):
        return pltpu.make_async_remote_copy(
            src_ref=src, dst_ref=dst, send_sem=send_sem, recv_sem=recv_sem,
            device_id={"docs": device}, device_id_type=MESH,
        )

    def ring(p, way, step, chunk):
        src = base[p] if step == 1 else passing[p][way][step - 2]
        rows = pl.ds(chunk * each, each)
        sems = has["zsend"].at[p, way, step - 1, chunk], has["zrecv"].at[p, way, step - 1, chunk]
        return remote(src.at[rows], passing[p][way][step - 1].at[rows], *sems, along_z[way])

    def last_hop(p, t):
        sems = has["lsend"].at[p, t], has["lrecv"].at[p, t]
        return remote(last_pick[p].at[t], far[p].at[t], *sems, along_z[2 * t // ny])

    def ring_of_pos(way, step):
        src, dst = (step - 1, step) if way == 0 else ((NZ - step + 1) % NZ, NZ - step)
        sems = has["psend"].at[way, step], has["precv"].at[way, step]
        return remote(ring_pos.at[src], ring_pos.at[dst], *sems, along_z[way])

    def pos_across(t):
        sems = has["psend"].at[0, half + t], has["precv"].at[0, half + t]
        return remote(ring_pos, all_pos.at[t], *sems, along_y[t])

    def aside(j):
        return along_y[1] if j % 2 == 0 else along_y[ny - 1]

    def relayed(t, j):
        return 2 * t == ny and j != half

    def across(p, t, j):
        src = far[p].at[t] if j == half else picked[p].at[t, j]
        dst = relay[p].at[j] if relayed(t, j) else ctx[p].at[t * NZ + j]
        recv = has["frecv"].at[p, j] if relayed(t, j) else has["yrecv"].at[p, t, j]
        return remote(src, dst, has["ysend"].at[p, t, j], recv, aside(j) if relayed(t, j) else along_y[t])

    def forward(p, j):
        sems = has["fsend"].at[p, j], has["yrecv"].at[p, ny // 2, j]
        return remote(relay[p].at[j], ctx[p].at[ny // 2 * NZ + j], *sems, aside(j))

    waiting = []

    def pass_on():
        for p, j in waiting:
            across(p, ny // 2, j).wait_recv()
            forward(p, j).start()
        waiting.clear()

    def pick(p, buf, j):
        for t in [ny // 2] + [t for t in range(1, ny) if 2 * t != ny] + [0]:
            doc = buf[lax.rem(table_ref[t * NZ + j], 8)]
            if t:
                picked[p][t, j] = doc
                across(p, t, j).start()
            else:
                ctx[p][j] = doc
        waiting.append((p, j))

    def begin(p):
        for chunk in range(CHUNKS):
            for way in range(2):
                ring(p, way, 1, chunk).start()

    def travel(p, tasks):
        todo = list(tasks)
        for step in range(1, half):
            for chunk in range(CHUNKS):
                for way in range(2):
                    ring(p, way, step, chunk).wait_recv()
                    if step < full:
                        ring(p, way, step + 1, chunk).start()
                if p == KEY and chunk == 0:
                    for way in range(2):
                        ring_of_pos(way, step).wait_recv()
                        if way == 0 or step < full:
                            ring_of_pos(way, step + 1).start()
                if chunk < CHUNKS - 1 and todo:
                    todo.pop(0)()
            if step == full:
                for t in range(ny):
                    buf = passing[p][2 * t // ny][full - 1]
                    last_pick[p][t] = buf[lax.rem(table_ref[2 * peers + t], 8)]
                    last_hop(p, t).start()
                if p == KEY:
                    fetch[VALUE].wait()
                    begin(VALUE)
            pass_on()
            pick(p, passing[p][0][step - 1], step)
            pick(p, passing[p][1][step - 1], NZ - step)
            if todo:
                todo.pop(0)()
        for task in todo:
            task()

    def arrive(p):
        for t in range(ny):
            last_hop(p, t).wait_recv()
        pass_on()
        for t in range(1, ny):
            across(p, t, half).start()
        ctx[p][half] = far[p][0]
        if p == KEY:
            ring_of_pos(0, half).wait_recv()
            for t in range(1, ny):
                pos_across(t).start()
            all_pos[0] = ring_pos[...]

    def slot_of(e):
        named = list_ref[e % slots, me * REQ_DEV + e // slots]
        owner = named // DOC_DEV
        t = lax.rem(y - owner // NZ + ny, ny)
        j = lax.rem(z - lax.rem(owner, NZ) + NZ, NZ)
        return t * NZ + j, t, j, named - owner * DOC_DEV

    token = lax.broadcasted_iota(jnp.int32, (doc_len, 128), 0)

    def settle(p):
        for j in range(NZ):
            for t in range(1, ny):
                if relayed(t, j):
                    forward(p, j).wait_recv()
                else:
                    across(p, t, j).wait_recv()
        if p == KEY:
            for t in range(1, ny):
                pos_across(t).wait_recv()
            fetch[3].wait()

    def lay_out(p, r):
        every[p][r, context : context + tokens] = has["own"][
            r * tokens : (r + 1) * tokens, p * head_dim : (p + 1) * head_dim
        ]
        for k in range(slots):
            e = r * slots + k
            slot, t, j, local = slot_of(e)
            doc = ctx[p][slot]
            every[p][r, k * doc_len : (k + 1) * doc_len] = doc
            hot = (all_pos[t, j, pl.ds(local, 1)] == token).astype(jnp.bfloat16)
            rows_of = lax.dot_general(hot, doc, (((0,), (0,)), ((), ())), preferred_element_type=jnp.float32)
            dev[p, e * dev_tok : (e + 1) * dev_tok] = rows_of[:dev_tok]

    def renew(p, r, g, weights, total):
        first = r * slots + g * group
        rows = slice(first * dev_tok, (first + group) * dev_tok)
        known = (g + 1) * group * doc_len
        summed = jnp.dot(weights, every[p][r, :known], preferred_element_type=jnp.float32)
        delta = gain_ref[:, p * head_dim : (p + 1) * head_dim] * (summed / total)
        renewed = (dev[p, rows] + delta).astype(jnp.bfloat16)
        for i in range(group):
            fresh[p][first + i] = renewed[i * dev_tok : (i + 1) * dev_tok]
        return jnp.sum(delta * delta, axis=1, keepdims=True) * (0.5 / head_dim)

    def key_update(r, g):
        first = r * slots + g * group
        rows = slice(first * dev_tok, (first + group) * dev_tok)
        known = (g + 1) * group * doc_len
        scores = lax.dot_general(
            dev[KEY, rows].astype(jnp.bfloat16),
            every[KEY][r, :known],
            (((1,), (1,)), ((), ())),
            preferred_element_type=jnp.float32,
        )
        shape = (group * dev_tok, group * doc_len)
        row_slot = lax.broadcasted_iota(jnp.int32, shape, 0) // dev_tok
        key_slot = lax.broadcasted_iota(jnp.int32, shape, 1) // doc_len
        newest = jnp.where(row_slot >= key_slot, scores[:, known - shape[1] :], very_low)
        scores = newest if g == 0 else jnp.concatenate([scores[:, : known - shape[1]], newest], axis=1)
        top = jnp.max(scores, axis=1, keepdims=True)
        weights = jnp.exp2((scores - top) * (scale * LOG2E))
        total = jnp.sum(weights, axis=1, keepdims=True)
        weights = weights.astype(jnp.bfloat16)
        weights_of[g][r] = weights
        square = renew(KEY, r, g, weights, total)
        totals[rows] = jnp.broadcast_to(total, (group * dev_tok, 128))
        columns[rows] = jnp.broadcast_to(square, (group * dev_tok, 128))

    lane_slot = lax.broadcasted_iota(jnp.int32, (1, group * dev_tok), 1) // dev_tok

    def value_update(r, g):
        first = r * slots + g * group
        rows = slice(first * dev_tok, (first + group) * dev_tok)
        square = renew(VALUE, r, g, weights_of[g][r], totals[rows])
        both = (columns[rows] + square).T[:1]
        squares[r * GROUPS + g : r * GROUPS + g + 1, : group * dev_tok] = jnp.where(
            lane_slot + g * group < count_ref[me * REQ_DEV + r], both, 0.0
        )

    def back(p, s):
        return remote(upd[p].at[s], ret[p].at[me], has["send"].at[p, s], has["recv"].at[p, s], holder(s))

    def turn_aside(p, t):
        s = t * NZ + half
        way = 1 - 2 * (t % 2)
        sems = has["send"].at[p, s], has["trecv"].at[p, t]
        return remote(upd[p].at[s], turn_buf[p].at[t], *sems, place(ny, y, z + way))

    def turn_forward(p, t):
        way = 1 - 2 * (t % 2)
        sems = has["tsend"].at[p, t], has["recv"].at[p, t * NZ + half]
        target = place(ny, y - t, z - way - half)
        return remote(turn_buf[p].at[t], ret[p].at[place(ny, y, z - way)], *sems, target)

    def renewed_for(p, s):
        code = table_ref[peers + s]
        e = lax.rem(code // 8, 64)
        r = e // slots
        used = jnp.logical_and(code >= 512, e - r * slots < count_ref[me * REQ_DEV + r])
        return fresh[p][jnp.where(used, e, entries)]

    def far_first(i):
        k = i // ny
        j = jnp.where(lax.rem(k, 2) == 0, half - 1 - k // 2, half + 1 + k // 2)
        return lax.rem(i, ny) * NZ + j

    def give_back(p):
        for t in range(ny):
            upd[p][t * NZ + half] = renewed_for(p, t * NZ + half)
            turn_aside(p, t).start()

        def launch(i, carry):
            s = far_first(i)
            upd[p][s] = renewed_for(p, s)
            back(p, s).start()
            return carry

        lax.fori_loop(0, ny * (NZ - 2), launch, 0)
        for t in range(1, ny):
            upd[p][t * NZ] = renewed_for(p, t * NZ)
            back(p, t * NZ).start()
        ret[p][me] = renewed_for(p, 0)

    def turn(p):
        for t in range(ny):
            turn_aside(p, t).wait_recv()
            turn_forward(p, t).start()

    def share(k):
        return pltpu.make_async_remote_copy(
            src_ref=squares,
            dst_ref=parts.at[head_at],
            send_sem=has["hsend"].at[k],
            recv_sem=has["hrecv"].at[k],
            device_id={"heads": fellows[k]},
            device_id_type=MESH,
        )

    begin(KEY)
    for way in range(2):
        ring_of_pos(way, 1).start()
    pick(KEY, base[KEY], 0)
    travel(KEY, [])

    idle = lambda: None
    tasks = [lambda: arrive(KEY), lambda: pick(VALUE, base[VALUE], 0), idle]
    tasks += [lambda: settle(KEY)] + [functools.partial(lay_out, KEY, r) for r in range(REQ_DEV)]
    tasks += [functools.partial(key_update, r, g) for r in range(REQ_DEV) for g in range(GROUPS)]
    travel(VALUE, tasks)

    give_back(KEY)
    arrive(VALUE)
    settle(VALUE)
    turn(KEY)
    for r in range(REQ_DEV):
        lay_out(VALUE, r)
    for r in range(REQ_DEV):
        for g in range(GROUPS):
            value_update(r, g)
    give_back(VALUE)
    for k in range(1, nh):
        share(k).start()
    parts[head_at] = squares[...]

    fetch[2].wait()
    row = lax.broadcasted_iota(jnp.int32, (tokens, span - context), 0)
    col = lax.broadcasted_iota(jnp.int32, (tokens, span - context), 1)
    causal = row >= col
    place_of = lax.broadcasted_iota(jnp.int32, (1, context), 1)
    for r in range(REQ_DEV):
        live = place_of < count_ref[me * REQ_DEV + r] * doc_len

        def head(i, carry):
            cols = pl.ds(pl.multiple_of(i * head_dim, head_dim), head_dim)
            scores = lax.dot_general(
                has["q"][r * tokens : (r + 1) * tokens, cols],
                every[KEY][r],
                (((1,), (1,)), ((), ())),
                preferred_element_type=jnp.float32,
            )
            docs = jnp.where(live, scores[:, :context], very_low)
            own = jnp.where(causal, scores[:, context:], very_low)
            top = jnp.maximum(jnp.max(docs, axis=1, keepdims=True), jnp.max(own, axis=1, keepdims=True))
            docs = jnp.exp2((docs - top) * (scale * LOG2E))
            own = jnp.exp2((own - top) * (scale * LOG2E))
            total = jnp.sum(docs, axis=1, keepdims=True) + jnp.sum(own, axis=1, keepdims=True)
            summed = jnp.dot(
                docs.astype(jnp.bfloat16), every[VALUE][r, :context], preferred_element_type=jnp.float32
            ) + jnp.dot(own.astype(jnp.bfloat16), every[VALUE][r, context:], preferred_element_type=jnp.float32)
            att_ref[r * tokens : (r + 1) * tokens, cols] = (summed / total).astype(jnp.bfloat16)
            return carry

        if r == 0:
            lax.fori_loop(0, 1, head, 0)
            turn(VALUE)
            lax.fori_loop(1, heads, head, 0)
        else:
            lax.fori_loop(0, heads, head, 0)

    for k in range(1, nh):
        share(k).wait()
    total = parts[0]
    for k in range(1, nh):
        total = total + parts[k]
    sum_ref[...] = total * (1.0 / KVH)

    for p in range(2):
        for way in range(2):
            for step in range(1, half):
                for chunk in range(CHUNKS):
                    ring(p, way, step, chunk).wait_send()
        for t in range(ny):
            last_hop(p, t).wait_send()
        for j in range(NZ):
            for t in range(1, ny):
                across(p, t, j).wait_send()
            if j != half:
                forward(p, j).wait_send()
    for way in range(2):
        for step in range(1, half + 1 - way):
            ring_of_pos(way, step).wait_send()
    for t in range(1, ny):
        pos_across(t).wait_send()

    for p in range(2):

        def land(i, carry):
            back(p, far_first(i)).wait()
            return carry

        lax.fori_loop(0, ny * (NZ - 2), land, 0)
        for t in range(ny):
            if t:
                back(p, t * NZ).wait()
            turn_aside(p, t).wait_send()
            turn_forward(p, t).wait()


def blend(slots, table, lists, counts, cache, pos, gain, queries, own):
    peers = lax.axis_size("docs")
    ny = peers // NZ
    nh = lax.axis_size("heads")
    half = NZ // 2
    full = half - 1
    entries = REQ_DEV * slots
    dev_tok = pos.shape[1]
    doc_len, width = cache.shape[1:]
    head_dim = width // 2
    tokens = own.shape[0] // REQ_DEV
    span = slots * doc_len + (tokens + 127) // 128 * 128
    rows = slots // GROUPS * dev_tok
    doc = (doc_len, head_dim)
    packet = (dev_tok, head_dim)
    square = jax.ShapeDtypeStruct((REQ_DEV * GROUPS, 128), jnp.float32)
    bf16, f32 = jnp.bfloat16, jnp.float32
    scratch = {}
    for p in range(2):
        for name, shape in (
            ("base", (DOC_DEV,) + doc),
            ("far", (ny,) + doc),
            ("last", (ny,) + doc),
            ("picked", (ny, NZ) + doc),
            ("relay", (NZ,) + doc),
            ("ctx", (peers,) + doc),
            ("all", (REQ_DEV, span, head_dim)),
            ("fresh", (entries + 1,) + packet),
            ("upd", (peers,) + packet),
            ("turn", (ny,) + packet),
        ):
            scratch["%s%d" % (name, p)] = VMEM(shape, bf16)
        for way in range(2):
            for step in range(full):
                scratch["ring%d%d%d" % (p, way, step)] = VMEM((DOC_DEV,) + doc, bf16)
    for g in range(GROUPS):
        scratch["weights%d" % g] = VMEM((REQ_DEV, rows, (g + 1) * slots // GROUPS * doc_len), bf16)
    scratch["q"] = VMEM(queries.shape, bf16)
    scratch["own"] = VMEM(own.shape, bf16)
    scratch["dev"] = VMEM((2, entries * dev_tok, head_dim), f32)
    scratch["totals"] = VMEM((entries * dev_tok, 128), f32)
    scratch["columns"] = VMEM((entries * dev_tok, 128), f32)
    scratch["squares"] = VMEM(square.shape, f32)
    scratch["parts"] = VMEM((nh,) + square.shape, f32)
    scratch["ring_pos"] = VMEM((NZ, 8, 128), jnp.int32)
    scratch["all_pos"] = VMEM((ny, NZ, 8, 128), jnp.int32)
    for name, shape in (
        ("zsend", (2, 2, full, CHUNKS)), ("zrecv", (2, 2, full, CHUNKS)),
        ("lsend", (2, ny)), ("lrecv", (2, ny)),
        ("psend", (2, half + ny)), ("precv", (2, half + ny)),
        ("ysend", (2, ny, NZ)), ("yrecv", (2, ny, NZ)),
        ("fsend", (2, NZ)), ("frecv", (2, NZ)),
        ("send", (2, peers)), ("recv", (2, peers)),
        ("tsend", (2, ny)), ("trecv", (2, ny)),
        ("hsend", (nh,)), ("hrecv", (nh,)),
        ("local_sem", (4,)),
    ):
        scratch[name] = DMA(shape)
    any_space, vmem = whole(pl.ANY), whole(VMEM)
    return pl.pallas_call(
        functools.partial(blend_kernel, ny, nh, slots, dev_tok, tuple(scratch)),
        out_shape=(
            jax.ShapeDtypeStruct(queries.shape, bf16),
            jax.ShapeDtypeStruct((peers,) + packet, bf16),
            jax.ShapeDtypeStruct((peers,) + packet, bf16),
            square,
        ),
        in_specs=[whole(SMEM)] * 3 + [any_space, vmem, vmem, any_space, any_space],
        out_specs=(vmem,) * 4,
        scratch_shapes=list(scratch.values()),
        compiler_params=pltpu.CompilerParams(
            collective_id=0, has_side_effects=True, vmem_limit_bytes=56 * 2**20
        ),
        name="blend",
    )(table, lists, counts, cache, pos, gain, queries, own)


def shards(queries, own_kv, cache, doc_lists, doc_counts, dev_pos, blend_gain):
    width = blend_gain.shape[1]
    peers = lax.axis_size("docs")
    ny = peers // NZ
    me = lax.axis_index("docs")
    y, z = me // NZ, me % NZ
    slots = doc_lists.shape[1]
    dev_tok = dev_pos.shape[1]
    doc_len = cache.shape[0] // DOC_DEV

    lists = doc_lists.T
    owner = lists // DOC_DEV
    k = lax.broadcasted_iota(jnp.int32, lists.shape, 0)
    request = lax.broadcasted_iota(jnp.int32, lists.shape, 1)
    pair = request // REQ_DEV * peers + owner
    code = 512 + 8 * (request % REQ_DEV * slots + k) + lists - owner * DOC_DEV
    n = jnp.arange(2 * peers + 128, dtype=jnp.int32)
    t, j = n // NZ % ny, n % NZ
    picks = ((y + t) % ny * NZ + z) * peers + y * NZ + (z - j) % NZ
    returns = me * peers + (y - t) % ny * NZ + (z - j) % NZ
    way = jnp.where(j < ny // 2, 1, -1)
    last = ((y + j) % ny * NZ + (z + way) % NZ) * peers + y * NZ + (z - way * (NZ // 2 - 1)) % NZ
    want = jnp.where(n < peers, picks, jnp.where(n < 2 * peers, returns, last))
    table = jnp.sum(jnp.where(pair[None] == want[:, None, None], code[None], 0), axis=(1, 2))

    att, retk, retv, sums = blend(
        slots, table, lists, doc_counts, cache.reshape(DOC_DEV, doc_len, width), dev_pos, blend_gain, queries, own_kv
    )
    group_rows = slots // GROUPS * dev_tok
    dev_score = sums.reshape(REQ_DEV, GROUPS, 128)[:, :, :group_rows].reshape(REQ_DEV, slots, dev_tok)
    return att, jnp.concatenate([retk, retv], axis=2), dev_score


def solution(mesh):
    return jax.shard_map(
        shards,
        mesh=mesh,
        in_specs=(
            P("docs", "heads"),
            P("docs", "heads"),
            P("docs", "heads"),
            P(),
            P(),
            P("docs", None),
            P("heads", None),
        ),
        out_specs=(P("docs", "heads"), P("docs", None, "heads"), P("docs", None, None)),
        check_vma=False,
    )
```

```python
import functools

import jax
import jax.numpy as jnp
from jax import lax
from jax.experimental import pallas as pl
from jax.experimental.pallas import tpu as pltpu
from jax.sharding import PartitionSpec as P

KVH = 8
REQ_DEV = 2
DOC_DEV = 6
NZ = 16
very_low = -1e30
VMEM = pltpu.VMEM
SMEM = pltpu.SMEM
DMA = pltpu.SemaphoreType.DMA
MESH = pl.DeviceIdType.MESH
LOG2E = 1.4426950408889634
GROUPS = 4
LEAD = 3
CHUNKS = 2
KEY, VALUE = 0, 1


def whole(space):
    return pl.BlockSpec(memory_space=space)


def place(ny, y, z):
    return lax.rem(y + 2 * ny, ny) * NZ + lax.rem(z + 2 * NZ, NZ)


def blend_kernel(
    ny, nh, slots, dev_tok, names, table_ref, list_ref, count_ref, cache_ref, pos_ref, gain_ref, q_ref, own_ref,
    att_ref, ret_ref, sum_ref, *scratch
):
    has = dict(zip(names, scratch))
    peers = ny * NZ
    entries = REQ_DEV * slots
    doc_len, head_dim = has["base0"].shape[1:]
    tokens = own_ref.shape[0] // REQ_DEV
    heads = q_ref.shape[1] // head_dim
    context = slots * doc_len
    span = has["all0"].shape[1]
    group = slots // GROUPS
    scale = head_dim ** (-0.5)
    half = NZ // 2
    full = half - 1
    each = DOC_DEV // CHUNKS
    me = lax.axis_index("docs")
    y, z = me // NZ, lax.rem(me, NZ)
    head_at = lax.axis_index("heads")
    fellows = [lax.rem(head_at + k, nh) for k in range(nh)]
    local_sem = has["local_sem"]

    def two(name):
        return has[name + "0"], has[name + "1"]

    base, far, last_pick, picked, ctx, every, fresh, upd, turn_buf = map(
        two, ("base", "far", "last", "picked", "ctx", "all", "fresh", "upd", "turn")
    )
    passing = [[[has["ring%d%d%d" % (p, way, s)] for s in range(full)] for way in range(2)] for p in range(2)]
    ring_pos, all_pos, dev, squares, parts = (has[n] for n in ("ring_pos", "all_pos", "dev", "squares", "parts"))
    weights_of = [has["weights%d" % g] for g in range(GROUPS)]
    totals, columns = has["totals"], has["columns"]

    fetch = [
        pltpu.make_async_copy(cache_ref.at[:, :, pl.ds(p * head_dim, head_dim)], base[p], local_sem.at[p])
        for p in range(2)
    ]
    fetch += [
        pltpu.make_async_copy(q_ref, has["q"], local_sem.at[2]),
        pltpu.make_async_copy(own_ref, has["own"], local_sem.at[3]),
    ]
    for one in fetch:
        one.start()
    barrier = pltpu.get_barrier_semaphore()

    def holder(s):
        return place(ny, y - s // NZ, z - lax.rem(s, NZ))

    def greet(s, carry):
        pl.semaphore_signal(barrier, inc=1, device_id={"docs": holder(s)}, device_id_type=MESH)
        return carry

    lax.fori_loop(1, peers, greet, 0)
    for k in range(1, nh):
        pl.semaphore_signal(barrier, inc=1, device_id={"heads": fellows[k]}, device_id_type=MESH)
    ring_pos[0] = jnp.full(ring_pos.shape[1:], -1, jnp.int32)
    ring_pos[0, :DOC_DEV, :dev_tok] = pos_ref[...]
    squares[...] = jnp.zeros_like(squares)
    for p in range(2):
        fresh[p][entries] = jnp.zeros(fresh[p].shape[1:], fresh[p].dtype)
        every[p][:, context:, :head_dim] = jnp.zeros((REQ_DEV, span - context, head_dim), jnp.bfloat16)
    every[VALUE][:, :, head_dim:] = jnp.ones((REQ_DEV, span, head_dim), jnp.bfloat16)
    fetch[KEY].wait()
    pl.semaphore_wait(barrier, peers + nh - 2)

    along_z = [place(ny, y, z + 1), place(ny, y, z - 1)]
    along_y = [place(ny, y + t, z) for t in range(ny)]

    def remote(src, dst, send_sem, recv_sem, device):
        return pltpu.make_async_remote_copy(
            src_ref=src, dst_ref=dst, send_sem=send_sem, recv_sem=recv_sem,
            device_id={"docs": device}, device_id_type=MESH,
        )

    def ring(p, way, step, chunk):
        src = base[p] if step == 1 else passing[p][way][step - 2]
        rows = pl.ds(chunk * each, each)
        sems = has["zsend"].at[p, way, step - 1, chunk], has["zrecv"].at[p, way, step - 1, chunk]
        return remote(src.at[rows], passing[p][way][step - 1].at[rows], *sems, along_z[way])

    def last_hop(p, t):
        sems = has["lsend"].at[p, t], has["lrecv"].at[p, t]
        return remote(last_pick[p].at[t], far[p].at[t], *sems, along_z[2 * t // ny])

    def ring_of_pos(way, step):
        src, dst = (step - 1, step) if way == 0 else ((NZ - step + 1) % NZ, NZ - step)
        sems = has["psend"].at[way, step], has["precv"].at[way, step]
        return remote(ring_pos.at[src], ring_pos.at[dst], *sems, along_z[way])

    def pos_across(t):
        sems = has["psend"].at[0, half + t], has["precv"].at[0, half + t]
        return remote(ring_pos, all_pos.at[t], *sems, along_y[t])

    def across(p, t, j):
        src = far[p].at[t] if j == half else picked[p].at[t, j]
        sems = has["ysend"].at[p, t, j], has["yrecv"].at[p, t, j]
        return remote(src, ctx[p].at[t * NZ + j], *sems, along_y[t])

    def pick(p, buf, j):
        for t in [ny // 2] + [t for t in range(1, ny) if 2 * t != ny] + [0]:
            doc = buf[lax.rem(table_ref[t * NZ + j], 8)]
            if t:
                picked[p][t, j] = doc
                across(p, t, j).start()
            else:
                ctx[p][j] = doc

    def begin(p):
        for chunk in range(CHUNKS):
            for way in range(2):
                ring(p, way, 1, chunk).start()

    def hop(p, step, todo):
        for chunk in range(CHUNKS):
            for way in range(2):
                ring(p, way, step, chunk).wait_recv()
                if step < full:
                    ring(p, way, step + 1, chunk).start()
            if p == KEY and chunk == 0:
                for way in range(2):
                    ring_of_pos(way, step).wait_recv()
                    if way == 0 or step < full:
                        ring_of_pos(way, step + 1).start()
            if chunk < CHUNKS - 1 and todo:
                todo.pop(0)()
        if step == full:
            for t in range(ny):
                buf = passing[p][2 * t // ny][full - 1]
                last_pick[p][t] = buf[lax.rem(table_ref[2 * peers + t], 8)]
                last_hop(p, t).start()
        pick(p, passing[p][0][step - 1], step)
        pick(p, passing[p][1][step - 1], NZ - step)
        if todo:
            todo.pop(0)()

    def arrive(p):
        for t in range(ny):
            last_hop(p, t).wait_recv()
        for t in range(1, ny):
            across(p, t, half).start()
        ctx[p][half] = far[p][0]
        if p == KEY:
            ring_of_pos(0, half).wait_recv()
            for t in range(1, ny):
                pos_across(t).start()
            all_pos[0] = ring_pos[...]

    def slot_of(e):
        named = list_ref[e % slots, me * REQ_DEV + e // slots]
        owner = named // DOC_DEV
        t = lax.rem(y - owner // NZ + ny, ny)
        j = lax.rem(z - lax.rem(owner, NZ) + NZ, NZ)
        return t * NZ + j, t, j, named - owner * DOC_DEV

    token = lax.broadcasted_iota(jnp.int32, (doc_len, 128), 0)

    def settle(p):
        for j in range(NZ):
            for t in range(1, ny):
                across(p, t, j).wait_recv()
        if p == KEY:
            for t in range(1, ny):
                pos_across(t).wait_recv()
            fetch[3].wait()

    def lay_out(p, r):
        every[p][r, context : context + tokens, :head_dim] = has["own"][
            r * tokens : (r + 1) * tokens, p * head_dim : (p + 1) * head_dim
        ]
        for k in range(slots):
            e = r * slots + k
            slot, t, j, local = slot_of(e)
            doc = ctx[p][slot]
            every[p][r, k * doc_len : (k + 1) * doc_len, :head_dim] = doc
            hot = (all_pos[t, j, pl.ds(local, 1)] == token).astype(jnp.bfloat16)
            rows_of = lax.dot_general(hot, doc, (((0,), (0,)), ((), ())), preferred_element_type=jnp.float32)
            dev[p, e * dev_tok : (e + 1) * dev_tok] = rows_of[:dev_tok]

    def renew(p, r, g, weights, total):
        first = r * slots + g * group
        rows = slice(first * dev_tok, (first + group) * dev_tok)
        known = (g + 1) * group * doc_len
        summed = jnp.dot(weights, every[p][r, :known, :head_dim], preferred_element_type=jnp.float32)
        delta = gain_ref[:, p * head_dim : (p + 1) * head_dim] * (summed / total)
        renewed = (dev[p, rows] + delta).astype(jnp.bfloat16)
        for i in range(group):
            fresh[p][first + i] = renewed[i * dev_tok : (i + 1) * dev_tok]
        return jnp.sum(delta * delta, axis=1, keepdims=True) * (0.5 / head_dim)

    def key_update(r, g):
        first = r * slots + g * group
        rows = slice(first * dev_tok, (first + group) * dev_tok)
        known = (g + 1) * group * doc_len
        scores = lax.dot_general(
            dev[KEY, rows].astype(jnp.bfloat16),
            every[KEY][r, :known],
            (((1,), (1,)), ((), ())),
            preferred_element_type=jnp.float32,
        )
        shape = (group * dev_tok, group * doc_len)
        row_slot = lax.broadcasted_iota(jnp.int32, shape, 0) // dev_tok
        key_slot = lax.broadcasted_iota(jnp.int32, shape, 1) // doc_len
        newest = jnp.where(row_slot >= key_slot, scores[:, known - shape[1] :], very_low)
        scores = newest if g == 0 else jnp.concatenate([scores[:, : known - shape[1]], newest], axis=1)
        top = jnp.max(scores, axis=1, keepdims=True)
        weights = jnp.exp2((scores - top) * (scale * LOG2E))
        total = jnp.sum(weights, axis=1, keepdims=True)
        weights = weights.astype(jnp.bfloat16)
        weights_of[g][r] = weights
        square = renew(KEY, r, g, weights, total)
        totals[rows] = jnp.broadcast_to(total, (group * dev_tok, 128))
        columns[rows] = jnp.broadcast_to(square, (group * dev_tok, 128))

    lane_slot = lax.broadcasted_iota(jnp.int32, (1, group * dev_tok), 1) // dev_tok

    def value_update(r, g):
        first = r * slots + g * group
        rows = slice(first * dev_tok, (first + group) * dev_tok)
        square = renew(VALUE, r, g, weights_of[g][r], totals[rows])
        both = (columns[rows] + square).T[:1]
        squares[r * GROUPS + g : r * GROUPS + g + 1, : group * dev_tok] = jnp.where(
            lane_slot + g * group < count_ref[me * REQ_DEV + r], both, 0.0
        )

    def ret_part(p, home):
        return ret_ref.at[home, :, pl.ds(p * head_dim, head_dim)]

    def back(p, s):
        return remote(upd[p].at[s], ret_part(p, me), has["send"].at[p, s], has["recv"].at[p, s], holder(s))

    def turn_aside(p, t):
        s = t * NZ + half
        way = 1 - 2 * (t % 2)
        sems = has["send"].at[p, s], has["trecv"].at[p, t]
        return remote(upd[p].at[s], turn_buf[p].at[t], *sems, place(ny, y, z + way))

    def turn_forward(p, t):
        way = 1 - 2 * (t % 2)
        sems = has["tsend"].at[p, t], has["recv"].at[p, t * NZ + half]
        target = place(ny, y - t, z - way - half)
        return remote(turn_buf[p].at[t], ret_part(p, place(ny, y, z - way)), *sems, target)

    def renewed_for(p, s):
        code = table_ref[peers + s]
        e = lax.rem(code // 8, 64)
        r = e // slots
        used = jnp.logical_and(code >= 512, e - r * slots < count_ref[me * REQ_DEV + r])
        return fresh[p][jnp.where(used, e, entries)]

    def far_first(i):
        k = i // ny
        j = jnp.where(lax.rem(k, 2) == 0, half - 1 - k // 2, half + 1 + k // 2)
        return lax.rem(i, ny) * NZ + j

    def give_back(p):
        for t in range(ny):
            upd[p][t * NZ + half] = renewed_for(p, t * NZ + half)
            turn_aside(p, t).start()

        def launch(i, carry):
            s = far_first(i)
            upd[p][s] = renewed_for(p, s)
            back(p, s).start()
            return carry

        lax.fori_loop(0, ny * (NZ - 2), launch, 0)
        for t in range(1, ny):
            upd[p][t * NZ] = renewed_for(p, t * NZ)
            back(p, t * NZ).start()
        ret_ref[me, :, p * head_dim : (p + 1) * head_dim] = renewed_for(p, 0)

    def turn(p):
        for t in range(ny):
            turn_aside(p, t).wait_recv()
            turn_forward(p, t).start()

    def share(k):
        return pltpu.make_async_remote_copy(
            src_ref=squares,
            dst_ref=parts.at[head_at],
            send_sem=has["hsend"].at[k],
            recv_sem=has["hrecv"].at[k],
            device_id={"heads": fellows[k]},
            device_id_type=MESH,
        )

    begin(KEY)
    for way in range(2):
        ring_of_pos(way, 1).start()
    pick(KEY, base[KEY], 0)
    tasks = [lambda: arrive(KEY), lambda: settle(KEY)]
    tasks += [functools.partial(lay_out, KEY, r) for r in range(REQ_DEV)]
    tasks += [functools.partial(key_update, r, g) for r in range(REQ_DEV) for g in range(GROUPS)]
    lead = min(LEAD, full)
    for tick in range(1, full + lead + 1):
        if tick <= full:
            hop(KEY, tick, [])
        if tick == lead:
            fetch[VALUE].wait()
            begin(VALUE)
            pick(VALUE, base[VALUE], 0)
        if tick > lead:
            todo = []
            if tick > full:
                share_of = -(-len(tasks) // (full + lead + 1 - tick))
                turns, tasks = tasks[:share_of], tasks[share_of:]
                middle = len(turns) // 2
                todo = [
                    functools.partial(lambda some: [one() for one in some], turns[:middle]),
                    functools.partial(lambda some: [one() for one in some], turns[middle:]),
                ]
            hop(VALUE, tick - lead, todo)

    give_back(KEY)
    arrive(VALUE)
    settle(VALUE)
    turn(KEY)
    for r in range(REQ_DEV):
        lay_out(VALUE, r)
    for r in range(REQ_DEV):
        for g in range(GROUPS):
            value_update(r, g)
    give_back(VALUE)
    for k in range(1, nh):
        share(k).start()
    parts[head_at] = squares[...]

    fetch[2].wait()
    row = lax.broadcasted_iota(jnp.int32, (tokens, span - context), 0)
    col = lax.broadcasted_iota(jnp.int32, (tokens, span - context), 1)
    causal = row >= col
    place_of = lax.broadcasted_iota(jnp.int32, (1, context), 1)

    def spot(n):
        n = jnp.clip(n, 0, REQ_DEV * heads - 1)
        r = n // heads
        rows = pl.ds(pl.multiple_of(r * tokens, 16), tokens)
        return r, rows, pl.ds(pl.multiple_of(lax.rem(n, heads) * head_dim, head_dim), head_dim)

    def scores_of(n, out):
        r, rows, cols = spot(n)
        out[...] = lax.dot_general(
            has["q"][rows, cols], every[KEY][r], (((1,), (1,)), ((), ())), preferred_element_type=jnp.float32
        )

    def weights_from(n, scores, out):
        r, _, _ = spot(n)
        docs = jnp.where(place_of < count_ref[me * REQ_DEV + r] * doc_len, scores[:, :context], very_low)
        own = jnp.where(causal, scores[:, context:], very_low)
        top = jnp.maximum(jnp.max(docs, axis=1, keepdims=True), jnp.max(own, axis=1, keepdims=True))
        out[:, :context] = jnp.exp2((docs - top) * (scale * LOG2E)).astype(jnp.bfloat16)
        out[:, context:] = jnp.exp2((own - top) * (scale * LOG2E)).astype(jnp.bfloat16)

    def output_of(n, weights):
        r, rows, cols = spot(n)
        summed = jnp.dot(weights[...], every[VALUE][r], preferred_element_type=jnp.float32)
        att_ref[rows, cols] = (summed[:, :head_dim] / summed[:, head_dim:]).astype(jnp.bfloat16)

    score_a, score_b, weight_a, weight_b = (has[n] for n in ("score0", "score1", "weight0", "weight1"))

    def pair(m, carry):
        scores_of(2 * m + 1, score_b)
        weights_from(2 * m, score_a, weight_a)
        output_of(2 * m - 1, weight_b)
        scores_of(2 * m + 2, score_a)
        weights_from(2 * m + 1, score_b, weight_b)
        output_of(2 * m, weight_a)
        return carry

    weight_b[...] = jnp.ones_like(weight_b)
    scores_of(0, score_a)
    lax.fori_loop(0, 1, pair, 0)
    turn(VALUE)
    lax.fori_loop(1, REQ_DEV * heads // 2, pair, 0)
    output_of(REQ_DEV * heads - 1, weight_b)

    for k in range(1, nh):
        share(k).wait()
    total = parts[0]
    for k in range(1, nh):
        total = total + parts[k]
    sum_ref[...] = total * (1.0 / KVH)

    for p in range(2):
        for way in range(2):
            for step in range(1, half):
                for chunk in range(CHUNKS):
                    ring(p, way, step, chunk).wait_send()
        for t in range(ny):
            last_hop(p, t).wait_send()
        for j in range(NZ):
            for t in range(1, ny):
                across(p, t, j).wait_send()
    for way in range(2):
        for step in range(1, half + 1 - way):
            ring_of_pos(way, step).wait_send()
    for t in range(1, ny):
        pos_across(t).wait_send()

    for p in range(2):

        def land(i, carry):
            back(p, far_first(i)).wait()
            return carry

        lax.fori_loop(0, ny * (NZ - 2), land, 0)
        for t in range(ny):
            if t:
                back(p, t * NZ).wait()
            turn_aside(p, t).wait_send()
            turn_forward(p, t).wait()


def blend(slots, table, lists, counts, cache, pos, gain, queries, own):
    peers = lax.axis_size("docs")
    ny = peers // NZ
    nh = lax.axis_size("heads")
    half = NZ // 2
    full = half - 1
    entries = REQ_DEV * slots
    dev_tok = pos.shape[1]
    doc_len, width = cache.shape[1:]
    head_dim = width // 2
    tokens = own.shape[0] // REQ_DEV
    span = slots * doc_len + (tokens + 127) // 128 * 128
    rows = slots // GROUPS * dev_tok
    doc = (doc_len, head_dim)
    packet = (dev_tok, head_dim)
    square = jax.ShapeDtypeStruct((REQ_DEV * GROUPS, 128), jnp.float32)
    bf16, f32 = jnp.bfloat16, jnp.float32
    scratch = {}
    for p in range(2):
        for name, shape in (
            ("base", (DOC_DEV,) + doc),
            ("far", (ny,) + doc),
            ("last", (ny,) + doc),
            ("picked", (ny, NZ) + doc),
            ("ctx", (peers,) + doc),
            ("all", (REQ_DEV, span, head_dim * (1 + p))),
            ("fresh", (entries + 1,) + packet),
            ("upd", (peers,) + packet),
            ("turn", (ny,) + packet),
        ):
            scratch["%s%d" % (name, p)] = VMEM(shape, bf16)
        for way in range(2):
            for step in range(full):
                scratch["ring%d%d%d" % (p, way, step)] = VMEM((DOC_DEV,) + doc, bf16)
    for g in range(GROUPS):
        scratch["weights%d" % g] = VMEM((REQ_DEV, rows, (g + 1) * slots // GROUPS * doc_len), bf16)
    for name in ("0", "1"):
        scratch["score" + name] = VMEM((tokens, span), f32)
        scratch["weight" + name] = VMEM((tokens, span), bf16)
    scratch["q"] = VMEM(queries.shape, bf16)
    scratch["own"] = VMEM(own.shape, bf16)
    scratch["dev"] = VMEM((2, entries * dev_tok, head_dim), f32)
    scratch["totals"] = VMEM((entries * dev_tok, 128), f32)
    scratch["columns"] = VMEM((entries * dev_tok, 128), f32)
    scratch["squares"] = VMEM(square.shape, f32)
    scratch["parts"] = VMEM((nh,) + square.shape, f32)
    scratch["ring_pos"] = VMEM((NZ, 8, 128), jnp.int32)
    scratch["all_pos"] = VMEM((ny, NZ, 8, 128), jnp.int32)
    for name, shape in (
        ("zsend", (2, 2, full, CHUNKS)), ("zrecv", (2, 2, full, CHUNKS)),
        ("lsend", (2, ny)), ("lrecv", (2, ny)),
        ("psend", (2, half + ny)), ("precv", (2, half + ny)),
        ("ysend", (2, ny, NZ)), ("yrecv", (2, ny, NZ)),
        ("send", (2, peers)), ("recv", (2, peers)),
        ("tsend", (2, ny)), ("trecv", (2, ny)),
        ("hsend", (nh,)), ("hrecv", (nh,)),
        ("local_sem", (4,)),
    ):
        scratch[name] = DMA(shape)
    any_space, vmem = whole(pl.ANY), whole(VMEM)
    return pl.pallas_call(
        functools.partial(blend_kernel, ny, nh, slots, dev_tok, tuple(scratch)),
        out_shape=(
            jax.ShapeDtypeStruct(queries.shape, bf16),
            jax.ShapeDtypeStruct((peers, dev_tok, width), bf16),
            square,
        ),
        in_specs=[whole(SMEM)] * 3 + [any_space, vmem, vmem, any_space, any_space],
        out_specs=(vmem,) * 3,
        scratch_shapes=list(scratch.values()),
        compiler_params=pltpu.CompilerParams(
            collective_id=0, has_side_effects=True, vmem_limit_bytes=56 * 2**20
        ),
        name="blend",
    )(table, lists, counts, cache, pos, gain, queries, own)


def shards(queries, own_kv, cache, doc_lists, doc_counts, dev_pos, blend_gain):
    width = blend_gain.shape[1]
    peers = lax.axis_size("docs")
    ny = peers // NZ
    me = lax.axis_index("docs")
    y, z = me // NZ, me % NZ
    slots = doc_lists.shape[1]
    dev_tok = dev_pos.shape[1]
    doc_len = cache.shape[0] // DOC_DEV

    lists = doc_lists.T
    owner = lists // DOC_DEV
    k = lax.broadcasted_iota(jnp.int32, lists.shape, 0)
    request = lax.broadcasted_iota(jnp.int32, lists.shape, 1)
    pair = request // REQ_DEV * peers + owner
    code = 512 + 8 * (request % REQ_DEV * slots + k) + lists - owner * DOC_DEV
    n = jnp.arange(2 * peers + 128, dtype=jnp.int32)
    t, j = n // NZ % ny, n % NZ
    picks = ((y + t) % ny * NZ + z) * peers + y * NZ + (z - j) % NZ
    returns = me * peers + (y - t) % ny * NZ + (z - j) % NZ
    way = jnp.where(j < ny // 2, 1, -1)
    last = ((y + j) % ny * NZ + (z + way) % NZ) * peers + y * NZ + (z - way * (NZ // 2 - 1)) % NZ
    want = jnp.where(n < peers, picks, jnp.where(n < 2 * peers, returns, last))
    table = jnp.sum(jnp.where(pair[None] == want[:, None, None], code[None], 0), axis=(1, 2))

    att, returned, sums = blend(
        slots, table, lists, doc_counts, cache.reshape(DOC_DEV, doc_len, width), dev_pos, blend_gain, queries, own_kv
    )
    group_rows = slots // GROUPS * dev_tok
    dev_score = sums.reshape(REQ_DEV, GROUPS, 128)[:, :, :group_rows].reshape(REQ_DEV, slots, dev_tok)
    return att, returned, dev_score


def solution(mesh):
    return jax.shard_map(
        shards,
        mesh=mesh,
        in_specs=(
            P("docs", "heads"),
            P("docs", "heads"),
            P("docs", "heads"),
            P(),
            P(),
            P("docs", None),
            P("heads", None),
        ),
        out_specs=(P("docs", "heads"), P("docs", None, "heads"), P("docs", None, None)),
        check_vma=False,
    )
```

```python
import functools

import jax
import jax.numpy as jnp
from jax import lax
from jax.experimental import pallas as pl
from jax.experimental.pallas import tpu as pltpu
from jax.sharding import PartitionSpec as P

KVH = 8
REQ_DEV = 2
DOC_DEV = 6
NZ = 16
very_low = -1e30
VMEM = pltpu.VMEM
SMEM = pltpu.SMEM
DMA = pltpu.SemaphoreType.DMA
MESH = pl.DeviceIdType.MESH
LOG2E = 1.4426950408889634
GROUPS = 4
LEAD = 4
CHUNKS = 2
EARLY = 4
KEY, VALUE = 0, 1


def whole(space):
    return pl.BlockSpec(memory_space=space)


def place(ny, y, z):
    return lax.rem(y + 2 * ny, ny) * NZ + lax.rem(z + 2 * NZ, NZ)


def blend_kernel(
    ny, nh, slots, dev_tok, names, table_ref, list_ref, count_ref, cache_ref, pos_ref, gain_ref, q_ref, own_ref,
    att_ref, ret_ref, sum_ref, *scratch
):
    has = dict(zip(names, scratch))
    peers = ny * NZ
    entries = REQ_DEV * slots
    doc_len, head_dim = has["base0"].shape[1:]
    tokens = own_ref.shape[0] // REQ_DEV
    heads = q_ref.shape[1] // head_dim
    context = slots * doc_len
    span = has["all0"].shape[1]
    group = slots // GROUPS
    scale = head_dim ** (-0.5)
    half = NZ // 2
    full = half - 1
    each = DOC_DEV // CHUNKS
    me = lax.axis_index("docs")
    y, z = me // NZ, lax.rem(me, NZ)
    head_at = lax.axis_index("heads")
    fellows = [lax.rem(head_at + k, nh) for k in range(nh)]
    local_sem = has["local_sem"]

    def two(name):
        return has[name + "0"], has[name + "1"]

    base, far, last_pick, picked, ctx, every, fresh, upd, turn_buf, mid = map(
        two, ("base", "far", "last", "picked", "ctx", "all", "fresh", "upd", "turn", "mid")
    )
    passing = [[[has["ring%d%d%d" % (p, way, s)] for s in range(full)] for way in range(2)] for p in range(2)]
    ring_pos, all_pos, dev, squares, parts = (has[n] for n in ("ring_pos", "all_pos", "dev", "squares", "parts"))
    weights_of = [has["weights%d" % g] for g in range(GROUPS)]
    totals, columns = has["totals"], has["columns"]

    fetch = [
        pltpu.make_async_copy(cache_ref.at[:, :, pl.ds(p * head_dim, head_dim)], base[p], local_sem.at[p])
        for p in range(2)
    ]
    fetch += [
        pltpu.make_async_copy(q_ref, has["q"], local_sem.at[2]),
        pltpu.make_async_copy(own_ref, has["own"], local_sem.at[3]),
    ]
    for one in fetch:
        one.start()
    barrier = pltpu.get_barrier_semaphore()

    def greet(j, carry):
        pl.semaphore_signal(barrier, inc=1, device_id={"docs": place(ny, y, z - j)}, device_id_type=MESH)
        return carry

    lax.fori_loop(1, NZ, greet, 0)
    for t in range(1, ny):
        pl.semaphore_signal(barrier, inc=1, device_id={"docs": place(ny, y + t, z)}, device_id_type=MESH)
    for k in range(1, nh):
        pl.semaphore_signal(barrier, inc=1, device_id={"heads": fellows[k]}, device_id_type=MESH)
    ring_pos[0] = jnp.full(ring_pos.shape[1:], -1, jnp.int32)
    ring_pos[0, :DOC_DEV, :dev_tok] = pos_ref[...]
    squares[...] = jnp.zeros_like(squares)
    for p in range(2):
        fresh[p][entries] = jnp.zeros(fresh[p].shape[1:], fresh[p].dtype)
        every[p][:, context:, :head_dim] = jnp.zeros((REQ_DEV, span - context, head_dim), jnp.bfloat16)
    every[VALUE][:, :, head_dim:] = jnp.ones((REQ_DEV, span, head_dim), jnp.bfloat16)
    fetch[KEY].wait()
    pl.semaphore_wait(barrier, NZ - 1 + ny - 1 + nh - 1)

    along_z = [place(ny, y, z + 1), place(ny, y, z - 1)]
    along_y = [place(ny, y + t, z) for t in range(ny)]

    def remote(src, dst, send_sem, recv_sem, device):
        return pltpu.make_async_remote_copy(
            src_ref=src, dst_ref=dst, send_sem=send_sem, recv_sem=recv_sem,
            device_id={"docs": device}, device_id_type=MESH,
        )

    def ring(p, way, step, chunk):
        src = base[p] if step == 1 else passing[p][way][step - 2]
        rows = pl.ds(chunk * each, each)
        sems = has["zsend"].at[p, way, step - 1, chunk], has["zrecv"].at[p, way, step - 1, chunk]
        return remote(src.at[rows], passing[p][way][step - 1].at[rows], *sems, along_z[way])

    def last_hop(p, t):
        sems = has["lsend"].at[p, t], has["lrecv"].at[p, t]
        return remote(last_pick[p].at[t], far[p].at[t], *sems, along_z[2 * t // ny])

    def ring_of_pos(way, step):
        src, dst = (step - 1, step) if way == 0 else ((NZ - step + 1) % NZ, NZ - step)
        sems = has["psend"].at[way, step], has["precv"].at[way, step]
        return remote(ring_pos.at[src], ring_pos.at[dst], *sems, along_z[way])

    def pos_across(t):
        sems = has["psend"].at[0, half + t], has["precv"].at[0, half + t]
        return remote(ring_pos, all_pos.at[t], *sems, along_y[t])

    def across(p, t, step):
        at = pl.ds(1 if step == half else 2 * step, 1 if step in (0, half) else 2)
        src = far[p].at[pl.ds(t, 1)] if step == half else picked[p].at[t, at]
        sems = has["ysend"].at[p, t, step], has["yrecv"].at[p, t, step]
        return remote(src, ctx[p].at[t, at], *sems, along_y[t])

    def pick(p, step):
        for t in list(range(1, ny)) + [0]:
            for way in range(1 if step == 0 else 2):
                buf = base[p] if step == 0 else passing[p][way][step - 1]
                j = step if way == 0 else NZ - step
                doc = buf[lax.rem(table_ref[t * NZ + j], 8)]
                if t:
                    picked[p][t, 2 * step + way] = doc
                else:
                    ctx[p][0, 2 * step + way] = doc
            if t:
                across(p, t, step).start()

    def begin(p):
        for chunk in range(CHUNKS):
            for way in range(2):
                ring(p, way, 1, chunk).start()

    def hop(p, step, todo):
        for chunk in range(CHUNKS):
            for way in range(2):
                ring(p, way, step, chunk).wait_recv()
                if step < full:
                    ring(p, way, step + 1, chunk).start()
            if p == KEY and chunk == 0:
                for way in range(2):
                    ring_of_pos(way, step).wait_recv()
                    if way == 0 or step < full:
                        ring_of_pos(way, step + 1).start()
            if chunk < CHUNKS - 1 and todo:
                todo.pop(0)()
        if step == full:
            for t in range(ny):
                buf = passing[p][2 * t // ny][full - 1]
                last_pick[p][t] = buf[lax.rem(table_ref[2 * peers + t], 8)]
                last_hop(p, t).start()
        pick(p, step)
        if todo:
            todo.pop(0)()

    def arrive(p):
        for t in range(ny):
            last_hop(p, t).wait_recv()
        for t in range(1, ny):
            across(p, t, half).start()
        ctx[p][0, 1] = far[p][0]
        if p == KEY:
            ring_of_pos(0, half).wait_recv()
            for t in range(1, ny):
                pos_across(t).start()
            all_pos[0] = ring_pos[...]

    def slot_of(e):
        named = list_ref[e % slots, me * REQ_DEV + e // slots]
        owner = named // DOC_DEV
        t = lax.rem(y - owner // NZ + ny, ny)
        j = lax.rem(z - lax.rem(owner, NZ) + NZ, NZ)
        at = jnp.where(j < half, 2 * j, 2 * (NZ - j) + 1)
        return t, jnp.where(j == half, 1, at), j, named - owner * DOC_DEV

    token = lax.broadcasted_iota(jnp.int32, (doc_len, 128), 0)

    def settle(p):
        for step in range(half + 1):
            for t in range(1, ny):
                across(p, t, step).wait_recv()
        if p == KEY:
            for t in range(1, ny):
                pos_across(t).wait_recv()
            fetch[3].wait()

    def lay_out(p, r):
        every[p][r, context : context + tokens, :head_dim] = has["own"][
            r * tokens : (r + 1) * tokens, p * head_dim : (p + 1) * head_dim
        ]
        for k in range(slots):
            e = r * slots + k
            t, at, j, local = slot_of(e)
            doc = ctx[p][t, at]
            every[p][r, k * doc_len : (k + 1) * doc_len, :head_dim] = doc
            hot = (all_pos[t, j, pl.ds(local, 1)] == token).astype(jnp.bfloat16)
            rows_of = lax.dot_general(hot, doc, (((0,), (0,)), ((), ())), preferred_element_type=jnp.float32)
            dev[p, e * dev_tok : (e + 1) * dev_tok] = rows_of[:dev_tok]

    def renew(p, r, g, weights, total):
        first = r * slots + g * group
        rows = slice(first * dev_tok, (first + group) * dev_tok)
        known = (g + 1) * group * doc_len
        summed = jnp.dot(weights, every[p][r, :known, :head_dim], preferred_element_type=jnp.float32)
        delta = gain_ref[:, p * head_dim : (p + 1) * head_dim] * (summed / total)
        renewed = (dev[p, rows] + delta).astype(jnp.bfloat16)
        for i in range(group):
            fresh[p][first + i] = renewed[i * dev_tok : (i + 1) * dev_tok]
        return jnp.sum(delta * delta, axis=1, keepdims=True) * (0.5 / head_dim)

    def key_update(r, g):
        first = r * slots + g * group
        rows = slice(first * dev_tok, (first + group) * dev_tok)
        known = (g + 1) * group * doc_len
        scores = lax.dot_general(
            dev[KEY, rows].astype(jnp.bfloat16),
            every[KEY][r, :known],
            (((1,), (1,)), ((), ())),
            preferred_element_type=jnp.float32,
        )
        shape = (group * dev_tok, group * doc_len)
        row_slot = lax.broadcasted_iota(jnp.int32, shape, 0) // dev_tok
        key_slot = lax.broadcasted_iota(jnp.int32, shape, 1) // doc_len
        newest = jnp.where(row_slot >= key_slot, scores[:, known - shape[1] :], very_low)
        scores = newest if g == 0 else jnp.concatenate([scores[:, : known - shape[1]], newest], axis=1)
        top = jnp.max(scores, axis=1, keepdims=True)
        weights = jnp.exp2((scores - top) * (scale * LOG2E))
        total = jnp.sum(weights, axis=1, keepdims=True)
        weights = weights.astype(jnp.bfloat16)
        weights_of[g][r] = weights
        square = renew(KEY, r, g, weights, total)
        totals[rows] = jnp.broadcast_to(total, (group * dev_tok, 128))
        columns[rows] = jnp.broadcast_to(square, (group * dev_tok, 128))

    lane_slot = lax.broadcasted_iota(jnp.int32, (1, group * dev_tok), 1) // dev_tok

    def value_update(r, g):
        first = r * slots + g * group
        rows = slice(first * dev_tok, (first + group) * dev_tok)
        square = renew(VALUE, r, g, weights_of[g][r], totals[rows])
        both = (columns[rows] + square).T[:1]
        squares[r * GROUPS + g : r * GROUPS + g + 1, : group * dev_tok] = jnp.where(
            lane_slot + g * group < count_ref[me * REQ_DEV + r], both, 0.0
        )

    side = ny // 2

    def back(p, j):
        return remote(
            upd[p].at[j], mid[p].at[:, z], has["send"].at[p, j], has["recv"].at[p, j], place(ny, y, z - j)
        )

    def turn_aside(p, w):
        src = upd[p].at[half, pl.ds(w * side, side)]
        sems = has["send"].at[p, NZ + w], has["trecv"].at[p, w]
        return remote(src, turn_buf[p].at[w], *sems, along_z[w])

    def turn_forward(p, w):
        origin = lax.rem(z + NZ - 1 + 2 * w, NZ)
        dst = mid[p].at[pl.ds(w * side, side), origin]
        sems = has["tsend"].at[p, w], has["recv"].at[p, NZ + w]
        return remote(turn_buf[p].at[w], dst, *sems, place(ny, y, origin - half))

    def spread(p, u):
        dst = ret_ref.at[pl.ds(y * NZ, NZ), :, pl.ds(p * head_dim, head_dim)]
        return remote(mid[p].at[u], dst, has["gsend"].at[p, u], has["grecv"].at[p, u], along_y[u])

    def renewed_for(p, u, j):
        code = table_ref[peers + (ny - u) % ny * NZ + j]
        e = lax.rem(code // 8, 64)
        r = e // slots
        used = jnp.logical_and(code >= 512, e - r * slots < count_ref[me * REQ_DEV + r])
        return fresh[p][jnp.where(used, e, entries)]

    def far_first(i):
        return jnp.where(lax.rem(i, 2) == 0, half - 1 - i // 2, half + 1 + i // 2)

    def give_back(p):
        for u in range(ny):
            upd[p][half, u] = renewed_for(p, u, half)
        for w in range(2):
            turn_aside(p, w).start()

        def launch(i, carry):
            j = far_first(i)
            for u in range(ny):
                upd[p][j, u] = renewed_for(p, u, j)
            back(p, j).start()
            return carry

        lax.fori_loop(0, NZ - 2, launch, 0)
        for u in range(ny):
            mid[p][u, z] = renewed_for(p, u, 0)

    def turn(p):
        for w in range(2):
            turn_aside(p, w).wait_recv()
            turn_forward(p, w).start()

    def spread_all(p):
        def land(i, carry):
            back(p, far_first(i)).wait_recv()
            return carry

        lax.fori_loop(0, NZ - 2, land, 0)
        for w in range(2):
            turn_forward(p, w).wait_recv()
        for u in range(1, ny):
            spread(p, u).start()
        ret_ref[pl.ds(y * NZ, NZ), :, p * head_dim : (p + 1) * head_dim] = mid[p][0]

    def share(k):
        return pltpu.make_async_remote_copy(
            src_ref=squares,
            dst_ref=parts.at[head_at],
            send_sem=has["hsend"].at[k],
            recv_sem=has["hrecv"].at[k],
            device_id={"heads": fellows[k]},
            device_id_type=MESH,
        )

    row = lax.broadcasted_iota(jnp.int32, (tokens, span - context), 0)
    col = lax.broadcasted_iota(jnp.int32, (tokens, span - context), 1)
    causal = row >= col
    place_of = lax.broadcasted_iota(jnp.int32, (1, context), 1)

    def spot(n):
        n = jnp.clip(n, 0, REQ_DEV * heads - 1)
        r = n // heads
        rows = pl.ds(pl.multiple_of(r * tokens, 16), tokens)
        return r, rows, pl.ds(pl.multiple_of(lax.rem(n, heads) * head_dim, head_dim), head_dim)

    def scores_of(n, out):
        r, rows, cols = spot(n)
        out[...] = lax.dot_general(
            has["q"][rows, cols], every[KEY][r], (((1,), (1,)), ((), ())), preferred_element_type=jnp.float32
        )

    def weights_from(n, scores, out):
        r, _, _ = spot(n)
        docs = jnp.where(place_of < count_ref[me * REQ_DEV + r] * doc_len, scores[:, :context], very_low)
        own = jnp.where(causal, scores[:, context:], very_low)
        top = jnp.maximum(jnp.max(docs, axis=1, keepdims=True), jnp.max(own, axis=1, keepdims=True))
        out[:, :context] = jnp.exp2((docs - top) * (scale * LOG2E)).astype(jnp.bfloat16)
        out[:, context:] = jnp.exp2((own - top) * (scale * LOG2E)).astype(jnp.bfloat16)

    def output_of(n, weights):
        r, rows, cols = spot(n)
        summed = jnp.dot(weights[...], every[VALUE][r], preferred_element_type=jnp.float32)
        att_ref[rows, cols] = (summed[:, :head_dim] / summed[:, head_dim:]).astype(jnp.bfloat16)

    score_a, score_b, weight_a, weight_b = (has[n] for n in ("score0", "score1", "weight0", "weight1"))
    early = [has["early%d" % n] for n in range(EARLY)]

    def early_head(n):
        if n == 0:
            fetch[2].wait()
        scores_of(n, score_a)
        weights_from(n, score_a, early[n])

    def pair(m, carry):
        scores_of(2 * m + 1, score_b)
        weights_from(2 * m, score_a, weight_a)
        output_of(2 * m - 1, weight_b)
        scores_of(2 * m + 2, score_a)
        weights_from(2 * m + 1, score_b, weight_b)
        output_of(2 * m, weight_a)
        return carry

    begin(KEY)
    for way in range(2):
        ring_of_pos(way, 1).start()
    pick(KEY, 0)
    tasks = [lambda: arrive(KEY), lambda: settle(KEY)]
    tasks += [functools.partial(lay_out, KEY, r) for r in range(REQ_DEV)]
    tasks += [functools.partial(key_update, r, g) for r in range(REQ_DEV) for g in range(GROUPS)]
    tasks += [functools.partial(early_head, n) for n in range(EARLY)]
    lead = min(LEAD, full)
    for tick in range(1, full + lead + 1):
        if tick <= full:
            hop(KEY, tick, [])
        if tick == lead:
            fetch[VALUE].wait()
            begin(VALUE)
            pick(VALUE, 0)
        if tick > lead:
            todo = []
            if tick > full:
                share_of = -(-len(tasks) // (full + lead + 1 - tick))
                turns, tasks = tasks[:share_of], tasks[share_of:]
                middle = len(turns) // 2
                todo = [
                    functools.partial(lambda some: [one() for one in some], turns[:middle]),
                    functools.partial(lambda some: [one() for one in some], turns[middle:]),
                ]
            hop(VALUE, tick - lead, todo)

    if nh > 1:
        other = has["other"]
        twin = head_at + 1 - 2 * lax.rem(head_at, 2)
        pl.semaphore_signal(other, inc=1, device_id={"heads": twin}, device_id_type=MESH)
        pl.semaphore_wait(other, 1)
    give_back(KEY)
    arrive(VALUE)
    settle(VALUE)
    turn(KEY)
    for r in range(REQ_DEV):
        lay_out(VALUE, r)
    for r in range(REQ_DEV):
        for g in range(GROUPS):
            value_update(r, g)
    give_back(VALUE)
    for k in range(1, nh):
        share(k).start()
    parts[head_at] = squares[...]

    weight_b[...] = jnp.ones_like(weight_b)
    scores_of(EARLY, score_a)
    for n in range(EARLY):
        output_of(n, early[n])
    turn(VALUE)
    pairs = REQ_DEV * heads // 2
    lax.fori_loop(EARLY // 2, EARLY // 2 + 1, pair, 0)
    output_of(EARLY - 1, early[EARLY - 1])
    lax.fori_loop(EARLY // 2 + 1, pairs - 2, pair, 0)
    spread_all(KEY)
    lax.fori_loop(pairs - 2, pairs, pair, 0)
    output_of(REQ_DEV * heads - 1, weight_b)
    spread_all(VALUE)

    for k in range(1, nh):
        share(k).wait()
    total = parts[0]
    for k in range(1, nh):
        total = total + parts[k]
    sum_ref[...] = total * (1.0 / KVH)

    for p in range(2):
        for way in range(2):
            for step in range(1, half):
                for chunk in range(CHUNKS):
                    ring(p, way, step, chunk).wait_send()
        for t in range(ny):
            last_hop(p, t).wait_send()
        for step in range(half + 1):
            for t in range(1, ny):
                across(p, t, step).wait_send()
    for way in range(2):
        for step in range(1, half + 1 - way):
            ring_of_pos(way, step).wait_send()
    for t in range(1, ny):
        pos_across(t).wait_send()

    for p in range(2):

        def leave(i, carry):
            back(p, far_first(i)).wait_send()
            return carry

        lax.fori_loop(0, NZ - 2, leave, 0)
        for w in range(2):
            turn_aside(p, w).wait_send()
            turn_forward(p, w).wait_send()
        for u in range(1, ny):
            spread(p, u).wait()


def blend(slots, table, lists, counts, cache, pos, gain, queries, own):
    peers = lax.axis_size("docs")
    ny = peers // NZ
    nh = lax.axis_size("heads")
    half = NZ // 2
    full = half - 1
    entries = REQ_DEV * slots
    dev_tok = pos.shape[1]
    doc_len, width = cache.shape[1:]
    head_dim = width // 2
    tokens = own.shape[0] // REQ_DEV
    span = slots * doc_len + (tokens + 127) // 128 * 128
    rows = slots // GROUPS * dev_tok
    doc = (doc_len, head_dim)
    packet = (dev_tok, head_dim)
    square = jax.ShapeDtypeStruct((REQ_DEV * GROUPS, 128), jnp.float32)
    bf16, f32 = jnp.bfloat16, jnp.float32
    scratch = {}
    for p in range(2):
        for name, shape in (
            ("base", (DOC_DEV,) + doc),
            ("far", (ny,) + doc),
            ("last", (ny,) + doc),
            ("picked", (ny, NZ) + doc),
            ("ctx", (ny, NZ) + doc),
            ("all", (REQ_DEV, span, head_dim * (1 + p))),
            ("fresh", (entries + 1,) + packet),
            ("upd", (NZ, ny) + packet),
            ("turn", (2, ny // 2) + packet),
            ("mid", (ny, NZ) + packet),
        ):
            scratch["%s%d" % (name, p)] = VMEM(shape, bf16)
        for way in range(2):
            for step in range(full):
                scratch["ring%d%d%d" % (p, way, step)] = VMEM((DOC_DEV,) + doc, bf16)
    for g in range(GROUPS):
        scratch["weights%d" % g] = VMEM((REQ_DEV, rows, (g + 1) * slots // GROUPS * doc_len), bf16)
    for name in ("0", "1"):
        scratch["score" + name] = VMEM((tokens, span), f32)
        scratch["weight" + name] = VMEM((tokens, span), bf16)
    for n in range(EARLY):
        scratch["early%d" % n] = VMEM((tokens, span), bf16)
    scratch["q"] = VMEM(queries.shape, bf16)
    scratch["own"] = VMEM(own.shape, bf16)
    scratch["dev"] = VMEM((2, entries * dev_tok, head_dim), f32)
    scratch["totals"] = VMEM((entries * dev_tok, 128), f32)
    scratch["columns"] = VMEM((entries * dev_tok, 128), f32)
    scratch["squares"] = VMEM(square.shape, f32)
    scratch["parts"] = VMEM((nh,) + square.shape, f32)
    scratch["ring_pos"] = VMEM((NZ, 8, 128), jnp.int32)
    scratch["all_pos"] = VMEM((ny, NZ, 8, 128), jnp.int32)
    for name, shape in (
        ("zsend", (2, 2, full, CHUNKS)), ("zrecv", (2, 2, full, CHUNKS)),
        ("lsend", (2, ny)), ("lrecv", (2, ny)),
        ("psend", (2, half + ny)), ("precv", (2, half + ny)),
        ("ysend", (2, ny, half + 1)), ("yrecv", (2, ny, half + 1)),
        ("send", (2, NZ + 2)), ("recv", (2, NZ + 2)),
        ("tsend", (2, 2)), ("trecv", (2, 2)), ("gsend", (2, ny)), ("grecv", (2, ny)),
        ("hsend", (nh,)), ("hrecv", (nh,)),
        ("local_sem", (4,)),
    ):
        scratch[name] = DMA(shape)
    scratch["other"] = pltpu.SemaphoreType.REGULAR
    any_space, vmem = whole(pl.ANY), whole(VMEM)
    return pl.pallas_call(
        functools.partial(blend_kernel, ny, nh, slots, dev_tok, tuple(scratch)),
        out_shape=(
            jax.ShapeDtypeStruct(queries.shape, bf16),
            jax.ShapeDtypeStruct((peers, dev_tok, width), bf16),
            square,
        ),
        in_specs=[whole(SMEM)] * 3 + [any_space, vmem, vmem, any_space, any_space],
        out_specs=(vmem,) * 3,
        scratch_shapes=list(scratch.values()),
        compiler_params=pltpu.CompilerParams(
            collective_id=0, has_side_effects=True, vmem_limit_bytes=56 * 2**20
        ),
        name="blend",
    )(table, lists, counts, cache, pos, gain, queries, own)


def shards(queries, own_kv, cache, doc_lists, doc_counts, dev_pos, blend_gain):
    width = blend_gain.shape[1]
    peers = lax.axis_size("docs")
    ny = peers // NZ
    me = lax.axis_index("docs")
    y, z = me // NZ, me % NZ
    slots = doc_lists.shape[1]
    dev_tok = dev_pos.shape[1]
    doc_len = cache.shape[0] // DOC_DEV

    lists = doc_lists.T
    owner = lists // DOC_DEV
    k = lax.broadcasted_iota(jnp.int32, lists.shape, 0)
    request = lax.broadcasted_iota(jnp.int32, lists.shape, 1)
    pair = request // REQ_DEV * peers + owner
    code = 512 + 8 * (request % REQ_DEV * slots + k) + lists - owner * DOC_DEV
    n = jnp.arange(2 * peers + 128, dtype=jnp.int32)
    t, j = n // NZ % ny, n % NZ
    picks = ((y + t) % ny * NZ + z) * peers + y * NZ + (z - j) % NZ
    returns = me * peers + (y - t) % ny * NZ + (z - j) % NZ
    way = jnp.where(j < ny // 2, 1, -1)
    last = ((y + j) % ny * NZ + (z + way) % NZ) * peers + y * NZ + (z - way * (NZ // 2 - 1)) % NZ
    want = jnp.where(n < peers, picks, jnp.where(n < 2 * peers, returns, last))
    table = jnp.sum(jnp.where(pair[None] == want[:, None, None], code[None], 0), axis=(1, 2))

    att, returned, sums = blend(
        slots, table, lists, doc_counts, cache.reshape(DOC_DEV, doc_len, width), dev_pos, blend_gain, queries, own_kv
    )
    group_rows = slots // GROUPS * dev_tok
    dev_score = sums.reshape(REQ_DEV, GROUPS, 128)[:, :, :group_rows].reshape(REQ_DEV, slots, dev_tok)
    return att, returned, dev_score


def solution(mesh):
    return jax.shard_map(
        shards,
        mesh=mesh,
        in_specs=(
            P("docs", "heads"),
            P("docs", "heads"),
            P("docs", "heads"),
            P(),
            P(),
            P("docs", None),
            P("heads", None),
        ),
        out_specs=(P("docs", "heads"), P("docs", None, "heads"), P("docs", None, None)),
        check_vma=False,
    )
```

```python
import functools

import jax
import jax.numpy as jnp
from jax import lax
from jax.experimental import pallas as pl
from jax.experimental.pallas import tpu as pltpu
from jax.sharding import PartitionSpec as P

KVH = 8
REQ_DEV = 2
DOC_DEV = 6
NZ = 16
very_low = -1e30
VMEM = pltpu.VMEM
SMEM = pltpu.SMEM
DMA = pltpu.SemaphoreType.DMA
MESH = pl.DeviceIdType.MESH
LOG2E = 1.4426950408889634
GROUPS = 4
LEAD = 6
CHUNKS = 2
EARLY = 2
KEY, VALUE = 0, 1


def whole(space):
    return pl.BlockSpec(memory_space=space)


def place(ny, y, z):
    return lax.rem(y + 2 * ny, ny) * NZ + lax.rem(z + 2 * NZ, NZ)


def blend_kernel(
    ny, nh, slots, dev_tok, names, table_ref, list_ref, count_ref, cache_ref, pos_ref, gain_ref, q_ref, own_ref,
    att_ref, ret_ref, sum_ref, *scratch
):
    has = dict(zip(names, scratch))
    peers = ny * NZ
    entries = REQ_DEV * slots
    doc_len, head_dim = has["base0"].shape[1:]
    tokens = own_ref.shape[0] // REQ_DEV
    heads = q_ref.shape[1] // head_dim
    context = slots * doc_len
    span = has["all0"].shape[1]
    group = slots // GROUPS
    scale = head_dim ** (-0.5)
    half = NZ // 2
    full = half - 1
    each = DOC_DEV // CHUNKS
    me = lax.axis_index("docs")
    y, z = me // NZ, lax.rem(me, NZ)
    head_at = lax.axis_index("heads")
    fellows = [lax.rem(head_at + k, nh) for k in range(nh)]
    local_sem = has["local_sem"]

    def two(name):
        return has[name + "0"], has[name + "1"]

    base, far, last_pick, picked, ctx, every, fresh, upd, turn_buf, mid = map(
        two, ("base", "far", "last", "picked", "ctx", "all", "fresh", "upd", "turn", "mid")
    )
    passing = [[[has["ring%d%d%d" % (p, way, s)] for s in range(full)] for way in range(2)] for p in range(2)]
    ring_pos, all_pos, dev, squares, parts = (has[n] for n in ("ring_pos", "all_pos", "dev", "squares", "parts"))
    weights_of = [has["weights%d" % g] for g in range(GROUPS)]
    totals, columns = has["totals"], has["columns"]

    fetch = [
        pltpu.make_async_copy(cache_ref.at[:, :, pl.ds(p * head_dim, head_dim)], base[p], local_sem.at[p])
        for p in range(2)
    ]
    fetch += [
        pltpu.make_async_copy(q_ref, has["q"], local_sem.at[2]),
        pltpu.make_async_copy(own_ref, has["own"], local_sem.at[3]),
    ]
    for one in fetch:
        one.start()
    barrier = pltpu.get_barrier_semaphore()

    def greet(j, carry):
        pl.semaphore_signal(barrier, inc=1, device_id={"docs": place(ny, y, z - j)}, device_id_type=MESH)
        return carry

    lax.fori_loop(1, NZ, greet, 0)
    for t in range(1, ny):
        pl.semaphore_signal(barrier, inc=1, device_id={"docs": place(ny, y + t, z)}, device_id_type=MESH)
    for k in range(1, nh):
        pl.semaphore_signal(barrier, inc=1, device_id={"heads": fellows[k]}, device_id_type=MESH)
    ring_pos[0] = jnp.full(ring_pos.shape[1:], -1, jnp.int32)
    ring_pos[0, :DOC_DEV, :dev_tok] = pos_ref[...]
    squares[...] = jnp.zeros_like(squares)
    for p in range(2):
        fresh[p][entries] = jnp.zeros(fresh[p].shape[1:], fresh[p].dtype)
        every[p][:, context:, :head_dim] = jnp.zeros((REQ_DEV, span - context, head_dim), jnp.bfloat16)
    every[VALUE][:, :, head_dim:] = jnp.ones((REQ_DEV, span, head_dim), jnp.bfloat16)
    fetch[KEY].wait()
    pl.semaphore_wait(barrier, NZ - 1 + ny - 1 + nh - 1)

    along_z = [place(ny, y, z + 1), place(ny, y, z - 1)]
    along_y = [place(ny, y + t, z) for t in range(ny)]

    def remote(src, dst, send_sem, recv_sem, device):
        return pltpu.make_async_remote_copy(
            src_ref=src, dst_ref=dst, send_sem=send_sem, recv_sem=recv_sem,
            device_id={"docs": device}, device_id_type=MESH,
        )

    def ring(p, way, step, chunk):
        src = base[p] if step == 1 else passing[p][way][step - 2]
        rows = pl.ds(chunk * each, each)
        sems = has["zsend"].at[p, way, step - 1, chunk], has["zrecv"].at[p, way, step - 1, chunk]
        return remote(src.at[rows], passing[p][way][step - 1].at[rows], *sems, along_z[way])

    def last_hop(p, t):
        sems = has["lsend"].at[p, t], has["lrecv"].at[p, t]
        return remote(last_pick[p].at[t], far[p].at[t], *sems, along_z[2 * t // ny])

    def ring_of_pos(way, step):
        src, dst = (step - 1, step) if way == 0 else ((NZ - step + 1) % NZ, NZ - step)
        sems = has["psend"].at[way, step], has["precv"].at[way, step]
        return remote(ring_pos.at[src], ring_pos.at[dst], *sems, along_z[way])

    def pos_across(t):
        sems = has["psend"].at[0, half + t], has["precv"].at[0, half + t]
        return remote(ring_pos, all_pos.at[t], *sems, along_y[t])

    def across(p, t, step):
        at = pl.ds(1 if step == half else 2 * step, 1 if step in (0, half) else 2)
        src = far[p].at[pl.ds(t, 1)] if step == half else picked[p].at[t, at]
        sems = has["ysend"].at[p, t, step], has["yrecv"].at[p, t, step]
        return remote(src, ctx[p].at[t, at], *sems, along_y[t])

    def pick(p, step):
        for t in list(range(1, ny)) + [0]:
            for way in range(1 if step == 0 else 2):
                buf = base[p] if step == 0 else passing[p][way][step - 1]
                j = step if way == 0 else NZ - step
                doc = buf[lax.rem(table_ref[t * NZ + j], 8)]
                if t:
                    picked[p][t, 2 * step + way] = doc
                else:
                    ctx[p][0, 2 * step + way] = doc
            if t:
                across(p, t, step).start()

    def begin(p):
        for chunk in range(CHUNKS):
            for way in range(2):
                ring(p, way, 1, chunk).start()

    def hop(p, step, todo):
        for chunk in range(CHUNKS):
            for way in range(2):
                ring(p, way, step, chunk).wait_recv()
                if step < full:
                    ring(p, way, step + 1, chunk).start()
            if p == KEY and chunk == 0:
                for way in range(2):
                    ring_of_pos(way, step).wait_recv()
                    if way == 0 or step < full:
                        ring_of_pos(way, step + 1).start()
            if chunk < CHUNKS - 1 and todo:
                todo.pop(0)()
        if step == full:
            for t in range(ny):
                buf = passing[p][2 * t // ny][full - 1]
                last_pick[p][t] = buf[lax.rem(table_ref[2 * peers + t], 8)]
                last_hop(p, t).start()
        pick(p, step)
        if todo:
            todo.pop(0)()

    def arrive(p):
        for t in range(ny):
            last_hop(p, t).wait_recv()
        for t in range(1, ny):
            across(p, t, half).start()
        ctx[p][0, 1] = far[p][0]
        if p == KEY:
            ring_of_pos(0, half).wait_recv()
            for t in range(1, ny):
                pos_across(t).start()
            all_pos[0] = ring_pos[...]

    def slot_of(e):
        named = list_ref[e % slots, me * REQ_DEV + e // slots]
        owner = named // DOC_DEV
        t = lax.rem(y - owner // NZ + ny, ny)
        j = lax.rem(z - lax.rem(owner, NZ) + NZ, NZ)
        at = jnp.where(j < half, 2 * j, 2 * (NZ - j) + 1)
        return t, jnp.where(j == half, 1, at), j, named - owner * DOC_DEV

    token = lax.broadcasted_iota(jnp.int32, (doc_len, 128), 0)

    def settle(p):
        for step in range(half + 1):
            for t in range(1, ny):
                across(p, t, step).wait_recv()
        if p == KEY:
            for t in range(1, ny):
                pos_across(t).wait_recv()
            fetch[3].wait()

    def lay_out(p, r):
        every[p][r, context : context + tokens, :head_dim] = has["own"][
            r * tokens : (r + 1) * tokens, p * head_dim : (p + 1) * head_dim
        ]
        for k in range(slots):
            e = r * slots + k
            t, at, j, local = slot_of(e)
            doc = ctx[p][t, at]
            every[p][r, k * doc_len : (k + 1) * doc_len, :head_dim] = doc
            hot = (all_pos[t, j, pl.ds(local, 1)] == token).astype(jnp.bfloat16)
            rows_of = lax.dot_general(hot, doc, (((0,), (0,)), ((), ())), preferred_element_type=jnp.float32)
            dev[p, e * dev_tok : (e + 1) * dev_tok] = rows_of[:dev_tok]

    def renew(p, r, g, weights, total):
        first = r * slots + g * group
        rows = slice(first * dev_tok, (first + group) * dev_tok)
        known = (g + 1) * group * doc_len
        summed = jnp.dot(weights, every[p][r, :known, :head_dim], preferred_element_type=jnp.float32)
        delta = gain_ref[:, p * head_dim : (p + 1) * head_dim] * (summed / total)
        renewed = (dev[p, rows] + delta).astype(jnp.bfloat16)
        for i in range(group):
            fresh[p][first + i] = renewed[i * dev_tok : (i + 1) * dev_tok]
        return jnp.sum(delta * delta, axis=1, keepdims=True) * (0.5 / head_dim)

    def key_update(r, g):
        first = r * slots + g * group
        rows = slice(first * dev_tok, (first + group) * dev_tok)
        known = (g + 1) * group * doc_len
        scores = lax.dot_general(
            dev[KEY, rows].astype(jnp.bfloat16),
            every[KEY][r, :known],
            (((1,), (1,)), ((), ())),
            preferred_element_type=jnp.float32,
        )
        shape = (group * dev_tok, group * doc_len)
        row_slot = lax.broadcasted_iota(jnp.int32, shape, 0) // dev_tok
        key_slot = lax.broadcasted_iota(jnp.int32, shape, 1) // doc_len
        newest = jnp.where(row_slot >= key_slot, scores[:, known - shape[1] :], very_low)
        scores = newest if g == 0 else jnp.concatenate([scores[:, : known - shape[1]], newest], axis=1)
        top = jnp.max(scores, axis=1, keepdims=True)
        weights = jnp.exp2((scores - top) * (scale * LOG2E))
        total = jnp.sum(weights, axis=1, keepdims=True)
        weights = weights.astype(jnp.bfloat16)
        weights_of[g][r] = weights
        square = renew(KEY, r, g, weights, total)
        totals[rows] = jnp.broadcast_to(total, (group * dev_tok, 128))
        columns[rows] = jnp.broadcast_to(square, (group * dev_tok, 128))

    lane_slot = lax.broadcasted_iota(jnp.int32, (1, group * dev_tok), 1) // dev_tok

    def value_update(r, g):
        first = r * slots + g * group
        rows = slice(first * dev_tok, (first + group) * dev_tok)
        square = renew(VALUE, r, g, weights_of[g][r], totals[rows])
        both = (columns[rows] + square).T[:1]
        squares[r * GROUPS + g : r * GROUPS + g + 1, : group * dev_tok] = jnp.where(
            lane_slot + g * group < count_ref[me * REQ_DEV + r], both, 0.0
        )

    side = ny // 2

    def back(p, j):
        return remote(
            upd[p].at[j], mid[p].at[:, z], has["send"].at[p, j], has["recv"].at[p, j], place(ny, y, z - j)
        )

    def turn_aside(p, w):
        src = upd[p].at[half, pl.ds(w * side, side)]
        sems = has["send"].at[p, NZ + w], has["trecv"].at[p, w]
        return remote(src, turn_buf[p].at[w], *sems, along_z[w])

    def turn_forward(p, w):
        origin = lax.rem(z + NZ - 1 + 2 * w, NZ)
        dst = mid[p].at[pl.ds(w * side, side), origin]
        sems = has["tsend"].at[p, w], has["recv"].at[p, NZ + w]
        return remote(turn_buf[p].at[w], dst, *sems, place(ny, y, origin - half))

    def spread(p, u):
        dst = ret_ref.at[pl.ds(y * NZ, NZ), :, pl.ds(p * head_dim, head_dim)]
        return remote(mid[p].at[u], dst, has["gsend"].at[p, u], has["grecv"].at[p, u], along_y[u])

    def renewed_for(p, u, j):
        code = table_ref[peers + (ny - u) % ny * NZ + j]
        e = lax.rem(code // 8, 64)
        r = e // slots
        used = jnp.logical_and(code >= 512, e - r * slots < count_ref[me * REQ_DEV + r])
        return fresh[p][jnp.where(used, e, entries)]

    def far_first(i):
        return jnp.where(lax.rem(i, 2) == 0, half - 1 - i // 2, half + 1 + i // 2)

    def give_back(p):
        for u in range(ny):
            upd[p][half, u] = renewed_for(p, u, half)
        for w in range(2):
            turn_aside(p, w).start()

        def launch(i, carry):
            j = far_first(i)
            for u in range(ny):
                upd[p][j, u] = renewed_for(p, u, j)
            back(p, j).start()
            return carry

        lax.fori_loop(0, NZ - 2, launch, 0)
        for u in range(ny):
            mid[p][u, z] = renewed_for(p, u, 0)

    def turn(p):
        for w in range(2):
            turn_aside(p, w).wait_recv()
            turn_forward(p, w).start()

    def spread_all(p):
        def land(i, carry):
            back(p, far_first(i)).wait_recv()
            return carry

        lax.fori_loop(0, NZ - 2, land, 0)
        for w in range(2):
            turn_forward(p, w).wait_recv()
        for u in range(1, ny):
            spread(p, u).start()
        ret_ref[pl.ds(y * NZ, NZ), :, p * head_dim : (p + 1) * head_dim] = mid[p][0]

    def share(k):
        return pltpu.make_async_remote_copy(
            src_ref=squares,
            dst_ref=parts.at[head_at],
            send_sem=has["hsend"].at[k],
            recv_sem=has["hrecv"].at[k],
            device_id={"heads": fellows[k]},
            device_id_type=MESH,
        )

    row = lax.broadcasted_iota(jnp.int32, (tokens, span - context), 0)
    col = lax.broadcasted_iota(jnp.int32, (tokens, span - context), 1)
    causal = row >= col
    place_of = lax.broadcasted_iota(jnp.int32, (1, context), 1)

    def spot(n):
        n = jnp.clip(n, 0, REQ_DEV * heads - 1)
        r = n // heads
        rows = pl.ds(pl.multiple_of(r * tokens, 16), tokens)
        return r, rows, pl.ds(pl.multiple_of(lax.rem(n, heads) * head_dim, head_dim), head_dim)

    def scores_of(n, out):
        r, rows, cols = spot(n)
        out[...] = lax.dot_general(
            has["q"][rows, cols], every[KEY][r], (((1,), (1,)), ((), ())), preferred_element_type=jnp.float32
        )

    def weights_from(n, scores, out):
        r, _, _ = spot(n)
        docs = jnp.where(place_of < count_ref[me * REQ_DEV + r] * doc_len, scores[:, :context], very_low)
        own = jnp.where(causal, scores[:, context:], very_low)
        top = jnp.maximum(jnp.max(docs, axis=1, keepdims=True), jnp.max(own, axis=1, keepdims=True))
        out[:, :context] = jnp.exp2((docs - top) * (scale * LOG2E)).astype(jnp.bfloat16)
        out[:, context:] = jnp.exp2((own - top) * (scale * LOG2E)).astype(jnp.bfloat16)

    def output_of(n, weights):
        r, rows, cols = spot(n)
        summed = jnp.dot(weights[...], every[VALUE][r], preferred_element_type=jnp.float32)
        att_ref[rows, cols] = (summed[:, :head_dim] / summed[:, head_dim:]).astype(jnp.bfloat16)

    score_a, score_b, weight_a, weight_b = (has[n] for n in ("score0", "score1", "weight0", "weight1"))
    early = [has["early%d" % n] for n in range(EARLY)]

    def early_head(n):
        if n == 0:
            fetch[2].wait()
        scores_of(n, score_a)
        weights_from(n, score_a, early[n])

    def pair(m, carry):
        scores_of(2 * m + 1, score_b)
        weights_from(2 * m, score_a, weight_a)
        output_of(2 * m - 1, weight_b)
        scores_of(2 * m + 2, score_a)
        weights_from(2 * m + 1, score_b, weight_b)
        output_of(2 * m, weight_a)
        return carry

    begin(KEY)
    for way in range(2):
        ring_of_pos(way, 1).start()
    pick(KEY, 0)
    tasks = [lambda: arrive(KEY), lambda: settle(KEY)]
    tasks += [functools.partial(lay_out, KEY, r) for r in range(REQ_DEV)]
    tasks += [functools.partial(key_update, r, g) for r in range(REQ_DEV) for g in range(GROUPS)]
    lead = min(LEAD, full)
    for tick in range(1, full + lead + 1):
        if tick <= full:
            hop(KEY, tick, [])
        if tick == lead:
            fetch[VALUE].wait()
            begin(VALUE)
            pick(VALUE, 0)
        if tick > lead:
            since = tick - full
            counts = (0, 1 if since in (2, 3) else 0)
            if since > 3:
                each_slot = -(-len(tasks) // (2 * (lead + 1 - since)))
                counts = (each_slot, each_slot)
            todo = []
            for some in counts:
                turns, tasks = tasks[:some], tasks[some:]
                todo.append(functools.partial(lambda turns: [one() for one in turns], turns))
            hop(VALUE, tick - lead, todo)

    for task in tasks:
        task()

    if nh > 1:
        other = has["other"]
        twin = head_at + 1 - 2 * lax.rem(head_at, 2)
        pl.semaphore_signal(other, inc=1, device_id={"heads": twin}, device_id_type=MESH)
        pl.semaphore_wait(other, 1)
    give_back(KEY)
    early_head(0)
    arrive(VALUE)
    for n in range(1, EARLY):
        early_head(n)
    settle(VALUE)
    turn(KEY)
    for r in range(REQ_DEV):
        lay_out(VALUE, r)
    for r in range(REQ_DEV):
        for g in range(GROUPS):
            value_update(r, g)
    give_back(VALUE)
    for k in range(1, nh):
        share(k).start()
    parts[head_at] = squares[...]

    weight_b[...] = jnp.ones_like(weight_b)
    scores_of(EARLY, score_a)
    for n in range(EARLY):
        output_of(n, early[n])
    turn(VALUE)
    pairs = REQ_DEV * heads // 2
    lax.fori_loop(EARLY // 2, EARLY // 2 + 1, pair, 0)
    output_of(EARLY - 1, early[EARLY - 1])
    lax.fori_loop(EARLY // 2 + 1, pairs - 2, pair, 0)
    spread_all(KEY)
    lax.fori_loop(pairs - 2, pairs, pair, 0)
    output_of(REQ_DEV * heads - 1, weight_b)
    spread_all(VALUE)

    for k in range(1, nh):
        share(k).wait()
    total = parts[0]
    for k in range(1, nh):
        total = total + parts[k]
    sum_ref[...] = total * (1.0 / KVH)

    for p in range(2):
        for way in range(2):
            for step in range(1, half):
                for chunk in range(CHUNKS):
                    ring(p, way, step, chunk).wait_send()
        for t in range(ny):
            last_hop(p, t).wait_send()
        for step in range(half + 1):
            for t in range(1, ny):
                across(p, t, step).wait_send()
    for way in range(2):
        for step in range(1, half + 1 - way):
            ring_of_pos(way, step).wait_send()
    for t in range(1, ny):
        pos_across(t).wait_send()

    for p in range(2):

        def leave(i, carry):
            back(p, far_first(i)).wait_send()
            return carry

        lax.fori_loop(0, NZ - 2, leave, 0)
        for w in range(2):
            turn_aside(p, w).wait_send()
            turn_forward(p, w).wait_send()
        for u in range(1, ny):
            spread(p, u).wait()


def blend(slots, table, lists, counts, cache, pos, gain, queries, own):
    peers = lax.axis_size("docs")
    ny = peers // NZ
    nh = lax.axis_size("heads")
    half = NZ // 2
    full = half - 1
    entries = REQ_DEV * slots
    dev_tok = pos.shape[1]
    doc_len, width = cache.shape[1:]
    head_dim = width // 2
    tokens = own.shape[0] // REQ_DEV
    span = slots * doc_len + (tokens + 127) // 128 * 128
    rows = slots // GROUPS * dev_tok
    doc = (doc_len, head_dim)
    packet = (dev_tok, head_dim)
    square = jax.ShapeDtypeStruct((REQ_DEV * GROUPS, 128), jnp.float32)
    bf16, f32 = jnp.bfloat16, jnp.float32
    scratch = {}
    for p in range(2):
        for name, shape in (
            ("base", (DOC_DEV,) + doc),
            ("far", (ny,) + doc),
            ("last", (ny,) + doc),
            ("picked", (ny, NZ) + doc),
            ("ctx", (ny, NZ) + doc),
            ("all", (REQ_DEV, span, head_dim * (1 + p))),
            ("fresh", (entries + 1,) + packet),
            ("upd", (NZ, ny) + packet),
            ("turn", (2, ny // 2) + packet),
            ("mid", (ny, NZ) + packet),
        ):
            scratch["%s%d" % (name, p)] = VMEM(shape, bf16)
        for way in range(2):
            for step in range(full):
                scratch["ring%d%d%d" % (p, way, step)] = VMEM((DOC_DEV,) + doc, bf16)
    for g in range(GROUPS):
        scratch["weights%d" % g] = VMEM((REQ_DEV, rows, (g + 1) * slots // GROUPS * doc_len), bf16)
    for name in ("0", "1"):
        scratch["score" + name] = VMEM((tokens, span), f32)
        scratch["weight" + name] = VMEM((tokens, span), bf16)
    for n in range(EARLY):
        scratch["early%d" % n] = VMEM((tokens, span), bf16)
    scratch["q"] = VMEM(queries.shape, bf16)
    scratch["own"] = VMEM(own.shape, bf16)
    scratch["dev"] = VMEM((2, entries * dev_tok, head_dim), f32)
    scratch["totals"] = VMEM((entries * dev_tok, 128), f32)
    scratch["columns"] = VMEM((entries * dev_tok, 128), f32)
    scratch["squares"] = VMEM(square.shape, f32)
    scratch["parts"] = VMEM((nh,) + square.shape, f32)
    scratch["ring_pos"] = VMEM((NZ, 8, 128), jnp.int32)
    scratch["all_pos"] = VMEM((ny, NZ, 8, 128), jnp.int32)
    for name, shape in (
        ("zsend", (2, 2, full, CHUNKS)), ("zrecv", (2, 2, full, CHUNKS)),
        ("lsend", (2, ny)), ("lrecv", (2, ny)),
        ("psend", (2, half + ny)), ("precv", (2, half + ny)),
        ("ysend", (2, ny, half + 1)), ("yrecv", (2, ny, half + 1)),
        ("send", (2, NZ + 2)), ("recv", (2, NZ + 2)),
        ("tsend", (2, 2)), ("trecv", (2, 2)), ("gsend", (2, ny)), ("grecv", (2, ny)),
        ("hsend", (nh,)), ("hrecv", (nh,)),
        ("local_sem", (4,)),
    ):
        scratch[name] = DMA(shape)
    scratch["other"] = pltpu.SemaphoreType.REGULAR
    any_space, vmem = whole(pl.ANY), whole(VMEM)
    return pl.pallas_call(
        functools.partial(blend_kernel, ny, nh, slots, dev_tok, tuple(scratch)),
        out_shape=(
            jax.ShapeDtypeStruct(queries.shape, bf16),
            jax.ShapeDtypeStruct((peers, dev_tok, width), bf16),
            square,
        ),
        in_specs=[whole(SMEM)] * 3 + [any_space, vmem, vmem, any_space, any_space],
        out_specs=(vmem,) * 3,
        scratch_shapes=list(scratch.values()),
        compiler_params=pltpu.CompilerParams(
            collective_id=0, has_side_effects=True, vmem_limit_bytes=56 * 2**20
        ),
        name="blend",
    )(table, lists, counts, cache, pos, gain, queries, own)


def shards(queries, own_kv, cache, doc_lists, doc_counts, dev_pos, blend_gain):
    width = blend_gain.shape[1]
    peers = lax.axis_size("docs")
    ny = peers // NZ
    me = lax.axis_index("docs")
    y, z = me // NZ, me % NZ
    slots = doc_lists.shape[1]
    dev_tok = dev_pos.shape[1]
    doc_len = cache.shape[0] // DOC_DEV

    lists = doc_lists.T
    owner = lists // DOC_DEV
    k = lax.broadcasted_iota(jnp.int32, lists.shape, 0)
    request = lax.broadcasted_iota(jnp.int32, lists.shape, 1)
    pair = request // REQ_DEV * peers + owner
    code = 512 + 8 * (request % REQ_DEV * slots + k) + lists - owner * DOC_DEV
    n = jnp.arange(2 * peers + 128, dtype=jnp.int32)
    t, j = n // NZ % ny, n % NZ
    picks = ((y + t) % ny * NZ + z) * peers + y * NZ + (z - j) % NZ
    returns = me * peers + (y - t) % ny * NZ + (z - j) % NZ
    way = jnp.where(j < ny // 2, 1, -1)
    last = ((y + j) % ny * NZ + (z + way) % NZ) * peers + y * NZ + (z - way * (NZ // 2 - 1)) % NZ
    want = jnp.where(n < peers, picks, jnp.where(n < 2 * peers, returns, last))
    table = jnp.sum(jnp.where(pair[None] == want[:, None, None], code[None], 0), axis=(1, 2))

    att, returned, sums = blend(
        slots, table, lists, doc_counts, cache.reshape(DOC_DEV, doc_len, width), dev_pos, blend_gain, queries, own_kv
    )
    group_rows = slots // GROUPS * dev_tok
    dev_score = sums.reshape(REQ_DEV, GROUPS, 128)[:, :, :group_rows].reshape(REQ_DEV, slots, dev_tok)
    return att, returned, dev_score


def solution(mesh):
    return jax.shard_map(
        shards,
        mesh=mesh,
        in_specs=(
            P("docs", "heads"),
            P("docs", "heads"),
            P("docs", "heads"),
            P(),
            P(),
            P("docs", None),
            P("heads", None),
        ),
        out_specs=(P("docs", "heads"), P("docs", None, "heads"), P("docs", None, None)),
        check_vma=False,
    )
```

```python
import functools

import jax
import jax.numpy as jnp
from jax import lax
from jax.experimental import pallas as pl
from jax.experimental.pallas import tpu as pltpu
from jax.sharding import PartitionSpec as P

KVH = 8
REQ_DEV = 2
DOC_DEV = 6
NZ = 16
very_low = -1e30
VMEM = pltpu.VMEM
SMEM = pltpu.SMEM
DMA = pltpu.SemaphoreType.DMA
MESH = pl.DeviceIdType.MESH
LOG2E = 1.4426950408889634
GROUPS = 4
LEAD = 6
CHUNKS = 2
EARLY = 2
KEY, VALUE = 0, 1


def whole(space):
    return pl.BlockSpec(memory_space=space)


def place(ny, y, z):
    return lax.rem(y + 2 * ny, ny) * NZ + lax.rem(z + 2 * NZ, NZ)


def blend_kernel(
    ny, nh, slots, dev_tok, names, table_ref, list_ref, count_ref, cache_ref, pos_ref, gain_ref, q_ref, own_ref,
    att_ref, ret_ref, sum_ref, *scratch
):
    has = dict(zip(names, scratch))
    peers = ny * NZ
    entries = REQ_DEV * slots
    doc_len, head_dim = has["base0"].shape[1:]
    tokens = own_ref.shape[0] // REQ_DEV
    heads = q_ref.shape[1] // head_dim
    context = slots * doc_len
    span = has["all0"].shape[1]
    group = slots // GROUPS
    scale = head_dim ** (-0.5)
    half = NZ // 2
    full = half - 1
    each = DOC_DEV // CHUNKS
    me = lax.axis_index("docs")
    y, z = me // NZ, lax.rem(me, NZ)
    head_at = lax.axis_index("heads")
    fellows = [lax.rem(head_at + k, nh) for k in range(nh)]
    local_sem = has["local_sem"]

    def two(name):
        return has[name + "0"], has[name + "1"]

    base, far, last_pick, picked, relay, ctx, every, fresh, upd, turn_buf, mid = map(
        two, ("base", "far", "last", "picked", "relay", "ctx", "all", "fresh", "upd", "turn", "mid")
    )
    passing = [[[has["ring%d%d%d" % (p, way, s)] for s in range(full)] for way in range(2)] for p in range(2)]
    ring_pos, all_pos, dev, squares, parts = (has[n] for n in ("ring_pos", "all_pos", "dev", "squares", "parts"))
    weights_of = [has["weights%d" % g] for g in range(GROUPS)]
    totals, columns = has["totals"], has["columns"]

    fetch = [
        pltpu.make_async_copy(cache_ref.at[:, :, pl.ds(p * head_dim, head_dim)], base[p], local_sem.at[p])
        for p in range(2)
    ]
    fetch += [
        pltpu.make_async_copy(q_ref, has["q"], local_sem.at[2]),
        pltpu.make_async_copy(own_ref, has["own"], local_sem.at[3]),
    ]
    for one in fetch:
        one.start()
    barrier = pltpu.get_barrier_semaphore()

    def greet(j, carry):
        pl.semaphore_signal(barrier, inc=1, device_id={"docs": place(ny, y, z - j)}, device_id_type=MESH)
        return carry

    lax.fori_loop(1, NZ, greet, 0)
    for t in range(1, ny):
        pl.semaphore_signal(barrier, inc=1, device_id={"docs": place(ny, y + t, z)}, device_id_type=MESH)
    for k in range(1, nh):
        pl.semaphore_signal(barrier, inc=1, device_id={"heads": fellows[k]}, device_id_type=MESH)
    ring_pos[0] = jnp.full(ring_pos.shape[1:], -1, jnp.int32)
    ring_pos[0, :DOC_DEV, :dev_tok] = pos_ref[...]
    squares[...] = jnp.zeros_like(squares)
    for p in range(2):
        fresh[p][entries] = jnp.zeros(fresh[p].shape[1:], fresh[p].dtype)
        every[p][:, context:, :head_dim] = jnp.zeros((REQ_DEV, span - context, head_dim), jnp.bfloat16)
    every[VALUE][:, :, head_dim:] = jnp.ones((REQ_DEV, span, head_dim), jnp.bfloat16)
    fetch[KEY].wait()
    pl.semaphore_wait(barrier, NZ - 1 + ny - 1 + nh - 1)

    along_z = [place(ny, y, z + 1), place(ny, y, z - 1)]
    along_y = [place(ny, y + t, z) for t in range(ny)]

    def remote(src, dst, send_sem, recv_sem, device):
        return pltpu.make_async_remote_copy(
            src_ref=src, dst_ref=dst, send_sem=send_sem, recv_sem=recv_sem,
            device_id={"docs": device}, device_id_type=MESH,
        )

    def ring(p, way, step, chunk):
        src = base[p] if step == 1 else passing[p][way][step - 2]
        rows = pl.ds(chunk * each, each)
        sems = has["zsend"].at[p, way, step - 1, chunk], has["zrecv"].at[p, way, step - 1, chunk]
        return remote(src.at[rows], passing[p][way][step - 1].at[rows], *sems, along_z[way])

    def last_hop(p, t):
        sems = has["lsend"].at[p, t], has["lrecv"].at[p, t]
        return remote(last_pick[p].at[t], far[p].at[t], *sems, along_z[2 * t // ny])

    def ring_of_pos(way, step):
        src, dst = (step - 1, step) if way == 0 else ((NZ - step + 1) % NZ, NZ - step)
        sems = has["psend"].at[way, step], has["precv"].at[way, step]
        return remote(ring_pos.at[src], ring_pos.at[dst], *sems, along_z[way])

    def pos_across(t):
        sems = has["psend"].at[0, half + t], has["precv"].at[0, half + t]
        return remote(ring_pos, all_pos.at[t], *sems, along_y[t])

    def across(p, t, step):
        at = pl.ds(1 if step == half else 2 * step, 1 if step in (0, half) else 2)
        src = far[p].at[pl.ds(t, 1)] if step == half else picked[p].at[t, at]
        if relayed(t, step):
            sems = has["ysend"].at[p, t, step], has["frecv"].at[p, step // 2]
            return remote(src, relay[p].at[step // 2], *sems, along_y[ny - 1])
        sems = has["ysend"].at[p, t, step], has["yrecv"].at[p, t, step]
        return remote(src, ctx[p].at[t, at], *sems, along_y[t])

    def relayed(t, step):
        return 2 * t == ny > 2 and step < half and step % 2 == 1

    def forward(p, step):
        sems = has["fsend"].at[p, step // 2], has["yrecv"].at[p, ny // 2, step]
        return remote(relay[p].at[step // 2], ctx[p].at[ny // 2, pl.ds(2 * step, 2)], *sems, along_y[ny - 1])

    def pass_on(p, step):
        if step > 0 and relayed(ny // 2, step):
            across(p, ny // 2, step).wait_recv()
            forward(p, step).start()

    def pick(p, step):
        for t in list(range(1, ny)) + [0]:
            for way in range(1 if step == 0 else 2):
                buf = base[p] if step == 0 else passing[p][way][step - 1]
                j = step if way == 0 else NZ - step
                doc = buf[lax.rem(table_ref[t * NZ + j], 8)]
                if t:
                    picked[p][t, 2 * step + way] = doc
                else:
                    ctx[p][0, 2 * step + way] = doc
            if t:
                across(p, t, step).start()

    def begin(p):
        for chunk in range(CHUNKS):
            for way in range(2):
                ring(p, way, 1, chunk).start()

    def hop(p, step, todo):
        for chunk in range(CHUNKS):
            for way in range(2):
                ring(p, way, step, chunk).wait_recv()
                if step < full:
                    ring(p, way, step + 1, chunk).start()
            if p == KEY and chunk == 0:
                for way in range(2):
                    ring_of_pos(way, step).wait_recv()
                    if way == 0 or step < full:
                        ring_of_pos(way, step + 1).start()
            if chunk < CHUNKS - 1 and todo:
                todo.pop(0)()
        if step == full:
            for t in range(ny):
                buf = passing[p][2 * t // ny][full - 1]
                last_pick[p][t] = buf[lax.rem(table_ref[2 * peers + t], 8)]
                last_hop(p, t).start()
        pick(p, step)
        pass_on(p, step - 2)
        if todo:
            todo.pop(0)()

    def arrive(p):
        for t in range(ny):
            last_hop(p, t).wait_recv()
        pass_on(p, full - 1)
        pass_on(p, full)
        for t in range(1, ny):
            across(p, t, half).start()
        ctx[p][0, 1] = far[p][0]
        if p == KEY:
            ring_of_pos(0, half).wait_recv()
            for t in range(1, ny):
                pos_across(t).start()
            all_pos[0] = ring_pos[...]

    def slot_of(e):
        named = list_ref[e % slots, me * REQ_DEV + e // slots]
        owner = named // DOC_DEV
        t = lax.rem(y - owner // NZ + ny, ny)
        j = lax.rem(z - lax.rem(owner, NZ) + NZ, NZ)
        at = jnp.where(j < half, 2 * j, 2 * (NZ - j) + 1)
        return t, jnp.where(j == half, 1, at), j, named - owner * DOC_DEV

    token = lax.broadcasted_iota(jnp.int32, (doc_len, 128), 0)

    def settle(p):
        for step in range(half + 1):
            for t in range(1, ny):
                (forward(p, step) if relayed(t, step) else across(p, t, step)).wait_recv()
        if p == KEY:
            for t in range(1, ny):
                pos_across(t).wait_recv()
            fetch[3].wait()

    def lay_out(p, r):
        every[p][r, context : context + tokens, :head_dim] = has["own"][
            r * tokens : (r + 1) * tokens, p * head_dim : (p + 1) * head_dim
        ]
        for k in range(slots):
            e = r * slots + k
            t, at, j, local = slot_of(e)
            doc = ctx[p][t, at]
            every[p][r, k * doc_len : (k + 1) * doc_len, :head_dim] = doc
            hot = (all_pos[t, j, pl.ds(local, 1)] == token).astype(jnp.bfloat16)
            rows_of = lax.dot_general(hot, doc, (((0,), (0,)), ((), ())), preferred_element_type=jnp.float32)
            dev[p, e * dev_tok : (e + 1) * dev_tok] = rows_of[:dev_tok]

    def renew(p, r, g, weights, total):
        first = r * slots + g * group
        rows = slice(first * dev_tok, (first + group) * dev_tok)
        known = (g + 1) * group * doc_len
        summed = jnp.dot(weights, every[p][r, :known, :head_dim], preferred_element_type=jnp.float32)
        delta = gain_ref[:, p * head_dim : (p + 1) * head_dim] * (summed / total)
        renewed = (dev[p, rows] + delta).astype(jnp.bfloat16)
        for i in range(group):
            fresh[p][first + i] = renewed[i * dev_tok : (i + 1) * dev_tok]
        return jnp.sum(delta * delta, axis=1, keepdims=True) * (0.5 / head_dim)

    def key_update(r, g):
        first = r * slots + g * group
        rows = slice(first * dev_tok, (first + group) * dev_tok)
        known = (g + 1) * group * doc_len
        scores = lax.dot_general(
            dev[KEY, rows].astype(jnp.bfloat16),
            every[KEY][r, :known],
            (((1,), (1,)), ((), ())),
            preferred_element_type=jnp.float32,
        )
        shape = (group * dev_tok, group * doc_len)
        row_slot = lax.broadcasted_iota(jnp.int32, shape, 0) // dev_tok
        key_slot = lax.broadcasted_iota(jnp.int32, shape, 1) // doc_len
        newest = jnp.where(row_slot >= key_slot, scores[:, known - shape[1] :], very_low)
        scores = newest if g == 0 else jnp.concatenate([scores[:, : known - shape[1]], newest], axis=1)
        top = jnp.max(scores, axis=1, keepdims=True)
        weights = jnp.exp2((scores - top) * (scale * LOG2E))
        total = jnp.sum(weights, axis=1, keepdims=True)
        weights = weights.astype(jnp.bfloat16)
        weights_of[g][r] = weights
        square = renew(KEY, r, g, weights, total)
        totals[rows] = jnp.broadcast_to(total, (group * dev_tok, 128))
        columns[rows] = jnp.broadcast_to(square, (group * dev_tok, 128))

    lane_slot = lax.broadcasted_iota(jnp.int32, (1, group * dev_tok), 1) // dev_tok

    def value_update(r, g):
        first = r * slots + g * group
        rows = slice(first * dev_tok, (first + group) * dev_tok)
        square = renew(VALUE, r, g, weights_of[g][r], totals[rows])
        both = (columns[rows] + square).T[:1]
        squares[r * GROUPS + g : r * GROUPS + g + 1, : group * dev_tok] = jnp.where(
            lane_slot + g * group < count_ref[me * REQ_DEV + r], both, 0.0
        )

    side = ny // 2

    def back(p, j):
        return remote(
            upd[p].at[j], mid[p].at[:, z], has["send"].at[p, j], has["recv"].at[p, j], place(ny, y, z - j)
        )

    def turn_aside(p, w):
        src = upd[p].at[half, pl.ds(w * side, side)]
        sems = has["send"].at[p, NZ + w], has["trecv"].at[p, w]
        return remote(src, turn_buf[p].at[w], *sems, along_z[w])

    def turn_forward(p, w):
        origin = lax.rem(z + NZ - 1 + 2 * w, NZ)
        dst = mid[p].at[pl.ds(w * side, side), origin]
        sems = has["tsend"].at[p, w], has["recv"].at[p, NZ + w]
        return remote(turn_buf[p].at[w], dst, *sems, place(ny, y, origin - half))

    def spread(p, u):
        dst = ret_ref.at[pl.ds(y * NZ, NZ), :, pl.ds(p * head_dim, head_dim)]
        return remote(mid[p].at[u], dst, has["gsend"].at[p, u], has["grecv"].at[p, u], along_y[u])

    def renewed_for(p, u, j):
        code = table_ref[peers + (ny - u) % ny * NZ + j]
        e = lax.rem(code // 8, 64)
        r = e // slots
        used = jnp.logical_and(code >= 512, e - r * slots < count_ref[me * REQ_DEV + r])
        return fresh[p][jnp.where(used, e, entries)]

    def far_first(i):
        return jnp.where(lax.rem(i, 2) == 0, half - 1 - i // 2, half + 1 + i // 2)

    def give_back(p):
        for u in range(ny):
            upd[p][half, u] = renewed_for(p, u, half)
        for w in range(2):
            turn_aside(p, w).start()

        def launch(i, carry):
            j = far_first(i)
            for u in range(ny):
                upd[p][j, u] = renewed_for(p, u, j)
            back(p, j).start()
            return carry

        lax.fori_loop(0, NZ - 2, launch, 0)
        for u in range(ny):
            mid[p][u, z] = renewed_for(p, u, 0)

    def turn(p):
        for w in range(2):
            turn_aside(p, w).wait_recv()
            turn_forward(p, w).start()

    def spread_all(p):
        def land(i, carry):
            back(p, far_first(i)).wait_recv()
            return carry

        lax.fori_loop(0, NZ - 2, land, 0)
        for w in range(2):
            turn_forward(p, w).wait_recv()
        for u in range(1, ny):
            spread(p, u).start()
        ret_ref[pl.ds(y * NZ, NZ), :, p * head_dim : (p + 1) * head_dim] = mid[p][0]

    def share(k):
        return pltpu.make_async_remote_copy(
            src_ref=squares,
            dst_ref=parts.at[head_at],
            send_sem=has["hsend"].at[k],
            recv_sem=has["hrecv"].at[k],
            device_id={"heads": fellows[k]},
            device_id_type=MESH,
        )

    row = lax.broadcasted_iota(jnp.int32, (tokens, span - context), 0)
    col = lax.broadcasted_iota(jnp.int32, (tokens, span - context), 1)
    causal = row >= col
    place_of = lax.broadcasted_iota(jnp.int32, (1, context), 1)

    def spot(n):
        n = jnp.clip(n, 0, REQ_DEV * heads - 1)
        r = n // heads
        rows = pl.ds(pl.multiple_of(r * tokens, 16), tokens)
        return r, rows, pl.ds(pl.multiple_of(lax.rem(n, heads) * head_dim, head_dim), head_dim)

    def scores_of(n, out):
        r, rows, cols = spot(n)
        out[...] = lax.dot_general(
            has["q"][rows, cols], every[KEY][r], (((1,), (1,)), ((), ())), preferred_element_type=jnp.float32
        )

    def weights_from(n, scores, out):
        r, _, _ = spot(n)
        docs = jnp.where(place_of < count_ref[me * REQ_DEV + r] * doc_len, scores[:, :context], very_low)
        own = jnp.where(causal, scores[:, context:], very_low)
        top = jnp.maximum(jnp.max(docs, axis=1, keepdims=True), jnp.max(own, axis=1, keepdims=True))
        out[:, :context] = jnp.exp2((docs - top) * (scale * LOG2E)).astype(jnp.bfloat16)
        out[:, context:] = jnp.exp2((own - top) * (scale * LOG2E)).astype(jnp.bfloat16)

    def output_of(n, weights):
        r, rows, cols = spot(n)
        summed = jnp.dot(weights[...], every[VALUE][r], preferred_element_type=jnp.float32)
        att_ref[rows, cols] = (summed[:, :head_dim] / summed[:, head_dim:]).astype(jnp.bfloat16)

    score_a, score_b, weight_a, weight_b = (has[n] for n in ("score0", "score1", "weight0", "weight1"))
    early = [has["early%d" % n] for n in range(EARLY)]

    def early_head(n):
        if n == 0:
            fetch[2].wait()
        scores_of(n, score_a)
        weights_from(n, score_a, early[n])

    def pair(m, carry):
        scores_of(2 * m + 1, score_b)
        weights_from(2 * m, score_a, weight_a)
        output_of(2 * m - 1, weight_b)
        scores_of(2 * m + 2, score_a)
        weights_from(2 * m + 1, score_b, weight_b)
        output_of(2 * m, weight_a)
        return carry

    begin(KEY)
    for way in range(2):
        ring_of_pos(way, 1).start()
    pick(KEY, 0)
    tasks = [lambda: arrive(KEY), lambda: settle(KEY)]
    tasks += [functools.partial(lay_out, KEY, r) for r in range(REQ_DEV)]
    tasks += [functools.partial(key_update, r, g) for r in range(REQ_DEV) for g in range(GROUPS)]
    lead = min(LEAD, full)
    for tick in range(1, full + lead + 1):
        if tick <= full:
            hop(KEY, tick, [])
        if tick == lead:
            fetch[VALUE].wait()
            begin(VALUE)
            pick(VALUE, 0)
        if tick > lead:
            since = tick - full
            counts = (0, 1 if since in (2, 3) else 0)
            if since > 3:
                each_slot = -(-len(tasks) // (2 * (lead + 1 - since)))
                counts = (each_slot, each_slot)
            todo = []
            for some in counts:
                turns, tasks = tasks[:some], tasks[some:]
                todo.append(functools.partial(lambda turns: [one() for one in turns], turns))
            hop(VALUE, tick - lead, todo)

    for task in tasks:
        task()

    if nh > 1:
        other = has["other"]
        twin = head_at + 1 - 2 * lax.rem(head_at, 2)
        pl.semaphore_signal(other, inc=1, device_id={"heads": twin}, device_id_type=MESH)
        pl.semaphore_wait(other, 1)
    give_back(KEY)
    early_head(0)
    arrive(VALUE)
    for n in range(1, EARLY):
        early_head(n)
    settle(VALUE)
    turn(KEY)
    for r in range(REQ_DEV):
        lay_out(VALUE, r)
    for r in range(REQ_DEV):
        for g in range(GROUPS):
            value_update(r, g)
    give_back(VALUE)
    for k in range(1, nh):
        share(k).start()
    parts[head_at] = squares[...]

    weight_b[...] = jnp.ones_like(weight_b)
    scores_of(EARLY, score_a)
    for n in range(EARLY):
        output_of(n, early[n])
    turn(VALUE)
    pairs = REQ_DEV * heads // 2
    lax.fori_loop(EARLY // 2, EARLY // 2 + 1, pair, 0)
    output_of(EARLY - 1, early[EARLY - 1])
    lax.fori_loop(EARLY // 2 + 1, pairs - 2, pair, 0)
    spread_all(KEY)
    lax.fori_loop(pairs - 2, pairs, pair, 0)
    output_of(REQ_DEV * heads - 1, weight_b)
    spread_all(VALUE)

    for k in range(1, nh):
        share(k).wait()
    total = parts[0]
    for k in range(1, nh):
        total = total + parts[k]
    sum_ref[...] = total * (1.0 / KVH)

    for p in range(2):
        for way in range(2):
            for step in range(1, half):
                for chunk in range(CHUNKS):
                    ring(p, way, step, chunk).wait_send()
        for t in range(ny):
            last_hop(p, t).wait_send()
        for step in range(half + 1):
            for t in range(1, ny):
                across(p, t, step).wait_send()
                if relayed(t, step):
                    forward(p, step).wait_send()
    for way in range(2):
        for step in range(1, half + 1 - way):
            ring_of_pos(way, step).wait_send()
    for t in range(1, ny):
        pos_across(t).wait_send()

    for p in range(2):

        def leave(i, carry):
            back(p, far_first(i)).wait_send()
            return carry

        lax.fori_loop(0, NZ - 2, leave, 0)
        for w in range(2):
            turn_aside(p, w).wait_send()
            turn_forward(p, w).wait_send()
        for u in range(1, ny):
            spread(p, u).wait()


def blend(slots, table, lists, counts, cache, pos, gain, queries, own):
    peers = lax.axis_size("docs")
    ny = peers // NZ
    nh = lax.axis_size("heads")
    half = NZ // 2
    full = half - 1
    entries = REQ_DEV * slots
    dev_tok = pos.shape[1]
    doc_len, width = cache.shape[1:]
    head_dim = width // 2
    tokens = own.shape[0] // REQ_DEV
    span = slots * doc_len + (tokens + 127) // 128 * 128
    rows = slots // GROUPS * dev_tok
    doc = (doc_len, head_dim)
    packet = (dev_tok, head_dim)
    square = jax.ShapeDtypeStruct((REQ_DEV * GROUPS, 128), jnp.float32)
    bf16, f32 = jnp.bfloat16, jnp.float32
    scratch = {}
    for p in range(2):
        for name, shape in (
            ("base", (DOC_DEV,) + doc),
            ("far", (ny,) + doc),
            ("last", (ny,) + doc),
            ("picked", (ny, NZ) + doc),
            ("relay", (half // 2, 2) + doc),
            ("ctx", (ny, NZ) + doc),
            ("all", (REQ_DEV, span, head_dim * (1 + p))),
            ("fresh", (entries + 1,) + packet),
            ("upd", (NZ, ny) + packet),
            ("turn", (2, ny // 2) + packet),
            ("mid", (ny, NZ) + packet),
        ):
            scratch["%s%d" % (name, p)] = VMEM(shape, bf16)
        for way in range(2):
            for step in range(full):
                scratch["ring%d%d%d" % (p, way, step)] = VMEM((DOC_DEV,) + doc, bf16)
    for g in range(GROUPS):
        scratch["weights%d" % g] = VMEM((REQ_DEV, rows, (g + 1) * slots // GROUPS * doc_len), bf16)
    for name in ("0", "1"):
        scratch["score" + name] = VMEM((tokens, span), f32)
        scratch["weight" + name] = VMEM((tokens, span), bf16)
    for n in range(EARLY):
        scratch["early%d" % n] = VMEM((tokens, span), bf16)
    scratch["q"] = VMEM(queries.shape, bf16)
    scratch["own"] = VMEM(own.shape, bf16)
    scratch["dev"] = VMEM((2, entries * dev_tok, head_dim), f32)
    scratch["totals"] = VMEM((entries * dev_tok, 128), f32)
    scratch["columns"] = VMEM((entries * dev_tok, 128), f32)
    scratch["squares"] = VMEM(square.shape, f32)
    scratch["parts"] = VMEM((nh,) + square.shape, f32)
    scratch["ring_pos"] = VMEM((NZ, 8, 128), jnp.int32)
    scratch["all_pos"] = VMEM((ny, NZ, 8, 128), jnp.int32)
    for name, shape in (
        ("zsend", (2, 2, full, CHUNKS)), ("zrecv", (2, 2, full, CHUNKS)),
        ("lsend", (2, ny)), ("lrecv", (2, ny)),
        ("psend", (2, half + ny)), ("precv", (2, half + ny)),
        ("ysend", (2, ny, half + 1)), ("yrecv", (2, ny, half + 1)),
        ("fsend", (2, half // 2)), ("frecv", (2, half // 2)),
        ("send", (2, NZ + 2)), ("recv", (2, NZ + 2)),
        ("tsend", (2, 2)), ("trecv", (2, 2)), ("gsend", (2, ny)), ("grecv", (2, ny)),
        ("hsend", (nh,)), ("hrecv", (nh,)),
        ("local_sem", (4,)),
    ):
        scratch[name] = DMA(shape)
    scratch["other"] = pltpu.SemaphoreType.REGULAR
    any_space, vmem = whole(pl.ANY), whole(VMEM)
    return pl.pallas_call(
        functools.partial(blend_kernel, ny, nh, slots, dev_tok, tuple(scratch)),
        out_shape=(
            jax.ShapeDtypeStruct(queries.shape, bf16),
            jax.ShapeDtypeStruct((peers, dev_tok, width), bf16),
            square,
        ),
        in_specs=[whole(SMEM)] * 3 + [any_space, vmem, vmem, any_space, any_space],
        out_specs=(vmem,) * 3,
        scratch_shapes=list(scratch.values()),
        compiler_params=pltpu.CompilerParams(
            collective_id=0, has_side_effects=True, vmem_limit_bytes=56 * 2**20
        ),
        name="blend",
    )(table, lists, counts, cache, pos, gain, queries, own)


def shards(queries, own_kv, cache, doc_lists, doc_counts, dev_pos, blend_gain):
    width = blend_gain.shape[1]
    peers = lax.axis_size("docs")
    ny = peers // NZ
    me = lax.axis_index("docs")
    y, z = me // NZ, me % NZ
    slots = doc_lists.shape[1]
    dev_tok = dev_pos.shape[1]
    doc_len = cache.shape[0] // DOC_DEV

    lists = doc_lists.T
    owner = lists // DOC_DEV
    k = lax.broadcasted_iota(jnp.int32, lists.shape, 0)
    request = lax.broadcasted_iota(jnp.int32, lists.shape, 1)
    pair = request // REQ_DEV * peers + owner
    code = 512 + 8 * (request % REQ_DEV * slots + k) + lists - owner * DOC_DEV
    n = jnp.arange(2 * peers + 128, dtype=jnp.int32)
    t, j = n // NZ % ny, n % NZ
    picks = ((y + t) % ny * NZ + z) * peers + y * NZ + (z - j) % NZ
    returns = me * peers + (y - t) % ny * NZ + (z - j) % NZ
    way = jnp.where(j < ny // 2, 1, -1)
    last = ((y + j) % ny * NZ + (z + way) % NZ) * peers + y * NZ + (z - way * (NZ // 2 - 1)) % NZ
    want = jnp.where(n < peers, picks, jnp.where(n < 2 * peers, returns, last))
    table = jnp.sum(jnp.where(pair[None] == want[:, None, None], code[None], 0), axis=(1, 2))

    att, returned, sums = blend(
        slots, table, lists, doc_counts, cache.reshape(DOC_DEV, doc_len, width), dev_pos, blend_gain, queries, own_kv
    )
    group_rows = slots // GROUPS * dev_tok
    dev_score = sums.reshape(REQ_DEV, GROUPS, 128)[:, :, :group_rows].reshape(REQ_DEV, slots, dev_tok)
    return att, returned, dev_score


def solution(mesh):
    return jax.shard_map(
        shards,
        mesh=mesh,
        in_specs=(
            P("docs", "heads"),
            P("docs", "heads"),
            P("docs", "heads"),
            P(),
            P(),
            P("docs", None),
            P("heads", None),
        ),
        out_specs=(P("docs", "heads"), P("docs", None, "heads"), P("docs", None, None)),
        check_vma=False,
    )
```
